32 devices in a mesh: seq: 16 (over z, y, x), head: 2 (over core).
Axes of the slice: x: 2, y: 2, z: 4, core: 2. Of those that a mesh axis runs over, the one named last changes fastest.
Arguments:
- x_in: bfloat16 [2048, 1536], P('seq'), may hold values from -6 to 6
- doc_start: int32 [2048], P('seq'), may hold values from 0 to 1, as said below
- norm1_gain: float32 [1536], replicated, may hold values from 0.5 to 1.5
- input_weight: bfloat16 [1536, 2, 3072], P(None, None, 'head'), may hold values from -0.15625 to 0.15625
- conv_w: float32 [4, 3072], P(None, 'head'), may hold values from -3 to 3
- conv_b: float32 [3072], P('head'), may hold values from -2.4 to 2.4
- w_x: bfloat16 [3072, 128], P('head'), may hold values from -0.109375 to 0.109375
- dt_gain: float32 [96], replicated, may hold values from 0.25 to 1.75
- b_gain: float32 [16], replicated, may hold values from 0.25 to 1.75
- c_gain: float32 [16], replicated, may hold values from 0.25 to 1.75
- w_dt: bfloat16 [96, 3072], P(None, 'head'), may hold values from -0.625 to 0.625
- dt_bias: float32 [3072], P('head'), may hold values from -5.5 to -4
- state_rate: float32 [3072, 16], P('head'), as said below
- skip: float32 [3072], P('head'), may hold values from 0.5 to 1.5
- w_out: bfloat16 [3072, 1536], P('head'), may hold values from -0.109375 to 0.109375
- norm2_gain: float32 [1536], replicated, may hold values from 0.5 to 1.5
- w_gu: bfloat16 [1536, 2, 4096], P(None, None, 'head'), may hold values from -0.15625 to 0.15625
- w_down: bfloat16 [4096, 1536], P('head'), may hold values from -0.09375 to 0.09375
- d_out: bfloat16 [2048, 1536], P('seq'), may hold values from -6 to 6
Outputs:
- output: bfloat16 [2048, 1536], P('seq')
- d_x: float32 [2048, 1536], P('seq')
- g_norm1: float32 [1536], P('seq')
- g_w_in: float32 [1536, 2, 3072], P('seq', None, 'head')
- g_conv_w: float32 [4, 3072], P(None, 'head')
- g_conv_b: float32 [3072], P('head')
- g_w_x: float32 [3072, 128], P('head')
- g_dt_gain: float32 [96], replicated
- g_b_gain: float32 [16], replicated
- g_c_gain: float32 [16], replicated
- g_w_dt: float32 [96, 3072], P(None, 'head')
- g_dt_bias: float32 [3072], P('head')
- g_state_rate: float32 [3072, 16], P('head')
- g_skip: float32 [3072], P('head')
- g_w_out: float32 [3072, 1536], P('head', 'seq')
- g_norm2: float32 [1536], P('seq')
- g_w_gu: float32 [1536, 2, 4096], P('seq', None, 'head')
- g_w_down: float32 [4096, 1536], P('head', 'seq')
The draws below stay inside these ranges and needn't reach their ends.
Inputs may be any that keep to these rules, and one draw needn't show every extreme that they name: `doc_start`: 1 marks a token that begins a document and 0 any other; the sequence holds exactly three documents: the first begins at token 0, the second begins among tokens 1 to 127, and the third begins among the last 127 tokens. `state_rate`: positive rates.
All inputs are finite; a program needn't handle non-finite values.
Results may differ from the reference program's by a relative error of at most 0.012.
The reference program's roundings to bfloat16 on the way count: a program that leaves them out, or rounds other values in their place, can miss the bound.
Values may be sent and summed in bfloat16 or wider, within the bound.
A program may use at most 256 MiB of HBM per device.

```python
import math
import jax
import jax.numpy as jnp
from jax import lax

D = 1536
E = 3072
N = 16
R = 96
FF = 4096
KW = 4
BLOCK = 64
TOK_DEV = 128
TOKENS = 2048


def draw_doc_start(key, part):
    key = jax.random.fold_in(key, 11)
    first_key, last_key = jax.random.split(key, 2)
    second_start = jax.random.randint(first_key, (), 1, TOK_DEV).astype(jnp.int32)
    third_start = (TOKENS - TOK_DEV + jax.random.randint(last_key, (), 1, TOK_DEV)).astype(jnp.int32)
    positions = jnp.arange(TOKENS, dtype=jnp.int32)
    flags = (positions == 0) | (positions == second_start) | (positions == third_start)
    return flags.astype(jnp.int32)


def draw_state_rate(key, part):
    key = jax.random.fold_in(key, 7)
    pick_key, slow_key, fast_key, spread_key = jax.random.split(key, 4)
    share = 0.5
    slow_mask = jax.random.uniform(pick_key, (E, 1), jnp.float32) < share
    slow_rate = jnp.exp(jax.random.uniform(slow_key, (E, 1), jnp.float32, math.log(30.0 / TOKENS), math.log(100.0 / TOKENS)))
    fast_rate = jnp.exp(jax.random.uniform(fast_key, (E, 1), jnp.float32, math.log(1.5), math.log(4.0)))
    base_rate = jnp.where(slow_mask, slow_rate, fast_rate)
    return base_rate * jnp.exp(jax.random.uniform(spread_key, (E, N), jnp.float32, -0.7, 0.7))


def levels(rng, dims, cuts, least, largest):
    def one(axis_at, shards_of):
        draws = jax.random.uniform(jax.random.fold_in(jax.random.fold_in(rng, 6), axis_at), (shards_of,), jnp.float32, least / len(cuts), largest / len(cuts))
        return jnp.repeat(jnp.exp(draws), dims[axis_at] // shards_of).reshape((-1,) + (1,) * (len(dims) - axis_at - 1))

    level = one(*cuts[0])
    for cut in cuts[1:]:
        level = level * one(*cut)
    return level


def gaussian(key, shape, width, bound, shards=(), kind=jnp.bfloat16):
    level = levels(key, shape, shards, -0.22, 0.18) if shards else 1.0
    drawn = jax.random.normal(key, shape, jnp.float32) * width * level
    return jnp.minimum(jnp.maximum(drawn, -bound), bound).astype(kind)


def setup_inputs(seed: int = 0) -> dict:
    key_of = jax.random.split(jax.random.key(seed), 20)
    x_in = gaussian(key_of[0], (TOKENS, D), 1.0, 6.0, ((0, 16),))
    doc_start = draw_doc_start(jax.random.fold_in(key_of[19], 71), 0)
    norm1_gain = jnp.clip(1.0 + 0.1 * jax.random.normal(key_of[2], (D,), jnp.float32), 0.5, 1.5)
    input_weight = gaussian(key_of[3], (D, 2, E), D ** -0.5, 0.15625, ((2, 2),))
    conv_w = gaussian(key_of[4], (KW, E), KW ** -0.5, 3.0, ((1, 2),), jnp.float32)
    conv_b = gaussian(key_of[5], (E,), 0.4, 2.4, ((0, 2),), jnp.float32)
    w_x = gaussian(key_of[6], (E, R + 2 * N), E ** -0.5, 0.109375, ((0, 2),))
    dt_gain = jnp.clip(1.0 + 0.15 * jax.random.normal(key_of[7], (R,), jnp.float32), 0.25, 1.75)
    b_gain = jnp.clip(1.0 + 0.15 * jax.random.normal(key_of[8], (N,), jnp.float32), 0.25, 1.75)
    c_gain = jnp.clip(1.0 + 0.15 * jax.random.normal(key_of[9], (N,), jnp.float32), 0.25, 1.75)
    w_dt = gaussian(key_of[10], (R, E), R ** -0.5, 0.625, ((1, 2),))
    dt_bias = jnp.clip(-5.5 + 1.5 * jax.random.uniform(key_of[11], (E,), jnp.float32) ** levels(key_of[11], (E,), ((0, 2),), -0.2, 0.2), -5.5, -4.0)
    state_rate = draw_state_rate(jax.random.fold_in(key_of[19], 71), 0)
    skip = jnp.clip(0.5 + 1.0 * jax.random.uniform(key_of[13], (E,), jnp.float32) ** levels(key_of[13], (E,), ((0, 2),), -0.2, 0.2), 0.5, 1.5)
    w_out = gaussian(key_of[14], (E, D), E ** -0.5, 0.109375, ((0, 2),))
    norm2_gain = jnp.clip(1.0 + 0.1 * jax.random.normal(key_of[15], (D,), jnp.float32), 0.5, 1.5)
    w_gu = gaussian(key_of[16], (D, 2, FF), D ** -0.5, 0.15625, ((2, 2),))
    w_down = gaussian(key_of[17], (FF, D), FF ** -0.5, 0.09375, ((0, 2),))
    d_out = gaussian(key_of[18], (TOKENS, D), 1.0, 6.0, ((0, 16),))
    return dict(x_in=x_in, doc_start=doc_start, norm1_gain=norm1_gain, input_weight=input_weight, conv_w=conv_w, conv_b=conv_b, w_x=w_x, dt_gain=dt_gain, b_gain=b_gain, c_gain=c_gain, w_dt=w_dt, dt_bias=dt_bias, state_rate=state_rate, skip=skip, w_out=w_out, norm2_gain=norm2_gain, w_gu=w_gu, w_down=w_down, d_out=d_out)


@jax.custom_vjp
def low(v):
    return lax.optimization_barrier(v.astype(jnp.bfloat16)).astype(jnp.float32)

@jax.custom_vjp
def low_back(v):
    return v

def low_keep(v):
    return (low(v), None)

def low_pass(kept, grad):
    return (grad,)

def back_keep(v):
    return (v, None)

def back_low(kept, grad):
    return (low(grad),)
low.defvjp(low_keep, low_pass)
low_back.defvjp(back_keep, back_low)
EPSILON = 1e-06
PRECISION_LEVEL = lax.Precision.HIGHEST

def rms_scale(values_in, norm_gain):
    return values_in * lax.rsqrt(lax.optimization_barrier(jnp.mean(values_in * values_in, axis=-1, keepdims=True)) + EPSILON) * norm_gain

def pair_combine(earlier, latter):
    return (earlier[0] * latter[0], latter[0] * earlier[1] + latter[1])

def block_states(start_state, step_blk, b_blk, c_blk, input_blk, keep_blk, rate_in):
    decays = jnp.exp(-step_blk[:, :, None] * rate_in[None]) * keep_blk[:, None, None]
    drives = (step_blk * input_blk)[:, :, None] * b_blk[:, None, :]
    prod_all, sum_all = lax.associative_scan(pair_combine, (decays, drives), axis=0)
    states = prod_all * start_state[None] + sum_all
    outputs = lax.optimization_barrier(jnp.sum(states * c_blk[:, None, :], axis=-1))
    return (states[-1], outputs)

def mixer_scan(step_sizes, b_rows, c_rows, mixed_act, keep_flags, rate_in):
    nblocks = step_sizes.shape[0] // BLOCK

    def blocked(array_in):
        return array_in.reshape((nblocks, BLOCK) + array_in.shape[1:])

    def one_block(state_now, pieces):
        step_blk, b_blk, c_blk, input_blk, keep_blk = pieces
        return jax.checkpoint(block_states)(state_now, step_blk, b_blk, c_blk, input_blk, keep_blk, rate_in)
    initial = jnp.zeros(rate_in.shape, jnp.float32)
    unused, outputs = lax.scan(one_block, initial, (blocked(step_sizes), blocked(b_rows), blocked(c_rows), blocked(mixed_act), blocked(keep_flags)))
    return outputs.reshape(step_sizes.shape)

def conv_mix(inner, segment_ids, conv_w, conv_b):
    totals = conv_b[None] + conv_w[3][None] * inner
    for offset in (1, 2, 3):
        shifted = jnp.concatenate([jnp.zeros((offset, inner.shape[1]), jnp.float32), inner[:-offset]], 0)
        seg_shift = jnp.concatenate([jnp.full((offset,), -1, jnp.int32), segment_ids[:-offset]], 0)
        same_doc = (seg_shift == segment_ids).astype(jnp.float32)
        totals = totals + conv_w[3 - offset][None] * shifted * same_doc[:, None]
    return totals

def layer(x_val, norm1_gain, input_weight, conv_w, conv_b, w_x, dt_gain, b_gain, c_gain, w_dt, dt_bias, state_rate, skip, w_out, norm2_gain, w_gu, w_down, segment_ids, keep_flags):
    normalized_input = low(rms_scale(x_val, norm1_gain))
    inner_and_gate = low(low_back(jnp.einsum('kv,vjm->kjm', normalized_input, input_weight, precision=PRECISION_LEVEL)))
    inner, gate_z = (inner_and_gate[:, 0], inner_and_gate[:, 1])
    mixed_act = jax.nn.silu(conv_mix(inner, segment_ids, conv_w, conv_b))
    projected = low_back(jnp.dot(low(mixed_act), w_x, precision=PRECISION_LEVEL))
    step_norm = low(rms_scale(projected[:, :R], dt_gain))
    b_rows = rms_scale(projected[:, R:R + N], b_gain)
    c_rows = rms_scale(projected[:, R + N:], c_gain)
    step_sizes = jax.nn.softplus(low_back(jnp.dot(step_norm, w_dt, precision=PRECISION_LEVEL)) + dt_bias)
    scanned = mixer_scan(step_sizes, b_rows, c_rows, mixed_act, keep_flags, state_rate) + skip * mixed_act
    gated_low = low(scanned * jax.nn.silu(gate_z))
    resid_mid = x_val + low_back(jnp.dot(gated_low, w_out, precision=PRECISION_LEVEL))
    normed_two = low(rms_scale(resid_mid, norm2_gain))
    gate_up = low_back(jnp.einsum('td,dsf->tsf', normed_two, w_gu, precision=PRECISION_LEVEL))
    hidden = low(jax.nn.silu(gate_up[:, 0]) * gate_up[:, 1])
    return resid_mid + low_back(jnp.dot(hidden, w_down, precision=PRECISION_LEVEL))

def reference(x_in, doc_start, norm1_gain, input_weight, conv_w, conv_b, w_x, dt_gain, b_gain, c_gain, w_dt, dt_bias, state_rate, skip, w_out, norm2_gain, w_gu, w_down, d_out):
    segment_ids = jnp.cumsum(doc_start).astype(jnp.int32)
    keep_flags = (1 - doc_start).astype(jnp.float32)
    params = (x_in.astype(jnp.float32), norm1_gain, input_weight.astype(jnp.float32), conv_w, conv_b, w_x.astype(jnp.float32), dt_gain, b_gain, c_gain, w_dt.astype(jnp.float32), dt_bias, state_rate, skip, w_out.astype(jnp.float32), norm2_gain, w_gu.astype(jnp.float32), w_down.astype(jnp.float32))

    def run_layer(*values):
        return layer(*values, segment_ids, keep_flags)
    result, pull_back = jax.vjp(run_layer, *params)
    gradients = pull_back(d_out.astype(jnp.float32))
    return (result.astype(jnp.bfloat16), gradients[0], gradients[1], gradients[2], gradients[3], gradients[4], gradients[5], gradients[6], gradients[7], gradients[8], gradients[9], gradients[10], gradients[11], gradients[12], gradients[13], gradients[14], gradients[15], gradients[16])
```

```python
import functools
import math

import jax
import jax.numpy as jnp
from jax import lax
from jax.experimental import pallas as pl
from jax.experimental.pallas import tpu as pltpu
from jax.sharding import PartitionSpec as P

EPSILON = 1e-06
LANES = 128
CG = 4
WIDTH = CG * LANES
PLANE = 4
LOG2E = math.log2(math.e)
LN2 = math.log(2.0)
MESH = pl.DeviceIdType.MESH
VMEM_BYTES = 56 * 1024 * 1024


def swap_cores(value):
    return lax.ppermute(value, "head", [(0, 1), (1, 0)])


def sum_cores(value):
    return value + swap_cores(value)


def from_behind(value, axis, steps):
    count = lax.axis_size(axis)
    initial, last = (max(0, -steps), min(count, count - steps))
    return lax.ppermute(value, axis, [(source, source + steps) for source in range(initial, last)])


def rms_scale(values_in, norm_gain):
    return (
        values_in
        * lax.rsqrt(jnp.mean(values_in * values_in, axis=-1, keepdims=True) + EPSILON)
        * norm_gain
    )


def spread_rows(source, target, states):
    tokens = source.shape[0]

    def step(block, carry):
        rows = source[pl.ds(pl.multiple_of(block * 8, 8), 8), :]
        for n in range(states):
            column = jnp.broadcast_to(rows[:, n : n + 1], (8, LANES))
            for group in range(CG):
                at = block * (8 * states * CG) + n * CG + group
                target[pl.ds(at, 8, stride=states * CG), :] = column
        return carry

    lax.fori_loop(0, tokens // 8, step, 0)


def spread_channels(read, target, tokens):
    def step(block, carry):
        for group in range(CG):
            value = read(block, group)
            target[pl.ds(block * 64 + group, 8, stride=8), :] = value
            target[pl.ds(block * 64 + CG + group, 8, stride=8), :] = value
        return carry

    lax.fori_loop(0, tokens // 8, step, 0)


def pick(ref, block, group):
    return ref[pl.ds(pl.multiple_of(block * 8, 8), 8), group * LANES : (group + 1) * LANES]


def fold_channels(source, block, group):
    return (
        source[pl.ds(block * 64 + group, 8, stride=8), :]
        + source[pl.ds(block * 64 + CG + group, 8, stride=8), :]
    )


def fold_states(source, target, states):
    tokens = target.shape[0]
    lane = lax.broadcasted_iota(jnp.int32, (8, states), 1)

    def step(block, carry):
        out = jnp.zeros((8, states), jnp.float32)
        for n in range(states):
            total = None
            for group in range(CG):
                at = block * (8 * states * CG) + n * CG + group
                part = source[pl.ds(at, 8, stride=states * CG), :]
                total = part if total is None else total + part
            out = jnp.where(lane == n, jnp.sum(total, axis=1, keepdims=True), out)
        target[pl.ds(pl.multiple_of(block * 8, 8), 8), :] = out
        return carry

    lax.fori_loop(0, tokens // 8, step, 0)


def rows8(ref, at):
    return ref[pl.ds(pl.multiple_of(at, 8), 8), :]


def state_rows(ref, p):
    per = ref.shape[2] // 8
    return ref[p // per, 0, (p % per) * 8 : (p % per) * 8 + 8, :]


def end_kernel(reverse, states, step_ref, other_ref, rows_ref, keep_ref, rate_ref, end_ref, sum_ref, steps, drive, spread):
    tokens = step_ref.shape[0]
    pairs = states // 2
    span = states * CG

    @pl.when(pl.program_id(0) == 0)
    def _():
        spread_rows(rows_ref, spread, states)

    spread_channels(functools.partial(pick, step_ref), steps, tokens)
    if reverse:
        spread_channels(functools.partial(pick, other_ref), drive, tokens)
    else:
        spread_channels(lambda b, g: pick(step_ref, b, g) * pick(other_ref, b, g), drive, tokens)
    rates = [rate_ref[0, p * 8 : p * 8 + 8, :] for p in range(pairs)]

    def body(k, carry):
        total, values = carry
        t = tokens - 1 - k if reverse else k
        size = rows8(steps, t * 8)
        push = rows8(drive, t * 8)
        keep = keep_ref[t]
        new = []
        for p in range(pairs):
            decay = jnp.exp2(size * rates[p])
            term = push * rows8(spread, t * span + p * 8)
            if reverse:
                new.append(decay * ((values[p] + term) * keep))
            else:
                new.append(decay * (values[p] * keep) + term)
        return total + size, tuple(new)

    zero = jnp.zeros((8, LANES), jnp.float32)
    total, values = lax.fori_loop(0, tokens, body, (zero, (zero,) * pairs), unroll=4)
    for p in range(pairs):
        end_ref[0, p * 8 : p * 8 + 8, :] = values[p]
    sum_ref[0] = total


def run_kernel(states, step_ref, mix_ref, b_ref, c_ref, keep_ref, rate_ref, start_ref, out_ref, seen_ref, last_ref, steps, drive, outs, b_spread, c_spread):
    tokens = step_ref.shape[0]
    pairs = states // 2
    span = states * CG

    @pl.when(pl.program_id(0) == 0)
    def _():
        spread_rows(b_ref, b_spread, states)
        spread_rows(c_ref, c_spread, states)

    spread_channels(functools.partial(pick, step_ref), steps, tokens)
    spread_channels(lambda b, g: pick(step_ref, b, g) * pick(mix_ref, b, g), drive, tokens)
    rates = [rate_ref[0, p * 8 : p * 8 + 8, :] for p in range(pairs)]

    def body(t, values):
        size = rows8(steps, t * 8)
        push = rows8(drive, t * 8)
        keep = keep_ref[t]
        new = []
        result = None
        for p in range(pairs):
            at = pl.multiple_of(t * span + p * 8, 8)
            seen_ref[0, pl.ds(at, 8), :] = values[p]
            decay = jnp.exp2(size * rates[p])
            value = decay * (values[p] * keep) + push * rows8(b_spread, at)
            term = value * rows8(c_spread, at)
            result = term if result is None else result + term
            new.append(value)
        outs[pl.ds(pl.multiple_of(t * 8, 8), 8), :] = result
        return tuple(new)

    values = lax.fori_loop(0, tokens, body, tuple(state_rows(start_ref, p) for p in range(pairs)), unroll=4)
    for p in range(pairs):
        last_ref[0, p * 8 : p * 8 + 8, :] = values[p]

    def finish(block, carry):
        for group in range(CG):
            out_ref[pl.ds(pl.multiple_of(block * 8, 8), 8), group * LANES : (group + 1) * LANES] = fold_channels(outs, block, group)
        return carry

    lax.fori_loop(0, tokens // 8, finish, 0)


def back_kernel(states, groups, step_ref, mix_ref, grad_ref, b_ref, c_ref, keep_ref, rate_ref, after_ref, seen_ref, last_ref,
                gstep_ref, gmix_ref, gb_ref, gc_ref, grate_ref,
                steps, drive, grads, lam_b, rate_q, b_spread, c_spread, b_grad, c_grad):
    tokens = step_ref.shape[0]
    pairs = states // 2
    span = states * CG
    zero = jnp.zeros((8, LANES), jnp.float32)

    @pl.when(pl.program_id(0) == 0)
    def _():
        spread_rows(b_ref, b_spread, states)
        spread_rows(c_ref, c_spread, states)

        def clear(t, carry):
            for p in range(pairs):
                at = pl.multiple_of(t * span + p * 8, 8)
                b_grad[pl.ds(at, 8), :] = zero
                c_grad[pl.ds(at, 8), :] = zero
            return carry

        lax.fori_loop(0, tokens, clear, 0)

    spread_channels(functools.partial(pick, step_ref), steps, tokens)
    spread_channels(functools.partial(pick, grad_ref), grads, tokens)
    spread_channels(lambda b, g: pick(step_ref, b, g) * pick(mix_ref, b, g), drive, tokens)
    rates = [rate_ref[0, p * 8 : p * 8 + 8, :] for p in range(pairs)]

    def body(k, carry):
        mus, states_now, rate_grads = carry
        t = tokens - 1 - k
        size = rows8(steps, t * 8)
        push = rows8(drive, t * 8)
        grad = rows8(grads, t * 8)
        keep = keep_ref[t]
        new_mu, new_state, new_rate = [], [], []
        lb = rq = None
        for p in range(pairs):
            at = pl.multiple_of(t * span + p * 8, 8)
            before = seen_ref[0, pl.ds(at, 8), :]
            b_value = rows8(b_spread, at)
            lam = rows8(c_spread, at) * grad + mus[p]
            mu = (jnp.exp2(size * rates[p]) * keep) * lam
            q = mu * before
            b_term = lam * b_value
            r_term = rates[p] * q
            lb = b_term if lb is None else lb + b_term
            rq = r_term if rq is None else rq + r_term
            b_grad[pl.ds(at, 8), :] += lam * push
            c_grad[pl.ds(at, 8), :] += states_now[p] * grad
            new_mu.append(mu)
            new_state.append(before)
            new_rate.append(rate_grads[p] + q * size)
        lam_b[pl.ds(pl.multiple_of(t * 8, 8), 8), :] = lb
        rate_q[pl.ds(pl.multiple_of(t * 8, 8), 8), :] = rq
        return tuple(new_mu), tuple(new_state), tuple(new_rate)

    start = (
        tuple(state_rows(after_ref, p) for p in range(pairs)),
        tuple(last_ref[0, p * 8 : p * 8 + 8, :] for p in range(pairs)),
        (zero,) * pairs,
    )
    unused_mu, unused_state, rate_grads = lax.fori_loop(0, tokens, body, start, unroll=4)
    for p in range(pairs):
        grate_ref[0, p * 8 : p * 8 + 8, :] = -rate_grads[p]

    def finish(block, carry):
        for group in range(CG):
            lb = fold_channels(lam_b, block, group)
            rq = fold_channels(rate_q, block, group)
            at = (pl.ds(pl.multiple_of(block * 8, 8), 8), slice(group * LANES, (group + 1) * LANES))
            gmix_ref[at] = pick(step_ref, block, group) * lb
            gstep_ref[at] = pick(mix_ref, block, group) * lb + LN2 * rq
        return carry

    lax.fori_loop(0, tokens // 8, finish, 0)

    @pl.when(pl.program_id(0) == groups - 1)
    def _():
        fold_states(b_grad, gb_ref, states)
        fold_states(c_grad, gc_ref, states)


def f32(*shape):
    return jax.ShapeDtypeStruct(shape, jnp.float32)


def scan_specs(tokens, states):
    span = states * CG
    return dict(
        channels=pl.BlockSpec((tokens, WIDTH), lambda g: (0, g)),
        rows=pl.BlockSpec((tokens, states), lambda g: (0, 0)),
        keep=pl.BlockSpec(memory_space=pltpu.SMEM),
        state=pl.BlockSpec((1, span, LANES), lambda g: (g, 0, 0)),
        total=pl.BlockSpec((1, 8, LANES), lambda g: (g, 0, 0)),
        parts=pl.BlockSpec((PLANE, 1, span // PLANE, LANES), lambda g: (0, g, 0, 0)),
        seen=pl.BlockSpec((1, tokens * span, LANES), lambda g: (g, 0, 0)),
    )


def params(**more):
    return pltpu.CompilerParams(vmem_limit_bytes=VMEM_BYTES, **more)


def scan_end(reverse, steps, other, rows, keep, rates):
    tokens, states = rows.shape
    groups, span, unused = rates.shape
    spec = scan_specs(tokens, states)
    return pl.pallas_call(
        functools.partial(end_kernel, reverse, states),
        grid=(groups,),
        out_shape=(f32(groups, span, LANES), f32(groups, 8, LANES)),
        in_specs=[spec["channels"], spec["channels"], spec["rows"], spec["keep"], spec["state"]],
        out_specs=(spec["state"], spec["total"]),
        scratch_shapes=[pltpu.VMEM((tokens * 8, LANES), jnp.float32)] * 2 + [pltpu.VMEM((tokens * span, LANES), jnp.float32)],
        compiler_params=params(),
        name="feed" if reverse else "end",
    )(steps, other, rows, keep, rates)


def scan_run(steps, mixed, b_rows, c_rows, keep, rates, start):
    tokens, states = b_rows.shape
    groups, span, unused = rates.shape
    spec = scan_specs(tokens, states)
    return pl.pallas_call(
        functools.partial(run_kernel, states),
        grid=(groups,),
        out_shape=(f32(*steps.shape), f32(groups, tokens * span, LANES), f32(groups, span, LANES)),
        in_specs=[spec["channels"], spec["channels"], spec["rows"], spec["rows"], spec["keep"], spec["state"], spec["parts"]],
        out_specs=(spec["channels"], spec["seen"], spec["state"]),
        scratch_shapes=[pltpu.VMEM((tokens * 8, LANES), jnp.float32)] * 3 + [pltpu.VMEM((tokens * span, LANES), jnp.float32)] * 2,
        compiler_params=params(),
        name="run",
    )(steps, mixed, b_rows, c_rows, keep, rates, start)


def scan_back(steps, mixed, grads, b_rows, c_rows, keep, rates, after, seen, last):
    tokens, states = b_rows.shape
    groups, span, unused = rates.shape
    spec = scan_specs(tokens, states)
    return pl.pallas_call(
        functools.partial(back_kernel, states, groups),
        grid=(groups,),
        out_shape=(f32(*steps.shape), f32(*steps.shape), f32(tokens, states), f32(tokens, states), f32(groups, span, LANES)),
        in_specs=[spec["channels"]] * 3 + [spec["rows"]] * 2 + [spec["keep"], spec["state"], spec["parts"], spec["seen"], spec["state"]],
        out_specs=(spec["channels"], spec["channels"], spec["rows"], spec["rows"], spec["state"]),
        scratch_shapes=[pltpu.VMEM((tokens * 8, LANES), jnp.float32)] * 5 + [pltpu.VMEM((tokens * span, LANES), jnp.float32)] * 4,
        compiler_params=params(),
        name="back",
    )(steps, mixed, grads, b_rows, c_rows, keep, rates, after, seen, last)


def rates_in(state_rate):
    channels, states = state_rate.shape
    groups = channels // WIDTH
    parts = state_rate.reshape(groups, CG, LANES, states)
    return jnp.transpose(parts, (0, 3, 1, 2)).reshape(groups, states * CG, LANES) * (-LOG2E)


def rates_out(grad):
    groups, span, lanes = grad.shape
    parts = grad.reshape(groups, span // CG, CG, lanes)
    return jnp.transpose(parts, (0, 2, 3, 1)).reshape(groups * WIDTH, span // CG)


def carry_kernel(planes, reverse, end_ref, sum_ref, rate_ref, out_ref, pay, got, zpay, zgot, back, final,
                 send_a, recv_a, send_b, recv_b, send_c, recv_c):
    me = lax.axis_index("seq")
    low = lax.rem(me, PLANE)
    high = lax.div(me, PLANE)
    quarter = end_ref.shape[1] // PLANE

    def in_plane(shift):
        return high * PLANE + lax.rem(low + shift, PLANE)

    def across(shift):
        return lax.rem(high + shift, planes) * PLANE + low

    barrier = pltpu.get_barrier_semaphore()
    for shift in range(1, PLANE):
        pl.semaphore_signal(barrier, inc=1, device_id={"seq": in_plane(shift)}, device_id_type=MESH)
    for shift in range(1, planes):
        pl.semaphore_signal(barrier, inc=1, device_id={"seq": across(shift)}, device_id_type=MESH)

    for k in range(PLANE):
        pay[k, :, :quarter, :] = end_ref[:, k * quarter : (k + 1) * quarter, :]
        pay[k, :, quarter:, :] = sum_ref[...]
    pl.semaphore_wait(barrier, PLANE - 1 + planes - 1)

    copies = []
    for shift in range(1, PLANE):
        copy = pltpu.make_async_remote_copy(
            src_ref=pay.at[lax.rem(low + shift, PLANE)],
            dst_ref=got.at[shift],
            send_sem=send_a.at[shift],
            recv_sem=recv_a.at[shift],
            device_id={"seq": in_plane(shift)},
            device_id_type=MESH,
        )
        copy.start()
        copies.append(copy)
    got[0] = pay[low]
    rates = rate_ref[low]
    for copy in copies:
        copy.wait()

    def decay(total):
        rows = rates.shape[1] // 8
        return jnp.exp2(rates * jnp.concatenate([total] * rows, axis=1))

    order = range(PLANE - 1, -1, -1) if reverse else range(PLANE)
    ends, decays = {}, {}
    plane_end = plane_sum = None
    for j in order:
        slot = lax.rem(low - j + PLANE, PLANE)
        part = got[slot]
        ends[j] = part[:, :quarter, :]
        size = part[:, quarter:, :]
        decays[j] = decay(size)
        plane_end = ends[j] if plane_end is None else plane_end * decays[j] + ends[j]
        plane_sum = size if plane_sum is None else plane_sum + size

    zpay[:, :quarter, :] = plane_end
    zpay[:, quarter:, :] = plane_sum
    copies = []
    for shift in range(1, planes):
        copy = pltpu.make_async_remote_copy(
            src_ref=zpay,
            dst_ref=zgot.at[shift],
            send_sem=send_b.at[shift],
            recv_sem=recv_b.at[shift],
            device_id={"seq": across(shift)},
            device_id_type=MESH,
        )
        copy.start()
        copies.append(copy)
    zgot[0] = zpay[...]
    for copy in copies:
        copy.wait()

    state = jnp.zeros_like(plane_end)
    for h in range(planes - 1, -1, -1) if reverse else range(planes):
        part = zgot[lax.rem(high - h + planes, planes)]
        after = state * decay(part[:, quarter:, :]) + part[:, :quarter, :]
        reached = h > high if reverse else h < high
        state = jnp.where(reached, after, state)

    for j in order:
        back[j] = state
        state = state * decays[j] + ends[j]
    copies = []
    for shift in range(1, PLANE):
        copy = pltpu.make_async_remote_copy(
            src_ref=back.at[lax.rem(low + shift, PLANE)],
            dst_ref=final.at[low],
            send_sem=send_c.at[shift],
            recv_sem=recv_c.at[shift],
            device_id={"seq": in_plane(shift)},
            device_id_type=MESH,
        )
        copy.start()
        copies.append(copy)
    final[low] = back[low]
    for copy in copies:
        copy.wait()
    out_ref[...] = final[...]


def carry(reverse, ends, sums, rates):
    groups, span, unused = rates.shape
    quarter = span // PLANE
    planes = lax.axis_size("seq") // PLANE
    vmem = pl.BlockSpec(memory_space=pltpu.VMEM)
    rate_parts = jnp.transpose(rates.reshape(groups, PLANE, quarter, LANES), (1, 0, 2, 3))
    dma = pltpu.SemaphoreType.DMA
    return pl.pallas_call(
        functools.partial(carry_kernel, planes, reverse),
        out_shape=f32(PLANE, groups, quarter, LANES),
        in_specs=[vmem] * 3,
        out_specs=vmem,
        scratch_shapes=[
            pltpu.VMEM((PLANE, groups, quarter + 8, LANES), jnp.float32),
            pltpu.VMEM((PLANE, groups, quarter + 8, LANES), jnp.float32),
            pltpu.VMEM((groups, quarter + 8, LANES), jnp.float32),
            pltpu.VMEM((planes, groups, quarter + 8, LANES), jnp.float32),
            pltpu.VMEM((PLANE, groups, quarter, LANES), jnp.float32),
            pltpu.VMEM((PLANE, groups, quarter, LANES), jnp.float32),
            dma((PLANE,)), dma((PLANE,)), dma((planes,)), dma((planes,)), dma((PLANE,)), dma((PLANE,)),
        ],
        compiler_params=params(collective_id=2 if reverse else 1, has_side_effects=True),
        name="carry_back" if reverse else "carry",
    )(ends, sums, rate_parts)


def plane_perm(shift):
    count = lax.axis_size("seq")
    return [(s, s - s % PLANE + (s + shift) % PLANE) for s in range(count)]


def gather_plane(value):
    return [value] + [lax.ppermute(value, "seq", plane_perm(shift)) for shift in range(1, PLANE)]


def gather_rows(value):
    tokens, width = value.shape
    count = lax.axis_size("seq")
    planes = count // PLANE
    low = lax.axis_index("seq") % PLANE
    parts = jnp.transpose(value.reshape(tokens, planes, PLANE, width // count), (2, 1, 0, 3))

    def of(index):
        return lax.dynamic_index_in_dim(parts, index, 0, keepdims=False)

    return [of(low)] + [
        lax.ppermute(of((low + shift) % PLANE), "seq", plane_perm(shift)) for shift in range(1, PLANE)
    ]


def weight_grad(rows, columns):
    count = lax.axis_size("seq")
    planes = count // PLANE
    high = lax.axis_index("seq") // PLANE
    left = jnp.concatenate(rows, 1)
    right = jnp.concatenate(columns, 0)

    def product(which):
        return jnp.einsum("ptd,tc->pdc", which, right, preferred_element_type=jnp.float32)

    steps = planes.bit_length() - 1
    width = left.shape[2]
    held = left.reshape((2,) * steps + left.shape[1:])
    total = None
    for k in range(steps):
        bit = (high >> k) & 1
        axis = steps - 1 - k
        if total is None:
            send = lax.dynamic_index_in_dim(held, 1 - bit, axis, keepdims=False)
            keep = lax.dynamic_index_in_dim(held, bit, axis, keepdims=False)
            rest = send.shape[:-2]
            send = product(send.reshape((-1,) + send.shape[-2:])).astype(jnp.bfloat16)
            got = lax.ppermute(send, "seq", [(s, s ^ (PLANE << k)) for s in range(count)])
            total = product(keep.reshape((-1,) + keep.shape[-2:])) + got.astype(jnp.float32)
            total = total.reshape(rest + total.shape[-2:])
        else:
            send = lax.dynamic_index_in_dim(total, 1 - bit, axis, keepdims=False).astype(jnp.bfloat16)
            keep = lax.dynamic_index_in_dim(total, bit, axis, keepdims=False)
            total = keep + lax.ppermute(send, "seq", [(s, s ^ (PLANE << k)) for s in range(count)]).astype(jnp.float32)
    return total


def conv_local(padded, conv_w, conv_b, lag_masks):
    token_count = padded.shape[0] - 3
    totals = conv_b[None] + conv_w[3][None] * padded[3:]
    for offset in (1, 2, 3):
        totals = (
            totals
            + conv_w[3 - offset][None]
            * padded[3 - offset : 3 - offset + token_count]
            * lag_masks[offset - 1][:, None]
        )
    return totals


def gate_norms(projected, step_gain, b_gain_in, c_gain_in):
    rank_size = step_gain.shape[0]
    state_size = b_gain_in.shape[0]
    return (
        rms_scale(projected[:, :rank_size], step_gain),
        rms_scale(projected[:, rank_size : rank_size + state_size], b_gain_in),
        rms_scale(projected[:, rank_size + state_size :], c_gain_in),
    )


def silu_slope(values_in):
    sigmoid_val = jax.nn.sigmoid(values_in)
    return sigmoid_val * (1.0 + values_in * (1.0 - sigmoid_val))


def local(
    x_in,
    doc_start,
    norm1_gain,
    input_weight,
    conv_w,
    conv_b,
    w_x,
    dt_gain,
    b_gain,
    c_gain,
    w_dt,
    dt_bias,
    state_rate,
    skip,
    w_out,
    norm2_gain,
    w_gu,
    w_down,
    d_out,
):
    tokens_here = x_in.shape[0]
    rank_size = dt_gain.shape[0]
    state_size = b_gain.shape[0]
    resid_in = x_in.astype(jnp.float32)
    keep_flags = (1 - doc_start).astype(jnp.float32)
    rates = rates_in(state_rate)

    normalized_input, norm_pull = jax.vjp(rms_scale, resid_in, norm1_gain)
    normalized_reduced = normalized_input.astype(jnp.bfloat16)
    both_low = jnp.einsum(
        "kv,vjm->kjm", normalized_reduced, input_weight, preferred_element_type=jnp.float32
    ).astype(jnp.bfloat16)
    inner_low = both_low[:, 0]
    gate_z = both_low[:, 1].astype(jnp.float32)
    tail_keep = jnp.stack(
        [keep_flags[-2] * keep_flags[-1], keep_flags[-1], jnp.ones((), jnp.float32)]
    )
    edge_send = (inner_low[-3:].astype(jnp.float32) * tail_keep[:, None]).astype(jnp.bfloat16)
    edge_recv = from_behind(edge_send, "seq", 1)
    padded = jnp.concatenate([edge_recv, inner_low], 0).astype(jnp.float32)
    padded_keep = jnp.concatenate([jnp.ones((3,), jnp.float32), keep_flags])
    lag_one = padded_keep[3:]
    lag_two = lag_one * padded_keep[2:-1]
    lag_three = lag_two * padded_keep[1:-2]
    lag_masks = (lag_one, lag_two, lag_three)

    def conv_part(padded_in, weight_in, bias_in):
        return conv_local(padded_in, weight_in, bias_in, lag_masks)

    conv_out, conv_pull = jax.vjp(conv_part, padded, conv_w, conv_b)
    mixed_act = jax.nn.silu(conv_out)
    mixed_low = mixed_act.astype(jnp.bfloat16)
    projected = sum_cores(jnp.dot(mixed_low, w_x, preferred_element_type=jnp.float32))
    (step_norm, b_rows, c_rows), gate_pull = jax.vjp(gate_norms, projected, dt_gain, b_gain, c_gain)
    step_low = step_norm.astype(jnp.bfloat16)
    step_pre = jnp.dot(step_low, w_dt, preferred_element_type=jnp.float32) + dt_bias
    step_sizes = jax.nn.softplus(step_pre)
    ends, sums = scan_end(False, step_sizes, mixed_act, b_rows, keep_flags, rates)
    state_in = carry(False, ends, sums, rates)
    scan_out, seen, last = scan_run(step_sizes, mixed_act, b_rows, c_rows, keep_flags, rates, state_in)
    scanned = scan_out + skip * mixed_act
    gate_act = jax.nn.silu(gate_z)
    gated_low = (scanned * gate_act).astype(jnp.bfloat16)
    mix_out = sum_cores(jnp.dot(gated_low, w_out, preferred_element_type=jnp.float32))
    resid_mid = resid_in + mix_out
    normed_two, norm_two_pull = jax.vjp(rms_scale, resid_mid, norm2_gain)
    normed_two_low = normed_two.astype(jnp.bfloat16)
    gate_up = jnp.einsum("td,dsf->tsf", normed_two_low, w_gu, preferred_element_type=jnp.float32)
    gate_part = gate_up[:, 0]
    up_part = gate_up[:, 1]
    gate_silu = jax.nn.silu(gate_part)
    hidden_low = (gate_silu * up_part).astype(jnp.bfloat16)
    ffn_out = sum_cores(jnp.dot(hidden_low, w_down, preferred_element_type=jnp.float32))
    output = (resid_mid + ffn_out).astype(jnp.bfloat16)
    grad_out = d_out.astype(jnp.float32)
    out_rows = gather_rows(d_out)
    red_down = weight_grad(out_rows, gather_plane(hidden_low)).T
    grad_hidden = jnp.einsum("td,fd->tf", d_out, w_down, preferred_element_type=jnp.float32)
    grad_gate = grad_hidden * up_part * silu_slope(gate_part)
    grad_up = grad_hidden * gate_silu
    grad_gate_low = grad_gate.astype(jnp.bfloat16)
    grad_up_low = grad_up.astype(jnp.bfloat16)
    two_rows = gather_rows(normed_two_low)
    red_gu = jnp.stack(
        [
            weight_grad(two_rows, gather_plane(grad_gate_low)),
            weight_grad(two_rows, gather_plane(grad_up_low)),
        ],
        1,
    )
    grad_gu_low = jnp.stack([grad_gate_low, grad_up_low], 1)
    grad_normed_two = sum_cores(
        jnp.einsum("tsf,dsf->td", grad_gu_low, w_gu, preferred_element_type=jnp.float32)
    )
    grad_mid_norm, grad_norm_two = norm_two_pull(grad_normed_two)
    grad_mid = grad_out + grad_mid_norm
    grad_mix_low = grad_mid.astype(jnp.bfloat16)
    red_out = weight_grad(gather_rows(grad_mix_low), gather_plane(gated_low)).T
    grad_gated = jnp.einsum("td,cd->tc", grad_mix_low, w_out, preferred_element_type=jnp.float32)
    grad_scanned = grad_gated * gate_act
    grad_z = grad_gated * scanned * silu_slope(gate_z)
    grad_skip = jnp.sum(grad_scanned * mixed_act, 0)
    one_rows = gather_rows(normalized_reduced)
    grad_z_low = grad_z.astype(jnp.bfloat16)
    red_in_z = weight_grad(one_rows, gather_plane(grad_z_low))
    feeds, unused_sums = scan_end(True, step_sizes, grad_scanned, c_rows, keep_flags, rates)
    grad_after = carry(True, feeds, sums, rates)
    grad_steps, grad_mix_scan, grad_b_all, grad_c_all, grad_rates = scan_back(
        step_sizes, mixed_act, grad_scanned, b_rows, c_rows, keep_flags, rates, grad_after, seen, last
    )
    grad_rate = rates_out(grad_rates)
    grad_mixed = grad_scanned * skip + grad_mix_scan
    grad_pre = grad_steps * jax.nn.sigmoid(step_pre)
    grad_dt_bias = jnp.sum(grad_pre, 0)
    grad_pre_low = grad_pre.astype(jnp.bfloat16)
    grad_w_dt = jnp.einsum("tr,tc->rc", step_low, grad_pre_low, preferred_element_type=jnp.float32)
    grad_step_part = jnp.einsum("tc,rc->tr", grad_pre_low, w_dt, preferred_element_type=jnp.float32)
    summed = sum_cores(jnp.concatenate([grad_step_part, grad_b_all, grad_c_all], 1))
    grad_proj, grad_dt_gain, grad_b_gain, grad_c_gain = gate_pull(
        (
            summed[:, :rank_size],
            summed[:, rank_size : rank_size + state_size],
            summed[:, rank_size + state_size :],
        )
    )
    grad_proj_low = grad_proj.astype(jnp.bfloat16)
    grad_w_x = jnp.einsum("tc,tk->ck", mixed_low, grad_proj_low, preferred_element_type=jnp.float32)
    grad_mixed = grad_mixed + jnp.einsum(
        "tk,ck->tc", grad_proj_low, w_x, preferred_element_type=jnp.float32
    )
    grad_conv_out = grad_mixed * silu_slope(conv_out)
    grad_padded, grad_conv_w, grad_conv_b = conv_pull(grad_conv_out)
    edge_grad = from_behind(grad_padded[:3], "seq", -1)
    grad_inner = jnp.concatenate(
        [grad_padded[3:-3], grad_padded[-3:] + edge_grad * tail_keep[:, None]], 0
    )
    grad_inner_low = grad_inner.astype(jnp.bfloat16)
    red_in = jnp.stack([weight_grad(one_rows, gather_plane(grad_inner_low)), red_in_z], 1)
    grad_normed = sum_cores(
        jnp.einsum(
            "ary,jry->aj",
            jnp.stack([grad_inner_low, grad_z_low], 1),
            input_weight,
            preferred_element_type=jnp.float32,
        )
    )
    grad_in_norm, grad_norm_one = norm_pull(grad_normed)
    grad_input = grad_mid + grad_in_norm
    small_sums = lax.psum(
        (
            grad_dt_gain,
            grad_b_gain,
            grad_c_gain,
            grad_conv_w,
            grad_conv_b,
            grad_dt_bias,
            grad_rate,
            grad_skip,
            grad_w_x,
            grad_w_dt,
        ),
        "seq",
    )
    red_norm_one, red_norm_two = (
        lax.psum_scatter(grad_norm_one, "seq", scatter_dimension=0, tiled=True),
        lax.psum_scatter(grad_norm_two, "seq", scatter_dimension=0, tiled=True),
    )
    return (
        output,
        grad_input,
        red_norm_one,
        red_in,
        small_sums[3],
        small_sums[4],
        small_sums[8],
        small_sums[0],
        small_sums[1],
        small_sums[2],
        small_sums[9],
        small_sums[5],
        small_sums[6],
        small_sums[7],
        red_out,
        red_norm_two,
        red_gu,
        red_down,
    )


def solution(mesh):
    placed = (
        P("seq", None),
        P("seq"),
        P(),
        P(None, None, "head"),
        P(None, "head"),
        P("head"),
        P("head", None),
        P(),
        P(),
        P(),
        P(None, "head"),
        P("head"),
        P("head", None),
        P("head"),
        P("head", None),
        P(),
        P(None, None, "head"),
        P("head", None),
        P("seq", None),
    )
    return jax.shard_map(
        local,
        mesh=mesh,
        in_specs=placed,
        out_specs=(
            P("seq", None),
            P("seq", None),
            P("seq"),
            P("seq", None, "head"),
            P(None, "head"),
            P("head"),
            P("head", None),
            P(),
            P(),
            P(),
            P(None, "head"),
            P("head"),
            P("head", None),
            P("head"),
            P("head", "seq"),
            P("seq"),
            P("seq", None, "head"),
            P("head", "seq"),
        ),
        check_vma=False,
    )
```

```python
import functools
import math

import jax
import jax.numpy as jnp
from jax import lax
from jax.experimental import pallas as pl
from jax.experimental.pallas import tpu as pltpu
from jax.sharding import PartitionSpec as P

EPSILON = 1e-06
LANES = 128
CG = 4
WIDTH = CG * LANES
PLANE = 4
LOG2E = math.log2(math.e)
LN2 = math.log(2.0)
MESH = pl.DeviceIdType.MESH
VMEM_BYTES = 56 * 1024 * 1024


def swap_cores(value):
    return lax.ppermute(value, "head", [(0, 1), (1, 0)])


def sum_cores(value):
    return value + swap_cores(value)


def from_behind(value, axis, steps):
    count = lax.axis_size(axis)
    initial, last = (max(0, -steps), min(count, count - steps))
    return lax.ppermute(value, axis, [(source, source + steps) for source in range(initial, last)])


def rms_scale(values_in, norm_gain):
    return (
        values_in
        * lax.rsqrt(jnp.mean(values_in * values_in, axis=-1, keepdims=True) + EPSILON)
        * norm_gain
    )


def spread_rows(source, target, states, first=0):
    tokens = source.shape[0]

    def step(block, carry):
        rows = source[pl.ds(pl.multiple_of(block * 8, 8), 8), :]
        for n in range(states):
            column = jnp.broadcast_to(rows[:, first + n : first + n + 1], (8, LANES))
            for group in range(CG):
                target[pl.ds((n * CG + group) * (tokens + 1) + block * 8, 8), :] = column
        return carry

    lax.fori_loop(0, tokens // 8, step, 0)


def spread_channels(read, target, tokens):
    def step(block, carry):
        for group in range(CG):
            value = read(block, group)
            target[pl.ds(group * (tokens + 1) + block * 8, 8), :] = value
            target[pl.ds((CG + group) * (tokens + 1) + block * 8, 8), :] = value
        return carry

    lax.fori_loop(0, tokens // 8, step, 0)


def pick(ref, block, group):
    return ref[pl.ds(pl.multiple_of(block * 8, 8), 8), group * LANES : (group + 1) * LANES]


def fold_channels(source, block, group, tokens):
    return (
        source[pl.ds(group * (tokens + 1) + block * 8, 8), :]
        + source[pl.ds((CG + group) * (tokens + 1) + block * 8, 8), :]
    )


def fold_states(source, target, states):
    tokens = target.shape[0]
    lane = lax.broadcasted_iota(jnp.int32, (8, states), 1)

    def step(block, carry):
        out = jnp.zeros((8, states), jnp.float32)
        for n in range(states):
            total = None
            for group in range(CG):
                part = source[pl.ds((n * CG + group) * (tokens + 1) + block * 8, 8), :]
                total = part if total is None else total + part
            out = jnp.where(lane == n, jnp.sum(total, axis=1, keepdims=True), out)
        target[pl.ds(pl.multiple_of(block * 8, 8), 8), :] = out
        return carry

    lax.fori_loop(0, tokens // 8, step, 0)


def rows8(ref, at):
    return ref[pl.ds(pl.multiple_of(at, 8), 8), :]


def token_rows(t, tokens, p=0):
    return pl.ds(t + p * 8 * (tokens + 1), 8, stride=tokens + 1)


def state_rows(ref, p):
    per = ref.shape[2] // 8
    return ref[p // per, 0, (p % per) * 8 : (p % per) * 8 + 8, :]


def end_kernel(reverse, states, step_ref, other_ref, rows_ref, keep_ref, rate_ref, end_ref, sum_ref, steps, drive, spread):
    tokens = step_ref.shape[0]
    pairs = states // 2
    span = states * CG

    @pl.when(pl.program_id(0) == 0)
    def _():
        spread_rows(rows_ref, spread, states)

    spread_channels(functools.partial(pick, step_ref), steps, tokens)
    if reverse:
        spread_channels(functools.partial(pick, other_ref), drive, tokens)
    else:
        spread_channels(lambda b, g: pick(step_ref, b, g) * pick(other_ref, b, g), drive, tokens)
    rates = [rate_ref[0, p * 8 : p * 8 + 8, :] for p in range(pairs)]

    def body(k, carry):
        total, values = carry
        t = tokens - 1 - k if reverse else k
        size = steps[token_rows(t, tokens), :]
        push = drive[token_rows(t, tokens), :]
        keep = keep_ref[t]
        new = []
        for p in range(pairs):
            decay = jnp.exp2(size * rates[p])
            term = push * spread[token_rows(t, tokens, p), :]
            if reverse:
                new.append(decay * ((values[p] + term) * keep))
            else:
                new.append(decay * (values[p] * keep) + term)
        return total + size, tuple(new)

    zero = jnp.zeros((8, LANES), jnp.float32)
    total, values = lax.fori_loop(0, tokens, body, (zero, (zero,) * pairs), unroll=4)
    for p in range(pairs):
        end_ref[0, p * 8 : p * 8 + 8, :] = values[p]
    sum_ref[0] = total


def run_kernel(states, step_ref, mix_ref, b_ref, c_ref, keep_ref, rate_ref, start_ref, out_ref, seen_ref, last_ref, steps, drive, outs, b_spread, c_spread):
    tokens = step_ref.shape[0]
    pairs = states // 2
    span = states * CG

    @pl.when(pl.program_id(0) == 0)
    def _():
        spread_rows(b_ref, b_spread, states)
        spread_rows(c_ref, c_spread, states)

    spread_channels(functools.partial(pick, step_ref), steps, tokens)
    spread_channels(lambda b, g: pick(step_ref, b, g) * pick(mix_ref, b, g), drive, tokens)
    rates = [rate_ref[0, p * 8 : p * 8 + 8, :] for p in range(pairs)]

    def body(t, values):
        size = steps[token_rows(t, tokens), :]
        push = drive[token_rows(t, tokens), :]
        keep = keep_ref[t]
        new = []
        result = None
        for p in range(pairs):
            at = pl.multiple_of(t * span + p * 8, 8)
            seen_ref[0, pl.ds(at, 8), :] = values[p]
            decay = jnp.exp2(size * rates[p])
            value = decay * (values[p] * keep) + push * b_spread[token_rows(t, tokens, p), :]
            term = value * c_spread[token_rows(t, tokens, p), :]
            result = term if result is None else result + term
            new.append(value)
        outs[token_rows(t, tokens), :] = result
        return tuple(new)

    values = lax.fori_loop(0, tokens, body, tuple(state_rows(start_ref, p) for p in range(pairs)), unroll=4)
    for p in range(pairs):
        last_ref[0, p * 8 : p * 8 + 8, :] = values[p]

    def finish(block, carry):
        for group in range(CG):
            out_ref[pl.ds(pl.multiple_of(block * 8, 8), 8), group * LANES : (group + 1) * LANES] = fold_channels(outs, block, group, tokens)
        return carry

    lax.fori_loop(0, tokens // 8, finish, 0)


def back_kernel(states, groups, step_ref, mix_ref, grad_ref, b_ref, c_ref, keep_ref, rate_ref, after_ref, seen_ref, last_ref,
                gstep_ref, gmix_ref, gb_ref, gc_ref, grate_ref,
                steps, drive, grads, lam_b, rate_q, b_spread, c_spread, b_grad, c_grad):
    tokens = step_ref.shape[0]
    pairs = states // 2
    span = states * CG
    zero = jnp.zeros((8, LANES), jnp.float32)

    @pl.when(pl.program_id(0) == 0)
    def _():
        spread_rows(b_ref, b_spread, states)
        spread_rows(c_ref, c_spread, states)

        b_grad[...] = jnp.zeros_like(b_grad)
        c_grad[...] = jnp.zeros_like(c_grad)

    spread_channels(functools.partial(pick, step_ref), steps, tokens)
    spread_channels(functools.partial(pick, grad_ref), grads, tokens)
    spread_channels(lambda b, g: pick(step_ref, b, g) * pick(mix_ref, b, g), drive, tokens)
    rates = [rate_ref[0, p * 8 : p * 8 + 8, :] for p in range(pairs)]

    def body(k, carry):
        mus, states_now, rate_grads = carry
        t = tokens - 1 - k
        size = steps[token_rows(t, tokens), :]
        push = drive[token_rows(t, tokens), :]
        grad = grads[token_rows(t, tokens), :]
        keep = keep_ref[t]
        new_mu, new_state, new_rate = [], [], []
        lb = rq = None
        for p in range(pairs):
            at = pl.multiple_of(t * span + p * 8, 8)
            before = seen_ref[0, pl.ds(at, 8), :]
            b_value = b_spread[token_rows(t, tokens, p), :]
            lam = c_spread[token_rows(t, tokens, p), :] * grad + mus[p]
            mu = (jnp.exp2(size * rates[p]) * keep) * lam
            q = mu * before
            b_term = lam * b_value
            r_term = rates[p] * q
            lb = b_term if lb is None else lb + b_term
            rq = r_term if rq is None else rq + r_term
            b_grad[token_rows(t, tokens, p), :] += lam * push
            c_grad[token_rows(t, tokens, p), :] += states_now[p] * grad
            new_mu.append(mu)
            new_state.append(before)
            new_rate.append(rate_grads[p] + q * size)
        lam_b[token_rows(t, tokens), :] = lb
        rate_q[token_rows(t, tokens), :] = rq
        return tuple(new_mu), tuple(new_state), tuple(new_rate)

    start = (
        tuple(state_rows(after_ref, p) for p in range(pairs)),
        tuple(last_ref[0, p * 8 : p * 8 + 8, :] for p in range(pairs)),
        (zero,) * pairs,
    )
    unused_mu, unused_state, rate_grads = lax.fori_loop(0, tokens, body, start, unroll=4)
    for p in range(pairs):
        grate_ref[0, p * 8 : p * 8 + 8, :] = -rate_grads[p]

    def finish(block, carry):
        for group in range(CG):
            lb = fold_channels(lam_b, block, group, tokens)
            rq = fold_channels(rate_q, block, group, tokens)
            at = (pl.ds(pl.multiple_of(block * 8, 8), 8), slice(group * LANES, (group + 1) * LANES))
            gmix_ref[at] = pick(step_ref, block, group) * lb
            gstep_ref[at] = pick(mix_ref, block, group) * lb + LN2 * rq
        return carry

    lax.fori_loop(0, tokens // 8, finish, 0)

    @pl.when(pl.program_id(0) == groups - 1)
    def _():
        fold_states(b_grad, gb_ref, states)
        fold_states(c_grad, gc_ref, states)


def f32(*shape):
    return jax.ShapeDtypeStruct(shape, jnp.float32)


def scan_specs(tokens, states):
    span = states * CG
    return dict(
        channels=pl.BlockSpec((tokens, WIDTH), lambda g: (0, g)),
        rows=pl.BlockSpec((tokens, states), lambda g: (0, 0)),
        keep=pl.BlockSpec(memory_space=pltpu.SMEM),
        state=pl.BlockSpec((1, span, LANES), lambda g: (g, 0, 0)),
        total=pl.BlockSpec((1, 8, LANES), lambda g: (g, 0, 0)),
        parts=pl.BlockSpec((PLANE, 1, span // PLANE, LANES), lambda g: (0, g, 0, 0)),
        seen=pl.BlockSpec((1, tokens * span, LANES), lambda g: (g, 0, 0)),
    )


def params(**more):
    return pltpu.CompilerParams(vmem_limit_bytes=VMEM_BYTES, **more)


def scan_end(reverse, steps, other, rows, keep, rates):
    tokens, states = rows.shape
    groups, span, unused = rates.shape
    spec = scan_specs(tokens, states)
    return pl.pallas_call(
        functools.partial(end_kernel, reverse, states),
        grid=(groups,),
        out_shape=(f32(groups, span, LANES), f32(groups, 8, LANES)),
        in_specs=[spec["channels"], spec["channels"], spec["rows"], spec["keep"], spec["state"]],
        out_specs=(spec["state"], spec["total"]),
        scratch_shapes=[pltpu.VMEM(((tokens + 1) * 8, LANES), jnp.float32)] * 2 + [pltpu.VMEM(((tokens + 1) * span, LANES), jnp.float32)],
        compiler_params=params(),
        name="feed" if reverse else "end",
    )(steps, other, rows, keep, rates)


def scan_run(steps, mixed, b_rows, c_rows, keep, rates, start):
    tokens, states = b_rows.shape
    groups, span, unused = rates.shape
    spec = scan_specs(tokens, states)
    return pl.pallas_call(
        functools.partial(run_kernel, states),
        grid=(groups,),
        out_shape=(f32(*steps.shape), f32(groups, tokens * span, LANES), f32(groups, span, LANES)),
        in_specs=[spec["channels"], spec["channels"], spec["rows"], spec["rows"], spec["keep"], spec["state"], spec["parts"]],
        out_specs=(spec["channels"], spec["seen"], spec["state"]),
        scratch_shapes=[pltpu.VMEM(((tokens + 1) * 8, LANES), jnp.float32)] * 3 + [pltpu.VMEM(((tokens + 1) * span, LANES), jnp.float32)] * 2,
        compiler_params=params(),
        name="run",
    )(steps, mixed, b_rows, c_rows, keep, rates, start)


def scan_back(steps, mixed, grads, b_rows, c_rows, keep, rates, after, seen, last):
    tokens, states = b_rows.shape
    groups, span, unused = rates.shape
    spec = scan_specs(tokens, states)
    return pl.pallas_call(
        functools.partial(back_kernel, states, groups),
        grid=(groups,),
        out_shape=(f32(*steps.shape), f32(*steps.shape), f32(tokens, states), f32(tokens, states), f32(groups, span, LANES)),
        in_specs=[spec["channels"]] * 3 + [spec["rows"]] * 2 + [spec["keep"], spec["state"], spec["parts"], spec["seen"], spec["state"]],
        out_specs=(spec["channels"], spec["channels"], spec["rows"], spec["rows"], spec["state"]),
        scratch_shapes=[pltpu.VMEM(((tokens + 1) * 8, LANES), jnp.float32)] * 5 + [pltpu.VMEM(((tokens + 1) * span, LANES), jnp.float32)] * 4,
        compiler_params=params(),
        name="back",
    )(steps, mixed, grads, b_rows, c_rows, keep, rates, after, seen, last)


def rates_in(state_rate):
    channels, states = state_rate.shape
    groups = channels // WIDTH
    parts = state_rate.reshape(groups, CG, LANES, states)
    return jnp.transpose(parts, (0, 3, 1, 2)).reshape(groups, states * CG, LANES) * (-LOG2E)


def rates_out(grad):
    groups, span, lanes = grad.shape
    parts = grad.reshape(groups, span // CG, CG, lanes)
    return jnp.transpose(parts, (0, 2, 3, 1)).reshape(groups * WIDTH, span // CG)


def carry_kernel(planes, reverse, end_ref, sum_ref, rate_ref, out_ref, pay, got, zpay, zgot, back, final,
                 send_a, recv_a, send_b, recv_b, send_c, recv_c):
    me = lax.axis_index("seq")
    low = lax.rem(me, PLANE)
    high = lax.div(me, PLANE)
    quarter = end_ref.shape[1] // PLANE

    def in_plane(shift):
        return high * PLANE + lax.rem(low + shift, PLANE)

    def across(shift):
        return lax.rem(high + shift, planes) * PLANE + low

    barrier = pltpu.get_barrier_semaphore()
    for shift in range(1, PLANE):
        pl.semaphore_signal(barrier, inc=1, device_id={"seq": in_plane(shift)}, device_id_type=MESH)
    for shift in range(1, planes):
        pl.semaphore_signal(barrier, inc=1, device_id={"seq": across(shift)}, device_id_type=MESH)

    for k in range(PLANE):
        pay[k, :, :quarter, :] = end_ref[:, k * quarter : (k + 1) * quarter, :]
        pay[k, :, quarter:, :] = sum_ref[...]
    pl.semaphore_wait(barrier, PLANE - 1 + planes - 1)

    copies = []
    for shift in range(1, PLANE):
        copy = pltpu.make_async_remote_copy(
            src_ref=pay.at[lax.rem(low + shift, PLANE)],
            dst_ref=got.at[shift],
            send_sem=send_a.at[shift],
            recv_sem=recv_a.at[shift],
            device_id={"seq": in_plane(shift)},
            device_id_type=MESH,
        )
        copy.start()
        copies.append(copy)
    got[0] = pay[low]
    rates = rate_ref[low]
    for copy in copies:
        copy.wait()

    def decay(total):
        rows = rates.shape[1] // 8
        return jnp.exp2(rates * jnp.concatenate([total] * rows, axis=1))

    order = range(PLANE - 1, -1, -1) if reverse else range(PLANE)
    ends, decays = {}, {}
    plane_end = plane_sum = None
    for j in order:
        slot = lax.rem(low - j + PLANE, PLANE)
        part = got[slot]
        ends[j] = part[:, :quarter, :]
        size = part[:, quarter:, :]
        decays[j] = decay(size)
        plane_end = ends[j] if plane_end is None else plane_end * decays[j] + ends[j]
        plane_sum = size if plane_sum is None else plane_sum + size

    zpay[:, :quarter, :] = plane_end
    zpay[:, quarter:, :] = plane_sum
    copies = []
    for shift in range(1, planes):
        copy = pltpu.make_async_remote_copy(
            src_ref=zpay,
            dst_ref=zgot.at[shift],
            send_sem=send_b.at[shift],
            recv_sem=recv_b.at[shift],
            device_id={"seq": across(shift)},
            device_id_type=MESH,
        )
        copy.start()
        copies.append(copy)
    zgot[0] = zpay[...]
    for copy in copies:
        copy.wait()

    state = jnp.zeros_like(plane_end)
    for h in range(planes - 1, -1, -1) if reverse else range(planes):
        part = zgot[lax.rem(high - h + planes, planes)]
        after = state * decay(part[:, quarter:, :]) + part[:, :quarter, :]
        reached = h > high if reverse else h < high
        state = jnp.where(reached, after, state)

    for j in order:
        back[j] = state
        state = state * decays[j] + ends[j]
    copies = []
    for shift in range(1, PLANE):
        copy = pltpu.make_async_remote_copy(
            src_ref=back.at[lax.rem(low + shift, PLANE)],
            dst_ref=final.at[low],
            send_sem=send_c.at[shift],
            recv_sem=recv_c.at[shift],
            device_id={"seq": in_plane(shift)},
            device_id_type=MESH,
        )
        copy.start()
        copies.append(copy)
    final[low] = back[low]
    for copy in copies:
        copy.wait()
    out_ref[...] = final[...]


def carry(reverse, ends, sums, rates):
    groups, span, unused = rates.shape
    quarter = span // PLANE
    planes = lax.axis_size("seq") // PLANE
    vmem = pl.BlockSpec(memory_space=pltpu.VMEM)
    rate_parts = jnp.transpose(rates.reshape(groups, PLANE, quarter, LANES), (1, 0, 2, 3))
    dma = pltpu.SemaphoreType.DMA
    return pl.pallas_call(
        functools.partial(carry_kernel, planes, reverse),
        out_shape=f32(PLANE, groups, quarter, LANES),
        in_specs=[vmem] * 3,
        out_specs=vmem,
        scratch_shapes=[
            pltpu.VMEM((PLANE, groups, quarter + 8, LANES), jnp.float32),
            pltpu.VMEM((PLANE, groups, quarter + 8, LANES), jnp.float32),
            pltpu.VMEM((groups, quarter + 8, LANES), jnp.float32),
            pltpu.VMEM((planes, groups, quarter + 8, LANES), jnp.float32),
            pltpu.VMEM((PLANE, groups, quarter, LANES), jnp.float32),
            pltpu.VMEM((PLANE, groups, quarter, LANES), jnp.float32),
            dma((PLANE,)), dma((PLANE,)), dma((planes,)), dma((planes,)), dma((PLANE,)), dma((PLANE,)),
        ],
        compiler_params=params(collective_id=2 if reverse else 1, has_side_effects=True),
        name="carry_back" if reverse else "carry",
    )(ends, sums, rate_parts)


def after(value, *others):
    return lax.optimization_barrier((value,) + others)[0]


def swap(value, mask):
    count = lax.axis_size("seq")
    return lax.ppermute(value, "seq", [(s, s ^ mask) for s in range(count)])


def gather_plane(value):
    return [value] + [swap(value, mask) for mask in range(1, PLANE)]


def gather_rows(value):
    tokens, width = value.shape
    count = lax.axis_size("seq")
    planes = count // PLANE
    low = lax.axis_index("seq") % PLANE
    parts = jnp.transpose(value.reshape(tokens, planes, PLANE, width // count), (2, 1, 0, 3))

    def of(index):
        return lax.dynamic_index_in_dim(parts, index, 0, keepdims=False)

    return [of(low)] + [swap(of(low ^ mask), mask) for mask in range(1, PLANE)]


def grad_first(rows, columns):
    planes = rows[0].shape[0]
    high = lax.axis_index("seq") // PLANE
    left = jnp.concatenate(rows, 1)
    right = jnp.concatenate(columns, 0)
    halves = left.reshape((planes // 2, 2) + left.shape[1:])
    bit = high % 2

    def product(which):
        mine = lax.dynamic_index_in_dim(halves, which, 1, keepdims=False)
        return jnp.einsum("ptd,tc->pdc", mine, right, preferred_element_type=jnp.float32)

    got = swap(product(1 - bit).astype(jnp.bfloat16), PLANE)
    return product(bit), got


def grad_rest(pair):
    kept, got = pair
    total = kept + got.astype(jnp.float32)
    high = lax.axis_index("seq") // PLANE
    k = 1
    while total.shape[0] > 1:
        total = total.reshape((total.shape[0] // 2, 2) + total.shape[1:])
        bit = (high >> k) & 1
        send = lax.dynamic_index_in_dim(total, 1 - bit, 1, keepdims=False).astype(jnp.bfloat16)
        kept = lax.dynamic_index_in_dim(total, bit, 1, keepdims=False)
        total = kept + swap(send, PLANE << k).astype(jnp.float32)
        k += 1
    return total[0]


def small_kernel(planes, wx_ref, wdt_ref, vec_ref, rate_ref, wx_out, wdt_out, vec_out, rate_out,
                 flat, sent, got, part, zsent, zgot, full, send_a, recv_a, send_b, recv_b, send_c, recv_c, send_d, recv_d):
    me = lax.axis_index("seq")
    low = lax.rem(me, PLANE)
    high = lax.div(me, PLANE)
    rows = flat.shape[0]
    quarter = rows // PLANE
    chunk = quarter // planes

    def in_plane(shift):
        return high * PLANE + lax.rem(low + shift, PLANE)

    def across(shift):
        return lax.rem(high + shift, planes) * PLANE + low

    def quarter_at(index):
        return pl.ds(pl.multiple_of(index * quarter, 16), quarter)

    def chunk_at(index):
        return pl.ds(pl.multiple_of(index * chunk, 16), chunk)

    barrier = pltpu.get_barrier_semaphore()
    for shift in range(1, PLANE):
        pl.semaphore_signal(barrier, inc=1, device_id={"seq": in_plane(shift)}, device_id_type=MESH)
    for shift in range(1, planes):
        pl.semaphore_signal(barrier, inc=1, device_id={"seq": across(shift)}, device_id_type=MESH)

    pieces = [(wx_ref, wx_out), (wdt_ref, wdt_out), (vec_ref, vec_out), (rate_ref, rate_out)]
    at = 0
    places = []
    for ref, out in pieces:
        for j in range(ref.shape[1] // LANES):
            flat[at : at + ref.shape[0], :] = ref[:, j * LANES : (j + 1) * LANES]
            places.append((at, out, j))
            at += ref.shape[0]
    if at < rows:
        flat[at:, :] = jnp.zeros((rows - at, LANES), jnp.float32)
    sent[...] = flat[...].astype(jnp.bfloat16)
    pl.semaphore_wait(barrier, PLANE - 1 + planes - 1)

    def send(source, target, sems, slot, device):
        copy = pltpu.make_async_remote_copy(
            src_ref=source,
            dst_ref=target,
            send_sem=sems[0].at[slot],
            recv_sem=sems[1].at[slot],
            device_id={"seq": device},
            device_id_type=MESH,
        )
        copy.start()
        return copy

    copies = [
        send(sent.at[quarter_at(lax.rem(low + shift, PLANE))], got.at[shift], (send_a, recv_a), shift, in_plane(shift))
        for shift in range(1, PLANE)
    ]
    part[...] = flat[quarter_at(low), :]
    for copy in copies:
        copy.wait()
    for shift in range(1, PLANE):
        part[...] += got[shift].astype(jnp.float32)
    zsent[...] = part[...].astype(jnp.bfloat16)
    copies = [
        send(zsent.at[chunk_at(lax.rem(high + shift, planes))], zgot.at[shift], (send_b, recv_b), shift, across(shift))
        for shift in range(1, planes)
    ]
    total = part[chunk_at(high), :]
    for copy in copies:
        copy.wait()
    for shift in range(1, planes):
        total += zgot[shift].astype(jnp.float32)

    mine = pl.ds(pl.multiple_of(low * quarter + high * chunk, 16), chunk)
    full[mine, :] = total.astype(jnp.bfloat16)
    copies = [
        send(full.at[mine], full.at[mine], (send_c, recv_c), shift, across(shift)) for shift in range(1, planes)
    ]
    for copy in copies:
        copy.wait()
    copies = [
        send(full.at[quarter_at(low)], full.at[quarter_at(low)], (send_d, recv_d), shift, in_plane(shift))
        for shift in range(1, PLANE)
    ]
    for copy in copies:
        copy.wait()
    for at, out, j in places:
        out[:, j * LANES : (j + 1) * LANES] = full[at : at + out.shape[0], :].astype(jnp.float32)


def small_sum(w_x, w_dt, vectors, rates):
    count = lax.axis_size("seq")
    planes = count // PLANE
    rows = sum(a.shape[0] * (a.shape[1] // LANES) for a in (w_x, w_dt, vectors, rates))
    rows += -rows % (16 * count)
    quarter = rows // PLANE
    chunk = quarter // planes
    vmem = pl.BlockSpec(memory_space=pltpu.VMEM)
    dma = pltpu.SemaphoreType.DMA
    low = jnp.bfloat16
    return pl.pallas_call(
        functools.partial(small_kernel, planes),
        out_shape=tuple(f32(*a.shape) for a in (w_x, w_dt, vectors, rates)),
        in_specs=[vmem] * 4,
        out_specs=(vmem,) * 4,
        scratch_shapes=[
            pltpu.VMEM((rows, LANES), jnp.float32),
            pltpu.VMEM((rows, LANES), low),
            pltpu.VMEM((PLANE, quarter, LANES), low),
            pltpu.VMEM((quarter, LANES), jnp.float32),
            pltpu.VMEM((quarter, LANES), low),
            pltpu.VMEM((planes, chunk, LANES), low),
            pltpu.VMEM((rows, LANES), low),
            dma((PLANE,)), dma((PLANE,)), dma((planes,)), dma((planes,)),
            dma((planes,)), dma((planes,)), dma((PLANE,)), dma((PLANE,)),
        ],
        compiler_params=params(collective_id=3, has_side_effects=True),
        name="small_sum",
    )(w_x, w_dt, vectors, rates)


def pick_even(odd):
    row = lax.broadcasted_iota(jnp.int32, (LANES, 2 * LANES), 0)
    column = lax.broadcasted_iota(jnp.int32, (LANES, 2 * LANES), 1)
    return (column == 2 * row + odd).astype(jnp.float32).astype(jnp.bfloat16)


def widen(source, target):
    tokens, width = source.shape
    for block in range(width // LANES):
        piece = source[:, block * LANES : (block + 1) * LANES]
        for odd in range(2):
            target[odd * tokens : (odd + 1) * tokens, block * 2 * LANES : (block + 1) * 2 * LANES] = jnp.dot(
                piece, pick_even(odd), preferred_element_type=jnp.float32
            ).astype(jnp.bfloat16)


def narrow(source, target):
    tokens, width = target.shape
    row = lax.broadcasted_iota(jnp.int32, (2 * LANES, LANES), 0)
    column = lax.broadcasted_iota(jnp.int32, (2 * LANES, LANES), 1)
    pairs = (lax.div(row, 2) == column).astype(jnp.float32).astype(jnp.bfloat16)
    even = lax.rem(lax.broadcasted_iota(jnp.int32, (tokens, 2 * LANES), 1), 2) == 0
    for block in range(width // LANES):
        columns = slice(block * 2 * LANES, (block + 1) * 2 * LANES)
        value = jnp.where(even, source[:tokens, columns], source[tokens:, columns])
        total = None
        for unused in range(3):
            piece = value.astype(jnp.bfloat16)
            value = value - piece.astype(jnp.float32)
            term = jnp.dot(piece, pairs, preferred_element_type=jnp.float32)
            total = term if total is None else total + term
        target[:, block * LANES : (block + 1) * LANES] = total


def ffn_kernel(normed_ref, d_ref, gu_ref, down_ref, hidden_ref, grad_ref, out_ref, back_ref, wide, total):
    tokens, width = normed_ref.shape
    step = pl.program_id(0)

    @pl.when(step == 0)
    def _():
        widen(normed_ref, wide)
        total[...] = jnp.zeros_like(total)
        out_ref[...] = jnp.zeros_like(out_ref)

    weights = gu_ref[...].reshape(2 * width, gu_ref.shape[2])
    both = jnp.dot(wide[...], weights, preferred_element_type=jnp.float32)
    gate, up = both[:tokens], both[tokens:]
    grad_hidden = lax.dot_general(
        d_ref[...], down_ref[...], (((1,), (1,)), ((), ())), preferred_element_type=jnp.float32
    )
    sigmoid = jax.nn.sigmoid(gate)
    act = gate * sigmoid
    hidden = (act * up).astype(jnp.bfloat16)
    grad_gate = (grad_hidden * up * (sigmoid * (1.0 + gate * (1.0 - sigmoid)))).astype(jnp.bfloat16)
    grad_up = (grad_hidden * act).astype(jnp.bfloat16)
    hidden_ref[...] = hidden
    grad_ref[0] = grad_gate
    grad_ref[1] = grad_up
    out_ref[...] += jnp.dot(hidden, down_ref[...], preferred_element_type=jnp.float32)
    total[...] += lax.dot_general(
        jnp.concatenate([grad_gate, grad_up], 0),
        weights,
        (((1,), (1,)), ((), ())),
        preferred_element_type=jnp.float32,
    )

    @pl.when(step == pl.num_programs(0) - 1)
    def _():
        narrow(total, back_ref)


def ffn(normed, d_out, w_gu, w_down):
    tokens, width = normed.shape
    units = w_down.shape[0]
    tile = 512
    whole = pl.BlockSpec((tokens, width), lambda j: (0, 0))
    bf16 = jnp.bfloat16
    return pl.pallas_call(
        ffn_kernel,
        grid=(units // tile,),
        out_shape=(
            jax.ShapeDtypeStruct((tokens, units), bf16),
            jax.ShapeDtypeStruct((2, tokens, units), bf16),
            f32(tokens, width),
            f32(tokens, width),
        ),
        in_specs=[
            whole,
            whole,
            pl.BlockSpec((width, 2, tile), lambda j: (0, 0, j)),
            pl.BlockSpec((tile, width), lambda j: (j, 0)),
        ],
        out_specs=(
            pl.BlockSpec((tokens, tile), lambda j: (0, j)),
            pl.BlockSpec((2, tokens, tile), lambda j: (0, 0, j)),
            whole,
            whole,
        ),
        scratch_shapes=[pltpu.VMEM((2 * tokens, 2 * width), bf16), pltpu.VMEM((2 * tokens, 2 * width), jnp.float32)],
        compiler_params=params(),
        name="ffn",
    )(normed, d_out, w_gu, w_down)


def copy_to(source, target, send_sem, recv_sem, where):
    copy = pltpu.make_async_remote_copy(
        src_ref=source, dst_ref=target, send_sem=send_sem, recv_sem=recv_sem, device_id=where, device_id_type=MESH
    )
    copy.start()
    return copy


def wait_all(copies):
    for copy in copies:
        copy.wait()


class Places:
    def __init__(self, planes):
        self.planes = planes
        self.count = planes * PLANE
        self.me = lax.axis_index("seq")
        self.low = lax.rem(self.me, PLANE)
        self.high = lax.div(self.me, PLANE)
        self.core = lax.axis_index("head")

    def other(self):
        return {"head": 1 - self.core}

    def in_plane(self, shift):
        return {"seq": self.high * PLANE + lax.rem(self.low + shift, PLANE)}

    def across(self, shift):
        return {"seq": lax.rem(self.high + shift, self.planes) * PLANE + self.low}

    def along(self, shift):
        return {"seq": lax.rem(self.me + shift + self.count, self.count)}

    def greet(self):
        partners = [self.other(), self.along(1), self.along(-1)]
        partners += [self.in_plane(shift) for shift in range(1, PLANE)]
        partners += [self.across(shift) for shift in range(1, self.planes)]
        barrier = pltpu.get_barrier_semaphore()
        for partner in partners:
            pl.semaphore_signal(barrier, inc=1, device_id=partner, device_id_type=MESH)
        return functools.partial(pl.semaphore_wait, barrier, len(partners))


def exchange_states(places, reverse, ends, sums, rates, pay, got, zpay, zgot, back, final, sems):
    low, high, planes = places.low, places.high, places.planes
    quarter = ends.shape[1] // PLANE
    send_a, recv_a, send_b, recv_b, send_c, recv_c = sems
    for k in range(PLANE):
        pay[k, :, :quarter, :] = ends[:, k * quarter : (k + 1) * quarter, :]
        pay[k, :, quarter:, :] = sums[...]
    copies = [
        copy_to(pay.at[lax.rem(low + shift, PLANE)], got.at[shift], send_a.at[shift], recv_a.at[shift], places.in_plane(shift))
        for shift in range(1, PLANE)
    ]
    got[0] = pay[low]
    mine = rates[:, pl.ds(pl.multiple_of(low * quarter, 8), quarter), :]

    def decay(total):
        return jnp.exp2(mine * jnp.concatenate([total] * (quarter // 8), axis=1))

    wait_all(copies)
    order = range(PLANE - 1, -1, -1) if reverse else range(PLANE)
    held, decays = {}, {}
    plane_end = plane_sum = None
    for j in order:
        part = got[lax.rem(low - j + PLANE, PLANE)]
        held[j] = part[:, :quarter, :]
        size = part[:, quarter:, :]
        decays[j] = decay(size)
        plane_end = held[j] if plane_end is None else plane_end * decays[j] + held[j]
        plane_sum = size if plane_sum is None else plane_sum + size
    zpay[:, :quarter, :] = plane_end
    zpay[:, quarter:, :] = plane_sum
    copies = [
        copy_to(zpay, zgot.at[shift], send_b.at[shift], recv_b.at[shift], places.across(shift))
        for shift in range(1, planes)
    ]
    zgot[0] = zpay[...]
    wait_all(copies)
    state = jnp.zeros_like(plane_end)
    for h in range(planes - 1, -1, -1) if reverse else range(planes):
        part = zgot[lax.rem(high - h + planes, planes)]
        after_h = state * decay(part[:, quarter:, :]) + part[:, :quarter, :]
        state = jnp.where(h > high if reverse else h < high, after_h, state)
    for j in order:
        back[j] = state
        state = state * decays[j] + held[j]
    copies = [
        copy_to(back.at[lax.rem(low + shift, PLANE)], final.at[low], send_c.at[shift], recv_c.at[shift], places.in_plane(shift))
        for shift in range(1, PLANE)
    ]
    final[low] = back[low]
    wait_all(copies)


def exchange_scratch(planes, groups, span):
    quarter = span // PLANE
    size = (groups, quarter + 8, LANES)
    dma = pltpu.SemaphoreType.DMA
    return [
        pltpu.VMEM((PLANE,) + size, jnp.float32),
        pltpu.VMEM((PLANE,) + size, jnp.float32),
        pltpu.VMEM(size, jnp.float32),
        pltpu.VMEM((planes,) + size, jnp.float32),
        pltpu.VMEM((PLANE, groups, quarter, LANES), jnp.float32),
        pltpu.VMEM((PLANE, groups, quarter, LANES), jnp.float32),
        dma((PLANE,)), dma((PLANE,)), dma((planes,)), dma((planes,)), dma((PLANE,)), dma((PLANE,)),
    ]


def block16(block):
    return pl.ds(pl.multiple_of(block * 16, 16), 16)


def lanes(j, width=WIDTH):
    return slice(j * width, (j + 1) * width)


def norm_rows(read, gain, write, tokens):
    def step(block, carry):
        rows = block16(block)
        value = read(rows)
        scale = lax.rsqrt(jnp.mean(value * value, axis=-1, keepdims=True) + EPSILON)
        write(rows, value * scale * gain[...])
        return carry

    lax.fori_loop(0, tokens // 16, step, 0)


def third_masks(shape, rank, states):
    lane = lax.broadcasted_iota(jnp.int32, shape, 1)
    return lane < rank, (lane >= rank) & (lane < rank + states), lane >= rank + states


def third_means(value, rank, states):
    out = None
    for mask, count in zip(third_masks(value.shape, rank, states), (rank, states, states)):
        mean = jnp.sum(jnp.where(mask, value, 0.0), axis=-1, keepdims=True) * (1.0 / count)
        part = jnp.where(mask, mean, 0.0)
        out = part if out is None else out + part
    return out


def mixer_kernel(planes, rank, states,
                 x_ref, starts_ref, start_column, gain1_ref, win_ref, conv_w_ref, conv_b_ref, wx_ref, gains_ref, wdt_ref,
                 dt_bias_ref, rate_ref, skip_ref, wout_ref, gain2_ref,
                 normed_ref, z_ref, conv_ref, mixed_ref, proj_ref, rows_ref, step_ref, pre_ref, scanned_ref, gated_ref, resid_ref,
                 two_ref, seen_ref, last_ref, sum_ref, padded,
                 wide, win, wout, keep_pad, edge_out, edge_in, mixed_low, proj_out, proj_in, wdt, steps, drive, outs, b_spread, c_spread,
                 ends, seen, mix_out, mix_in, pay, got, zpay, zgot, back, final,
                 send_a, recv_a, send_b, recv_b, send_c, recv_c, load_sem, save_sem, edge_sem, proj_sem, mix_sem):
    tokens, width = x_ref.shape
    channels = step_ref.shape[1]
    groups = channels // WIDTH
    span = states * CG
    pairs = states // 2
    places = Places(planes)
    greeted = places.greet()
    loads = []
    for j in range(groups):
        load = pltpu.make_async_copy(win_ref.at[:, :, pl.ds(j * WIDTH, WIDTH)], win.at[j], load_sem.at[j])
        load.start()
        loads.append(load)
    load_out = pltpu.make_async_copy(wout_ref, wout, load_sem.at[groups])
    load_out.start()

    def put_normed(rows, value):
        normed_ref[rows, :] = value.astype(jnp.bfloat16)

    norm_rows(lambda rows: x_ref[rows, :].astype(jnp.float32), gain1_ref, put_normed, tokens)
    widen(normed_ref, wide)
    keep_pad[:8, :] = jnp.ones((8, 1), jnp.float32)
    keep_pad[8:, :] = (1 - start_column[...]).astype(jnp.float32)
    wdt[:rank, :] = wdt_ref[...]
    wdt[rank:, :] = jnp.zeros((LANES - rank, channels), jnp.bfloat16)
    for j in range(groups):
        loads[j].wait()
        both = jnp.dot(wide[...], win[j].reshape(2 * width, WIDTH), preferred_element_type=jnp.float32).astype(jnp.bfloat16)
        padded[8:, lanes(j)] = both[:tokens].astype(jnp.float32)
        z_ref[:, lanes(j)] = both[tokens:]

    last_keep = (1 - starts_ref[tokens - 1]).astype(jnp.float32)
    before_keep = (1 - starts_ref[tokens - 2]).astype(jnp.float32)
    row = lax.broadcasted_iota(jnp.int32, (16, 1), 0)
    tail = jnp.where(
        row == 15, 1.0, jnp.where(row == 14, last_keep, jnp.where(row == 13, last_keep * before_keep, 0.0))
    )
    edge_out[...] = (padded[tokens - 8 :, :] * tail).astype(jnp.bfloat16)
    greeted()
    edge = copy_to(edge_out, edge_in, edge_sem.at[0], edge_sem.at[1], places.along(1))
    edge.wait()
    padded[:8, :] = edge_in[8:, :].astype(jnp.float32)

    def conv(block, carry):
        start = block * 16
        rows = block16(block)
        near = pl.ds(pl.multiple_of(start, 8), 24)
        keeps = keep_pad[near, :]
        keep = keeps[8:]
        two = keep * keeps[7:23]
        three = two * keeps[6:22]
        for j in range(groups):
            values = padded[near, lanes(j)]
            total = conv_b_ref[:, lanes(j)] + conv_w_ref[3:4, lanes(j)] * values[8:]
            for offset, mask in ((1, keep), (2, two), (3, three)):
                total += conv_w_ref[3 - offset : 4 - offset, lanes(j)] * values[8 - offset : 24 - offset] * mask
            conv_ref[rows, lanes(j)] = total
            mixed = total * jax.nn.sigmoid(total)
            mixed_ref[rows, lanes(j)] = mixed
            mixed_low[rows, lanes(j)] = mixed.astype(jnp.bfloat16)
        return carry

    lax.fori_loop(0, tokens // 16, conv, 0)
    proj_out[...] = jnp.dot(mixed_low[...], wx_ref[...], preferred_element_type=jnp.float32)
    proj = copy_to(proj_out, proj_in, proj_sem.at[0], proj_sem.at[1], places.other())
    proj.wait()
    projected = proj_out[...] + proj_in[...]
    proj_ref[...] = projected
    scaled = projected * lax.rsqrt(third_means(projected * projected, rank, states) + EPSILON) * gains_ref[...]
    rows_ref[...] = scaled
    low_rows = jnp.where(third_masks(scaled.shape, rank, states)[0], scaled, 0.0).astype(jnp.bfloat16)
    for j in range(groups):
        pre = jnp.dot(low_rows, wdt[:, lanes(j)], preferred_element_type=jnp.float32) + dt_bias_ref[:, lanes(j)]
        pre_ref[:, lanes(j)] = pre
        step_ref[:, lanes(j)] = jnp.maximum(pre, 0.0) + jnp.log1p(jnp.exp(-jnp.abs(pre)))

    spread_rows(rows_ref, b_spread, states, rank)
    spread_rows(rows_ref, c_spread, states, rank + states)
    for g in range(groups):
        spread_channels(lambda b, k: pick(step_ref, b, g * CG + k), steps.at[g], tokens)
        spread_channels(lambda b, k: pick(step_ref, b, g * CG + k) * pick(mixed_ref, b, g * CG + k), drive.at[g], tokens)

    zero = jnp.zeros((8, LANES), jnp.float32)
    for g in range(groups):
        rates = [rate_ref[g, p * 8 : p * 8 + 8, :] for p in range(pairs)]

        def end_body(t, carry):
            total, values = carry
            size = steps[g, token_rows(t, tokens), :]
            push = drive[g, token_rows(t, tokens), :]
            keep = (1 - starts_ref[t]).astype(jnp.float32)
            new = []
            for p in range(pairs):
                decay = jnp.exp2(size * rates[p])
                new.append(decay * (values[p] * keep) + push * b_spread[token_rows(t, tokens, p), :])
            return total + size, tuple(new)

        total, values = lax.fori_loop(0, tokens, end_body, (zero, (zero,) * pairs), unroll=4)
        for p in range(pairs):
            ends[g, p * 8 : p * 8 + 8, :] = values[p]
        sum_ref[g] = total

    exchange_states(places, False, ends, sum_ref, rate_ref, pay, got, zpay, zgot, back, final,
                    (send_a, recv_a, send_b, recv_b, send_c, recv_c))

    saves = []
    per = pairs // PLANE
    for g in range(groups):
        rates = [rate_ref[g, p * 8 : p * 8 + 8, :] for p in range(pairs)]

        def run_body(t, values):
            size = steps[g, token_rows(t, tokens), :]
            push = drive[g, token_rows(t, tokens), :]
            keep = (1 - starts_ref[t]).astype(jnp.float32)
            new = []
            result = None
            for p in range(pairs):
                at = pl.multiple_of(t * span + p * 8, 8)
                seen[g, pl.ds(at, 8), :] = values[p]
                decay = jnp.exp2(size * rates[p])
                value = decay * (values[p] * keep) + push * b_spread[token_rows(t, tokens, p), :]
                term = value * c_spread[token_rows(t, tokens, p), :]
                result = term if result is None else result + term
                new.append(value)
            outs[g, token_rows(t, tokens), :] = result
            return tuple(new)

        first = tuple(final[p // per, g, (p % per) * 8 : (p % per) * 8 + 8, :] for p in range(pairs))
        values = lax.fori_loop(0, tokens, run_body, first, unroll=4)
        for p in range(pairs):
            last_ref[g, p * 8 : p * 8 + 8, :] = values[p]
        save = pltpu.make_async_copy(seen.at[g], seen_ref.at[g], save_sem.at[g])
        save.start()
        saves.append(save)

    def finish(block, carry):
        rows = block16(block)
        for j in range(channels // LANES):
            g, k = j // CG, j % CG
            cols = lanes(j, LANES)
            folded = [
                outs[g, pl.ds(k * (tokens + 1) + block * 16 + 8 * i, 8), :]
                + outs[g, pl.ds((CG + k) * (tokens + 1) + block * 16 + 8 * i, 8), :]
                for i in range(2)
            ]
            scanned = jnp.concatenate(folded, 0) + skip_ref[:, cols] * mixed_ref[rows, cols]
            scanned_ref[rows, cols] = scanned
            z = z_ref[rows, cols].astype(jnp.float32)
            gated_ref[rows, cols] = (scanned * (z * jax.nn.sigmoid(z))).astype(jnp.bfloat16)
        return carry

    lax.fori_loop(0, tokens // 16, finish, 0)
    load_out.wait()
    copies = []
    for j in range(width // WIDTH):
        mix_out[j] = jnp.dot(gated_ref[...], wout[:, lanes(j)], preferred_element_type=jnp.float32)
        copies.append(copy_to(mix_out.at[j], mix_in.at[j], mix_sem.at[0, j], mix_sem.at[1, j], places.other()))
    wait_all(copies)

    def put_two(rows, value):
        two_ref[rows, :] = value.astype(jnp.bfloat16)

    def read_mid(rows):
        for j in range(width // WIDTH):
            resid_ref[rows, lanes(j)] = x_ref[rows, lanes(j)].astype(jnp.float32) + (mix_out[j, rows, :] + mix_in[j, rows, :])
        return resid_ref[rows, :]

    norm_rows(read_mid, gain2_ref, put_two, tokens)
    wait_all(saves)


def mixer(x_in, doc_start, norm1_gain, input_weight, conv_w, conv_b, w_x, gains, w_dt, dt_bias, rates, skip, w_out, norm2_gain, states):
    tokens, width = x_in.shape
    channels = conv_w.shape[1]
    rank = w_dt.shape[0]
    groups, span, unused = rates.shape
    planes = lax.axis_size("seq") // PLANE
    vmem = pl.BlockSpec(memory_space=pltpu.VMEM)
    smem = pl.BlockSpec(memory_space=pltpu.SMEM)
    hbm = pl.BlockSpec(memory_space=pl.ANY)
    dma = pltpu.SemaphoreType.DMA
    bf16 = jnp.bfloat16
    wide_bf16 = jax.ShapeDtypeStruct((tokens, channels), bf16)
    chunks = width // WIDTH
    slots = (tokens + 1) * 8
    return pl.pallas_call(
        functools.partial(mixer_kernel, planes, rank, states),
        out_shape=(
            jax.ShapeDtypeStruct((tokens, width), bf16),
            wide_bf16,
            f32(tokens, channels),
            f32(tokens, channels),
            f32(tokens, LANES),
            f32(tokens, LANES),
            f32(tokens, channels),
            f32(tokens, channels),
            f32(tokens, channels),
            wide_bf16,
            f32(tokens, width),
            jax.ShapeDtypeStruct((tokens, width), bf16),
            f32(groups, tokens * span, LANES),
            f32(groups, span, LANES),
            f32(groups, 8, LANES),
            f32(tokens + 8, channels),
        ),
        in_specs=[vmem, smem, vmem, vmem, hbm, vmem, vmem, vmem, vmem, vmem, vmem, vmem, vmem, hbm, vmem],
        out_specs=(vmem,) * 12 + (hbm, vmem, vmem, vmem),
        scratch_shapes=[
            pltpu.VMEM((2 * tokens, 2 * width), bf16),
            pltpu.VMEM((groups, width, 2, WIDTH), bf16),
            pltpu.VMEM((channels, width), bf16),
            pltpu.VMEM((tokens + 8, 1), jnp.float32),
            pltpu.VMEM((16, channels), bf16),
            pltpu.VMEM((16, channels), bf16),
            pltpu.VMEM((tokens, channels), bf16),
            pltpu.VMEM((tokens, LANES), jnp.float32),
            pltpu.VMEM((tokens, LANES), jnp.float32),
            pltpu.VMEM((LANES, channels), bf16),
            pltpu.VMEM((groups, slots, LANES), jnp.float32),
            pltpu.VMEM((groups, slots, LANES), jnp.float32),
            pltpu.VMEM((groups, slots, LANES), jnp.float32),
            pltpu.VMEM(((tokens + 1) * span, LANES), jnp.float32),
            pltpu.VMEM(((tokens + 1) * span, LANES), jnp.float32),
            pltpu.VMEM((groups, span, LANES), jnp.float32),
            pltpu.VMEM((groups, tokens * span, LANES), jnp.float32),
            pltpu.VMEM((chunks, tokens, WIDTH), jnp.float32),
            pltpu.VMEM((chunks, tokens, WIDTH), jnp.float32),
        ]
        + exchange_scratch(planes, groups, span)
        + [dma((groups + 1,)), dma((groups,)), dma((2,)), dma((2,)), dma((2, chunks))],
        compiler_params=params(collective_id=1, has_side_effects=True),
        name="mixer",
    )(
        x_in, doc_start, doc_start[:, None], norm1_gain[None], input_weight, conv_w, conv_b[None], w_x, gains[None], w_dt,
        dt_bias[None], rates, skip[None], w_out, norm2_gain[None],
    )


def conv_local(padded, conv_w, conv_b, lag_masks):
    token_count = padded.shape[0] - 3
    totals = conv_b[None] + conv_w[3][None] * padded[3:]
    for offset in (1, 2, 3):
        totals = (
            totals
            + conv_w[3 - offset][None]
            * padded[3 - offset : 3 - offset + token_count]
            * lag_masks[offset - 1][:, None]
        )
    return totals


def gate_norms(projected, step_gain, b_gain_in, c_gain_in):
    rank_size = step_gain.shape[0]
    state_size = b_gain_in.shape[0]
    return (
        rms_scale(projected[:, :rank_size], step_gain),
        rms_scale(projected[:, rank_size : rank_size + state_size], b_gain_in),
        rms_scale(projected[:, rank_size + state_size :], c_gain_in),
    )


def silu_slope(values_in):
    sigmoid_val = jax.nn.sigmoid(values_in)
    return sigmoid_val * (1.0 + values_in * (1.0 - sigmoid_val))


def local(
    x_in,
    doc_start,
    norm1_gain,
    input_weight,
    conv_w,
    conv_b,
    w_x,
    dt_gain,
    b_gain,
    c_gain,
    w_dt,
    dt_bias,
    state_rate,
    skip,
    w_out,
    norm2_gain,
    w_gu,
    w_down,
    d_out,
):
    tokens_here = x_in.shape[0]
    rank_size = dt_gain.shape[0]
    state_size = b_gain.shape[0]
    resid_in = x_in.astype(jnp.float32)
    keep_flags = (1 - doc_start).astype(jnp.float32)
    rates = rates_in(state_rate)

    gains = jnp.concatenate([dt_gain, b_gain, c_gain])
    (
        normalized_reduced, z_low, conv_out, mixed_act, projected, rows, step_sizes, step_pre, scanned, gated_low, resid_mid,
        normed_two_low, seen, last, sums, padded,
    ) = mixer(
        x_in, doc_start, norm1_gain, input_weight, conv_w, conv_b, w_x, gains, w_dt, dt_bias, rates, skip, w_out, norm2_gain,
        state_size,
    )
    unused_norm, norm_pull = jax.vjp(rms_scale, resid_in, norm1_gain)
    unused_two, norm_two_pull = jax.vjp(rms_scale, resid_mid, norm2_gain)
    unused_rows, gate_pull = jax.vjp(gate_norms, projected, dt_gain, b_gain, c_gain)
    step_low = rows[:, :rank_size].astype(jnp.bfloat16)
    b_rows = rows[:, rank_size : rank_size + state_size]
    c_rows = rows[:, rank_size + state_size :]
    mixed_low = mixed_act.astype(jnp.bfloat16)
    gate_z = z_low.astype(jnp.float32)
    gate_act = jax.nn.silu(gate_z)
    tail_keep = jnp.stack(
        [keep_flags[-2] * keep_flags[-1], keep_flags[-1], jnp.ones((), jnp.float32)]
    )
    padded_keep = jnp.concatenate([jnp.ones((3,), jnp.float32), keep_flags])
    lag_one = padded_keep[3:]
    lag_two = lag_one * padded_keep[2:-1]
    lag_three = lag_two * padded_keep[1:-2]
    lag_masks = (lag_one, lag_two, lag_three)
    padded = padded[5:]

    def conv_part(padded_in, weight_in, bias_in):
        return conv_local(padded_in, weight_in, bias_in, lag_masks)

    unused_conv, conv_pull = jax.vjp(conv_part, padded, conv_w, conv_b)
    grad_out = d_out.astype(jnp.float32)
    hidden_low, grad_gu_low, ffn_part, grad_two_part = ffn(normed_two_low, d_out, w_gu, w_down)
    gated_columns = gather_plane(gated_low)
    out_rows = gather_rows(d_out)
    two_rows = gather_rows(normed_two_low)
    hidden_columns = gather_plane(hidden_low)
    gate_columns = gather_plane(grad_gu_low[0])
    up_columns = gather_plane(grad_gu_low[1])
    output = (resid_mid + sum_cores(ffn_part)).astype(jnp.bfloat16)
    grad_normed_two = sum_cores(grad_two_part)
    grad_mid_norm, grad_norm_two = norm_two_pull(grad_normed_two)
    grad_mid = grad_out + grad_mid_norm
    grad_mix_low = grad_mid.astype(jnp.bfloat16)
    mix_rows = gather_rows(grad_mix_low)
    grad_gated = jnp.einsum("td,cd->tc", grad_mix_low, w_out, preferred_element_type=jnp.float32)
    grad_scanned = grad_gated * gate_act
    grad_z = grad_gated * scanned * silu_slope(gate_z)
    grad_skip = jnp.sum(grad_scanned * mixed_act, 0)
    one_rows = gather_rows(normalized_reduced)
    grad_z_low = grad_z.astype(jnp.bfloat16)
    z_columns = gather_plane(grad_z_low)
    feeds, unused_sums = scan_end(True, step_sizes, grad_scanned, c_rows, keep_flags, rates)
    gated_columns = [after(c, feeds) for c in gated_columns]
    hidden_columns = [after(c, feeds) for c in hidden_columns]
    out_pair = grad_first(mix_rows, gated_columns)
    down_pair = grad_first(out_rows, hidden_columns)
    feeds, out_pair, down_pair = lax.optimization_barrier((feeds, out_pair, down_pair))
    grad_after = carry(True, feeds, sums, rates)
    grad_steps, grad_mix_scan, grad_b_all, grad_c_all, grad_rates = scan_back(
        step_sizes, mixed_act, grad_scanned, b_rows, c_rows, keep_flags, rates, grad_after, seen, last
    )
    gate_columns = [after(c, grad_steps) for c in gate_columns]
    up_columns = [after(c, grad_steps) for c in up_columns]
    gate_pair = grad_first(two_rows, gate_columns)
    up_pair = grad_first(two_rows, up_columns)
    grad_mixed = grad_scanned * skip + grad_mix_scan
    grad_pre = grad_steps * jax.nn.sigmoid(step_pre)
    grad_dt_bias = jnp.sum(grad_pre, 0)
    grad_pre_low = grad_pre.astype(jnp.bfloat16)
    grad_w_dt = jnp.einsum("tr,tc->rc", step_low, grad_pre_low, preferred_element_type=jnp.float32)
    grad_step_part = jnp.einsum("tc,rc->tr", grad_pre_low, w_dt, preferred_element_type=jnp.float32)
    summed = sum_cores(jnp.concatenate([grad_step_part, grad_b_all, grad_c_all], 1))
    grad_proj, grad_dt_gain, grad_b_gain, grad_c_gain = gate_pull(
        (
            summed[:, :rank_size],
            summed[:, rank_size : rank_size + state_size],
            summed[:, rank_size + state_size :],
        )
    )
    grad_proj_low = grad_proj.astype(jnp.bfloat16)
    grad_w_x = jnp.einsum("tc,tk->ck", mixed_low, grad_proj_low, preferred_element_type=jnp.float32)
    grad_mixed = grad_mixed + jnp.einsum(
        "tk,ck->tc", grad_proj_low, w_x, preferred_element_type=jnp.float32
    )
    grad_conv_out = grad_mixed * silu_slope(conv_out)
    grad_padded, grad_conv_w, grad_conv_b = conv_pull(grad_conv_out)
    edge_grad = from_behind(grad_padded[:3], "seq", -1)
    grad_inner = jnp.concatenate(
        [grad_padded[3:-3], grad_padded[-3:] + edge_grad * tail_keep[:, None]], 0
    )
    grad_inner_low = grad_inner.astype(jnp.bfloat16)
    inner_columns = gather_plane(grad_inner_low)
    z_pair = grad_first(one_rows, z_columns)
    grad_normed = sum_cores(
        jnp.einsum(
            "ary,jry->aj",
            jnp.stack([grad_inner_low, grad_z_low], 1),
            input_weight,
            preferred_element_type=jnp.float32,
        )
    )
    grad_in_norm, grad_norm_one = norm_pull(grad_normed)
    grad_input = grad_mid + grad_in_norm
    inner_pair = grad_first(one_rows, inner_columns)
    red_down = grad_rest(down_pair).T
    red_out = grad_rest(out_pair).T
    red_gu = jnp.stack([grad_rest(gate_pair), grad_rest(up_pair)], 1)
    red_in = jnp.stack([grad_rest(inner_pair), grad_rest(z_pair)], 1)
    gains = jnp.concatenate([grad_dt_gain, grad_b_gain, grad_c_gain])
    vectors = jnp.concatenate(
        [
            grad_conv_w,
            grad_conv_b[None],
            grad_dt_bias[None],
            grad_skip[None],
            grad_norm_one.reshape(-1, grad_skip.shape[0]),
            grad_norm_two.reshape(-1, grad_skip.shape[0]),
            jnp.pad(gains, (0, grad_skip.shape[0] - gains.shape[0]))[None],
        ],
        0,
    )
    count_vectors = vectors.shape[0]
    vectors = jnp.pad(vectors, ((0, -count_vectors % 16), (0, 0)))
    groups, span, lanes = grad_rates.shape
    wx_sum, wdt_sum, vector_sum, rate_sum = small_sum(
        grad_w_x, grad_w_dt, vectors, grad_rates.reshape(groups * span, lanes)
    )
    grad_rate = rates_out(rate_sum.reshape(groups, span, lanes))
    taps = grad_conv_w.shape[0]
    norm_rows = norm1_gain.shape[0] // grad_skip.shape[0]
    norm_at = taps + 3
    gain_row = vector_sum[norm_at + 2 * norm_rows]
    share = norm1_gain.shape[0] // lax.axis_size("seq")

    def own(row):
        whole = vector_sum[row : row + norm_rows].reshape(-1)
        return lax.dynamic_slice(whole, (lax.axis_index("seq") * share,), (share,))

    return (
        output,
        grad_input,
        own(norm_at),
        red_in,
        vector_sum[:taps],
        vector_sum[taps],
        wx_sum,
        gain_row[:rank_size],
        gain_row[rank_size : rank_size + state_size],
        gain_row[rank_size + state_size : rank_size + 2 * state_size],
        wdt_sum,
        vector_sum[taps + 1],
        grad_rate,
        vector_sum[taps + 2],
        red_out,
        own(norm_at + norm_rows),
        red_gu,
        red_down,
    )


def solution(mesh):
    placed = (
        P("seq", None),
        P("seq"),
        P(),
        P(None, None, "head"),
        P(None, "head"),
        P("head"),
        P("head", None),
        P(),
        P(),
        P(),
        P(None, "head"),
        P("head"),
        P("head", None),
        P("head"),
        P("head", None),
        P(),
        P(None, None, "head"),
        P("head", None),
        P("seq", None),
    )
    return jax.shard_map(
        local,
        mesh=mesh,
        in_specs=placed,
        out_specs=(
            P("seq", None),
            P("seq", None),
            P("seq"),
            P("seq", None, "head"),
            P(None, "head"),
            P("head"),
            P("head", None),
            P(),
            P(),
            P(),
            P(None, "head"),
            P("head"),
            P("head", None),
            P("head"),
            P("head", "seq"),
            P("seq"),
            P("seq", None, "head"),
            P("head", "seq"),
        ),
        check_vma=False,
    )
```

```python
import functools
import math

import jax
import jax.numpy as jnp
from jax import lax
from jax.experimental import pallas as pl
from jax.experimental.pallas import tpu as pltpu
from jax.sharding import PartitionSpec as P

EPSILON = 1e-06
LANES = 128
CG = 4
WIDTH = CG * LANES
PLANE = 4
LOG2E = math.log2(math.e)
LN2 = math.log(2.0)
MESH = pl.DeviceIdType.MESH
VMEM_BYTES = 60 * 1024 * 1024


def swap_cores(value):
    return lax.ppermute(value, "head", [(0, 1), (1, 0)])


def spread_rows(source, target, states, first=0):
    tokens = source.shape[0]

    def step(block, carry):
        rows = source[pl.ds(pl.multiple_of(block * 8, 8), 8), :]
        for n in range(states):
            column = jnp.broadcast_to(rows[:, first + n : first + n + 1], (8, LANES))
            for group in range(CG):
                target[pl.ds((n * CG + group) * (tokens + 1) + block * 8, 8), :] = column
        return carry

    lax.fori_loop(0, tokens // 8, step, 0)


def spread_channels(read, target, tokens):
    def step(block, carry):
        for group in range(CG):
            value = read(block, group)
            target[pl.ds(group * (tokens + 1) + block * 8, 8), :] = value
            target[pl.ds((CG + group) * (tokens + 1) + block * 8, 8), :] = value
        return carry

    lax.fori_loop(0, tokens // 8, step, 0)


def pick(ref, block, group):
    return ref[pl.ds(pl.multiple_of(block * 8, 8), 8), group * LANES : (group + 1) * LANES]


def token_rows(t, tokens, p=0):
    return pl.ds(t + p * 8 * (tokens + 1), 8, stride=tokens + 1)


def f32(*shape):
    return jax.ShapeDtypeStruct(shape, jnp.float32)


def params(**more):
    return pltpu.CompilerParams(vmem_limit_bytes=VMEM_BYTES, **more)


def rates_in(state_rate):
    channels, states = state_rate.shape
    groups = channels // WIDTH
    parts = state_rate.reshape(groups, CG, LANES, states)
    return jnp.transpose(parts, (0, 3, 1, 2)).reshape(groups, states * CG, LANES) * (-LOG2E)


def rates_out(grad):
    groups, span, lanes = grad.shape
    parts = grad.reshape(groups, span // CG, CG, lanes)
    return jnp.transpose(parts, (0, 2, 3, 1)).reshape(groups * WIDTH, span // CG)


def pick_even(odd):
    row = lax.broadcasted_iota(jnp.int32, (LANES, 2 * LANES), 0)
    column = lax.broadcasted_iota(jnp.int32, (LANES, 2 * LANES), 1)
    return (column == 2 * row + odd).astype(jnp.float32).astype(jnp.bfloat16)


def widen(source, target):
    tokens, width = source.shape
    for block in range(width // LANES):
        piece = source[:, block * LANES : (block + 1) * LANES]
        for odd in range(2):
            target[odd * tokens : (odd + 1) * tokens, block * 2 * LANES : (block + 1) * 2 * LANES] = jnp.dot(
                piece, pick_even(odd), preferred_element_type=jnp.float32
            ).astype(jnp.bfloat16)


def narrow(source, target):
    tokens, width = target.shape
    row = lax.broadcasted_iota(jnp.int32, (2 * LANES, LANES), 0)
    column = lax.broadcasted_iota(jnp.int32, (2 * LANES, LANES), 1)
    pairs = (lax.div(row, 2) == column).astype(jnp.float32).astype(jnp.bfloat16)
    even = lax.rem(lax.broadcasted_iota(jnp.int32, (tokens, 2 * LANES), 1), 2) == 0
    for block in range(width // LANES):
        columns = slice(block * 2 * LANES, (block + 1) * 2 * LANES)
        value = jnp.where(even, source[:tokens, columns], source[tokens:, columns])
        total = None
        for unused in range(3):
            piece = value.astype(jnp.bfloat16)
            value = value - piece.astype(jnp.float32)
            term = jnp.dot(piece, pairs, preferred_element_type=jnp.float32)
            total = term if total is None else total + term
        target[:, block * LANES : (block + 1) * LANES] = total


def ffn_kernel(normed_ref, d_ref, gu_ref, down_ref, hidden_ref, grad_ref, out_ref, back_ref, wide, total):
    tokens, width = normed_ref.shape
    step = pl.program_id(0)

    @pl.when(step == 0)
    def _():
        widen(normed_ref, wide)
        total[...] = jnp.zeros_like(total)
        out_ref[...] = jnp.zeros_like(out_ref)

    weights = gu_ref[...].reshape(2 * width, gu_ref.shape[2])
    both = jnp.dot(wide[...], weights, preferred_element_type=jnp.float32)
    gate, up = both[:tokens], both[tokens:]
    grad_hidden = lax.dot_general(
        d_ref[...], down_ref[...], (((1,), (1,)), ((), ())), preferred_element_type=jnp.float32
    )
    sigmoid = jax.nn.sigmoid(gate)
    act = gate * sigmoid
    hidden = (act * up).astype(jnp.bfloat16)
    grad_gate = (grad_hidden * up * (sigmoid * (1.0 + gate * (1.0 - sigmoid)))).astype(jnp.bfloat16)
    grad_up = (grad_hidden * act).astype(jnp.bfloat16)
    hidden_ref[...] = hidden
    grad_ref[0] = grad_gate
    grad_ref[1] = grad_up
    out_ref[...] += jnp.dot(hidden, down_ref[...], preferred_element_type=jnp.float32)
    total[...] += lax.dot_general(
        jnp.concatenate([grad_gate, grad_up], 0),
        weights,
        (((1,), (1,)), ((), ())),
        preferred_element_type=jnp.float32,
    )

    @pl.when(step == pl.num_programs(0) - 1)
    def _():
        narrow(total, back_ref)


def ffn(normed, d_out, w_gu, w_down):
    tokens, width = normed.shape
    units = w_down.shape[0]
    tile = 512
    whole = pl.BlockSpec((tokens, width), lambda j: (0, 0))
    bf16 = jnp.bfloat16
    return pl.pallas_call(
        ffn_kernel,
        grid=(units // tile,),
        out_shape=(
            jax.ShapeDtypeStruct((tokens, units), bf16),
            jax.ShapeDtypeStruct((2, tokens, units), bf16),
            f32(tokens, width),
            f32(tokens, width),
        ),
        in_specs=[
            whole,
            whole,
            pl.BlockSpec((width, 2, tile), lambda j: (0, 0, j)),
            pl.BlockSpec((tile, width), lambda j: (j, 0)),
        ],
        out_specs=(
            pl.BlockSpec((tokens, tile), lambda j: (0, j)),
            pl.BlockSpec((2, tokens, tile), lambda j: (0, 0, j)),
            whole,
            whole,
        ),
        scratch_shapes=[pltpu.VMEM((2 * tokens, 2 * width), bf16), pltpu.VMEM((2 * tokens, 2 * width), jnp.float32)],
        compiler_params=params(),
        name="ffn",
    )(normed, d_out, w_gu, w_down)


def copy_to(source, target, send_sem, recv_sem, where):
    copy = pltpu.make_async_remote_copy(
        src_ref=source, dst_ref=target, send_sem=send_sem, recv_sem=recv_sem, device_id=where, device_id_type=MESH
    )
    copy.start()
    return copy


def wait_all(copies):
    for copy in copies:
        copy.wait()


class Places:
    def __init__(self, planes):
        self.planes = planes
        self.count = planes * PLANE
        self.me = lax.axis_index("seq")
        self.low = lax.rem(self.me, PLANE)
        self.high = lax.div(self.me, PLANE)
        self.core = lax.axis_index("head")

    def other(self):
        return {"head": 1 - self.core}

    def in_plane(self, shift):
        return {"seq": self.high * PLANE + lax.rem(self.low + shift, PLANE)}

    def across(self, shift):
        return {"seq": lax.rem(self.high + shift, self.planes) * PLANE + self.low}

    def along(self, shift):
        return {"seq": lax.rem(self.me + shift + self.count, self.count)}

    def greet(self):
        partners = [self.other(), self.along(1), self.along(-1)]
        partners += [self.in_plane(shift) for shift in range(1, PLANE)]
        partners += [self.across(shift) for shift in range(1, self.planes)]
        barrier = pltpu.get_barrier_semaphore()
        for partner in partners:
            pl.semaphore_signal(barrier, inc=1, device_id=partner, device_id_type=MESH)
        return functools.partial(pl.semaphore_wait, barrier, len(partners))


def exchange_states(places, reverse, ends, sums, rates, pay, got, zpay, zgot, back, final, sems):
    low, high, planes = places.low, places.high, places.planes
    quarter = ends.shape[1] // PLANE
    send_a, recv_a, send_b, recv_b, send_c, recv_c = sems
    for k in range(PLANE):
        pay[k, :, :quarter, :] = ends[:, k * quarter : (k + 1) * quarter, :]
        pay[k, :, quarter:, :] = sums[...]
    copies = [
        copy_to(pay.at[lax.rem(low + shift, PLANE)], got.at[shift], send_a.at[shift], recv_a.at[shift], places.in_plane(shift))
        for shift in range(1, PLANE)
    ]
    got[0] = pay[low]
    mine = rates[:, pl.ds(pl.multiple_of(low * quarter, 8), quarter), :]

    def decay(total):
        return jnp.exp2(mine * jnp.concatenate([total] * (quarter // 8), axis=1))

    wait_all(copies)
    order = range(PLANE - 1, -1, -1) if reverse else range(PLANE)
    held, decays = {}, {}
    plane_end = plane_sum = None
    for j in order:
        part = got[lax.rem(low - j + PLANE, PLANE)]
        held[j] = part[:, :quarter, :]
        size = part[:, quarter:, :]
        decays[j] = decay(size)
        plane_end = held[j] if plane_end is None else plane_end * decays[j] + held[j]
        plane_sum = size if plane_sum is None else plane_sum + size
    zpay[:, :quarter, :] = plane_end
    zpay[:, quarter:, :] = plane_sum
    copies = [
        copy_to(zpay, zgot.at[shift], send_b.at[shift], recv_b.at[shift], places.across(shift))
        for shift in range(1, planes)
    ]
    zgot[0] = zpay[...]
    wait_all(copies)
    state = jnp.zeros_like(plane_end)
    for h in range(planes - 1, -1, -1) if reverse else range(planes):
        part = zgot[lax.rem(high - h + planes, planes)]
        after_h = state * decay(part[:, quarter:, :]) + part[:, :quarter, :]
        state = jnp.where(h > high if reverse else h < high, after_h, state)
    for j in order:
        back[j] = state
        state = state * decays[j] + held[j]
    copies = [
        copy_to(back.at[lax.rem(low + shift, PLANE)], final.at[low], send_c.at[shift], recv_c.at[shift], places.in_plane(shift))
        for shift in range(1, PLANE)
    ]
    final[low] = back[low]
    wait_all(copies)


def exchange_scratch(planes, groups, span):
    quarter = span // PLANE
    size = (groups, quarter + 8, LANES)
    dma = pltpu.SemaphoreType.DMA
    return [
        pltpu.VMEM((PLANE,) + size, jnp.float32),
        pltpu.VMEM((PLANE,) + size, jnp.float32),
        pltpu.VMEM(size, jnp.float32),
        pltpu.VMEM((planes,) + size, jnp.float32),
        pltpu.VMEM((PLANE, groups, quarter, LANES), jnp.float32),
        pltpu.VMEM((PLANE, groups, quarter, LANES), jnp.float32),
        dma((PLANE,)), dma((PLANE,)), dma((planes,)), dma((planes,)), dma((PLANE,)), dma((PLANE,)),
    ]


def block16(block):
    return pl.ds(pl.multiple_of(block * 16, 16), 16)


def lanes(j, width=WIDTH):
    return slice(j * width, (j + 1) * width)


def norm_rows(read, gain, write, tokens):
    def step(block, carry):
        rows = block16(block)
        value = read(rows)
        scale = lax.rsqrt(jnp.mean(value * value, axis=-1, keepdims=True) + EPSILON)
        write(rows, value * scale * gain[...])
        return carry

    lax.fori_loop(0, tokens // 16, step, 0)


def third_masks(shape, rank, states):
    lane = lax.broadcasted_iota(jnp.int32, shape, 1)
    return lane < rank, (lane >= rank) & (lane < rank + states), lane >= rank + states


def third_means(value, rank, states):
    out = None
    for mask, count in zip(third_masks(value.shape, rank, states), (rank, states, states)):
        mean = jnp.sum(jnp.where(mask, value, 0.0), axis=-1, keepdims=True) * (1.0 / count)
        part = jnp.where(mask, mean, 0.0)
        out = part if out is None else out + part
    return out


def mixer_kernel(planes, rank, states,
                 x_ref, starts_ref, start_column, gain1_ref, win_ref, conv_w_ref, conv_b_ref, wx_ref, gains_ref, wdt_ref,
                 dt_bias_ref, rate_ref, skip_ref, wout_ref, gain2_ref,
                 normed_ref, z_ref, conv_ref, mixed_ref, proj_ref, rows_ref, step_ref, pre_ref, scanned_ref, gated_ref, resid_ref,
                 two_ref, seen_ref, sum_ref, padded,
                 wide, win, wout, keep_pad, edge_out, edge_in, mixed_low, proj_out, proj_in, wdt, steps, drive, outs, b_spread, c_spread,
                 ends, seen, mix_out, mix_in, pay, got, zpay, zgot, back, final,
                 send_a, recv_a, send_b, recv_b, send_c, recv_c, load_sem, save_sem, edge_sem, proj_sem, mix_sem):
    tokens, width = x_ref.shape
    channels = step_ref.shape[1]
    groups = channels // WIDTH
    span = states * CG
    pairs = states // 2
    places = Places(planes)
    greeted = places.greet()
    loads = []
    for j in range(groups):
        load = pltpu.make_async_copy(win_ref.at[:, :, pl.ds(j * WIDTH, WIDTH)], win.at[j], load_sem.at[j])
        load.start()
        loads.append(load)
    load_out = pltpu.make_async_copy(wout_ref, wout, load_sem.at[groups])
    load_out.start()

    def put_normed(rows, value):
        normed_ref[rows, :] = value.astype(jnp.bfloat16)

    norm_rows(lambda rows: x_ref[rows, :].astype(jnp.float32), gain1_ref, put_normed, tokens)
    widen(normed_ref, wide)
    keep_pad[:8, :] = jnp.ones((8, 1), jnp.float32)
    keep_pad[8:, :] = (1 - start_column[...]).astype(jnp.float32)
    wdt[:rank, :] = wdt_ref[...]
    wdt[rank:, :] = jnp.zeros((LANES - rank, channels), jnp.bfloat16)
    for j in range(groups):
        loads[j].wait()
        both = jnp.dot(wide[...], win[j].reshape(2 * width, WIDTH), preferred_element_type=jnp.float32).astype(jnp.bfloat16)
        padded[8:, lanes(j)] = both[:tokens].astype(jnp.float32)
        z_ref[:, lanes(j)] = both[tokens:]

    last_keep = (1 - starts_ref[tokens - 1]).astype(jnp.float32)
    before_keep = (1 - starts_ref[tokens - 2]).astype(jnp.float32)
    row = lax.broadcasted_iota(jnp.int32, (16, 1), 0)
    tail = jnp.where(
        row == 15, 1.0, jnp.where(row == 14, last_keep, jnp.where(row == 13, last_keep * before_keep, 0.0))
    )
    edge_out[...] = (padded[tokens - 8 :, :] * tail).astype(jnp.bfloat16)
    greeted()
    edge = copy_to(edge_out, edge_in, edge_sem.at[0], edge_sem.at[1], places.along(1))
    edge.wait()
    padded[:8, :] = edge_in[8:, :].astype(jnp.float32)

    def conv(block, carry):
        start = block * 16
        rows = block16(block)
        near = pl.ds(pl.multiple_of(start, 8), 24)
        keeps = keep_pad[near, :]
        keep = keeps[8:]
        two = keep * keeps[7:23]
        three = two * keeps[6:22]
        for j in range(groups):
            values = padded[near, lanes(j)]
            total = conv_b_ref[:, lanes(j)] + conv_w_ref[3:4, lanes(j)] * values[8:]
            for offset, mask in ((1, keep), (2, two), (3, three)):
                total += conv_w_ref[3 - offset : 4 - offset, lanes(j)] * values[8 - offset : 24 - offset] * mask
            conv_ref[rows, lanes(j)] = total
            mixed = total * jax.nn.sigmoid(total)
            mixed_ref[rows, lanes(j)] = mixed
            mixed_low[rows, lanes(j)] = mixed.astype(jnp.bfloat16)
        return carry

    lax.fori_loop(0, tokens // 16, conv, 0)
    proj_out[...] = jnp.dot(mixed_low[...], wx_ref[...], preferred_element_type=jnp.float32)
    proj = copy_to(proj_out, proj_in, proj_sem.at[0], proj_sem.at[1], places.other())
    proj.wait()
    projected = proj_out[...] + proj_in[...]
    proj_ref[...] = projected
    scaled = projected * lax.rsqrt(third_means(projected * projected, rank, states) + EPSILON) * gains_ref[...]
    rows_ref[...] = scaled
    low_rows = jnp.where(third_masks(scaled.shape, rank, states)[0], scaled, 0.0).astype(jnp.bfloat16)
    for j in range(groups):
        pre = jnp.dot(low_rows, wdt[:, lanes(j)], preferred_element_type=jnp.float32) + dt_bias_ref[:, lanes(j)]
        pre_ref[:, lanes(j)] = pre
        step_ref[:, lanes(j)] = jnp.maximum(pre, 0.0) + jnp.log1p(jnp.exp(-jnp.abs(pre)))

    spread_rows(rows_ref, b_spread, states, rank)
    spread_rows(rows_ref, c_spread, states, rank + states)
    for g in range(groups):
        spread_channels(lambda b, k: pick(step_ref, b, g * CG + k), steps.at[g], tokens)
        spread_channels(lambda b, k: pick(step_ref, b, g * CG + k) * pick(mixed_ref, b, g * CG + k), drive.at[g], tokens)

    zero = jnp.zeros((8, LANES), jnp.float32)
    for g in range(groups):
        rates = [rate_ref[g, p * 8 : p * 8 + 8, :] for p in range(pairs)]

        def end_body(t, carry):
            total, values = carry
            size = steps[g, token_rows(t, tokens), :]
            push = drive[g, token_rows(t, tokens), :]
            keep = (1 - starts_ref[t]).astype(jnp.float32)
            new = []
            for p in range(pairs):
                decay = jnp.exp2(size * rates[p])
                new.append(decay * (values[p] * keep) + push * b_spread[token_rows(t, tokens, p), :])
            return total + size, tuple(new)

        total, values = lax.fori_loop(0, tokens, end_body, (zero, (zero,) * pairs), unroll=4)
        for p in range(pairs):
            ends[g, p * 8 : p * 8 + 8, :] = values[p]
        sum_ref[g] = total

    exchange_states(places, False, ends, sum_ref, rate_ref, pay, got, zpay, zgot, back, final,
                    (send_a, recv_a, send_b, recv_b, send_c, recv_c))

    saves = []
    per = pairs // PLANE
    for g in range(groups):
        rates = [rate_ref[g, p * 8 : p * 8 + 8, :] for p in range(pairs)]

        def run_body(t, values):
            size = steps[g, token_rows(t, tokens), :]
            push = drive[g, token_rows(t, tokens), :]
            keep = (1 - starts_ref[t]).astype(jnp.float32)
            new = []
            result = None
            for p in range(pairs):
                at = pl.multiple_of(t * span + p * 8, 8)
                seen[g, pl.ds(at, 8), :] = values[p]
                decay = jnp.exp2(size * rates[p])
                value = decay * (values[p] * keep) + push * b_spread[token_rows(t, tokens, p), :]
                term = value * c_spread[token_rows(t, tokens, p), :]
                result = term if result is None else result + term
                new.append(value)
            outs[g, token_rows(t, tokens), :] = result
            return tuple(new)

        first = tuple(final[p // per, g, (p % per) * 8 : (p % per) * 8 + 8, :] for p in range(pairs))
        values = lax.fori_loop(0, tokens, run_body, first, unroll=4)
        for p in range(pairs):
            seen[g, tokens * span + p * 8 : tokens * span + p * 8 + 8, :] = values[p]
        save = pltpu.make_async_copy(seen.at[g], seen_ref.at[g], save_sem.at[g])
        save.start()
        saves.append(save)

    def finish(block, carry):
        rows = block16(block)
        for j in range(channels // LANES):
            g, k = j // CG, j % CG
            cols = lanes(j, LANES)
            folded = [
                outs[g, pl.ds(k * (tokens + 1) + block * 16 + 8 * i, 8), :]
                + outs[g, pl.ds((CG + k) * (tokens + 1) + block * 16 + 8 * i, 8), :]
                for i in range(2)
            ]
            scanned = jnp.concatenate(folded, 0) + skip_ref[:, cols] * mixed_ref[rows, cols]
            scanned_ref[rows, cols] = scanned
            z = z_ref[rows, cols].astype(jnp.float32)
            gated_ref[rows, cols] = (scanned * (z * jax.nn.sigmoid(z))).astype(jnp.bfloat16)
        return carry

    lax.fori_loop(0, tokens // 16, finish, 0)
    load_out.wait()
    copies = []
    for j in range(width // WIDTH):
        mix_out[j] = jnp.dot(gated_ref[...], wout[:, lanes(j)], preferred_element_type=jnp.float32)
        copies.append(copy_to(mix_out.at[j], mix_in.at[j], mix_sem.at[0, j], mix_sem.at[1, j], places.other()))
    wait_all(copies)

    def put_two(rows, value):
        two_ref[rows, :] = value.astype(jnp.bfloat16)

    def read_mid(rows):
        for j in range(width // WIDTH):
            resid_ref[rows, lanes(j)] = x_ref[rows, lanes(j)].astype(jnp.float32) + (mix_out[j, rows, :] + mix_in[j, rows, :])
        return resid_ref[rows, :]

    norm_rows(read_mid, gain2_ref, put_two, tokens)
    wait_all(saves)


def mixer(x_in, doc_start, norm1_gain, input_weight, conv_w, conv_b, w_x, gains, w_dt, dt_bias, rates, skip, w_out, norm2_gain, states):
    tokens, width = x_in.shape
    channels = conv_w.shape[1]
    rank = w_dt.shape[0]
    groups, span, unused = rates.shape
    planes = lax.axis_size("seq") // PLANE
    vmem = pl.BlockSpec(memory_space=pltpu.VMEM)
    smem = pl.BlockSpec(memory_space=pltpu.SMEM)
    hbm = pl.BlockSpec(memory_space=pl.ANY)
    dma = pltpu.SemaphoreType.DMA
    bf16 = jnp.bfloat16
    wide_bf16 = jax.ShapeDtypeStruct((tokens, channels), bf16)
    chunks = width // WIDTH
    slots = (tokens + 1) * 8
    return pl.pallas_call(
        functools.partial(mixer_kernel, planes, rank, states),
        out_shape=(
            jax.ShapeDtypeStruct((tokens, width), bf16),
            wide_bf16,
            f32(tokens, channels),
            f32(tokens, channels),
            f32(tokens, LANES),
            f32(tokens, LANES),
            f32(tokens, channels),
            f32(tokens, channels),
            f32(tokens, channels),
            wide_bf16,
            f32(tokens, width),
            jax.ShapeDtypeStruct((tokens, width), bf16),
            f32(groups, (tokens + 1) * span, LANES),
            f32(groups, 8, LANES),
            f32(tokens + 8, channels),
        ),
        in_specs=[vmem, smem, vmem, vmem, hbm, vmem, vmem, vmem, vmem, vmem, vmem, vmem, vmem, hbm, vmem],
        out_specs=(vmem,) * 12 + (hbm, vmem, vmem),
        scratch_shapes=[
            pltpu.VMEM((2 * tokens, 2 * width), bf16),
            pltpu.VMEM((groups, width, 2, WIDTH), bf16),
            pltpu.VMEM((channels, width), bf16),
            pltpu.VMEM((tokens + 8, 1), jnp.float32),
            pltpu.VMEM((16, channels), bf16),
            pltpu.VMEM((16, channels), bf16),
            pltpu.VMEM((tokens, channels), bf16),
            pltpu.VMEM((tokens, LANES), jnp.float32),
            pltpu.VMEM((tokens, LANES), jnp.float32),
            pltpu.VMEM((LANES, channels), bf16),
            pltpu.VMEM((groups, slots, LANES), jnp.float32),
            pltpu.VMEM((groups, slots, LANES), jnp.float32),
            pltpu.VMEM((groups, slots, LANES), jnp.float32),
            pltpu.VMEM(((tokens + 1) * span, LANES), jnp.float32),
            pltpu.VMEM(((tokens + 1) * span, LANES), jnp.float32),
            pltpu.VMEM((groups, span, LANES), jnp.float32),
            pltpu.VMEM((groups, (tokens + 1) * span, LANES), jnp.float32),
            pltpu.VMEM((chunks, tokens, WIDTH), jnp.float32),
            pltpu.VMEM((chunks, tokens, WIDTH), jnp.float32),
        ]
        + exchange_scratch(planes, groups, span)
        + [dma((groups + 1,)), dma((groups,)), dma((2,)), dma((2,)), dma((2, chunks))],
        compiler_params=params(collective_id=1, has_side_effects=True),
        name="mixer",
    )(
        x_in, doc_start, doc_start[:, None], norm1_gain[None], input_weight, conv_w, conv_b[None], w_x, gains[None], w_dt,
        dt_bias[None], rates, skip[None], w_out, norm2_gain[None],
    )


RING = 3
NEAR = 8


def near_rows(i, p=0):
    return pl.ds(i + p * 8 * (NEAR + 1), 8, stride=NEAR + 1)


def near_slot(slot):
    return pl.ds(slot * (NEAR + 1), NEAR)


def near_spread_rows(rows, first, states, target):
    for n in range(states):
        column = jnp.broadcast_to(rows[:, first + n : first + n + 1], (NEAR, LANES))
        for group in range(CG):
            target[near_slot(n * CG + group), :] = column


def near_spread_channels(value, target):
    for j in range(value.shape[1] // LANES):
        g, k = j // CG, j % CG
        piece = value[:, lanes(j, LANES)]
        target[g, near_slot(k), :] = piece
        target[g, near_slot(CG + k), :] = piece


def near_fold_channels(source, g, k):
    return source[g, near_slot(k), :] + source[g, near_slot(CG + k), :]


def near_fold_rows(source, states, first, out):
    lane = lax.broadcasted_iota(jnp.int32, out.shape, 1)
    for n in range(states):
        total = None
        for group in range(CG):
            part = source[near_slot(n * CG + group), :]
            total = part if total is None else total + part
        out = jnp.where(lane == first + n, jnp.sum(total, axis=1, keepdims=True), out)
    return out


def flip_bits(k, high, planes):
    out = 0
    step = 1
    while step < planes:
        out = out + lax.rem(lax.div(k, step) + lax.div(high, step), 2) * step
        step *= 2
    return out


def slot_place(k, planes):
    return k // 2 + (k % 2) * (planes // 2)


def rms_back(grad, value, gain):
    scale = lax.rsqrt(jnp.mean(value * value, axis=-1, keepdims=True) + EPSILON)
    scaled = value * scale
    pull = grad * gain
    inner = jnp.mean(pull * scaled, axis=-1, keepdims=True)
    return scale * (pull - scaled * inner), grad * scaled


def silu_and_slope(value):
    sigmoid = jax.nn.sigmoid(value)
    return value * sigmoid, sigmoid * (1.0 + value * (1.0 - sigmoid))


def sum8(value):
    total = value[:8]
    for i in range(1, value.shape[0] // 8):
        total = total + value[i * 8 : (i + 1) * 8]
    return total


def back_kernel(planes, rank, states, share, units,
                d_ref, x_ref, z_ref, normed_ref, two_ref, resid_ref, conv_ref, mixed_ref, proj_ref, rows_ref, step_ref, pre_ref,
                scanned_ref, inner_ref, gtwo_ref, sum_ref, starts_ref, start_column, gain1_ref, gain2_ref, gains_ref, conv_w_ref,
                skip_ref, wx_ref, wdt_ref, rate_ref,
                hidden_ref, ggu_ref, gated_ref, seen_ref, wout_ref, win_ref,
                dx_ref, grads_ref, wx_out, wdt_out, vec_out, rate_out, xin, zr0,
                wout, win, wide, seen, rows_out, rows_all, xbuf, zbuf, zs0, zs_more, zr_more, acc,
                gtwo_in, gmix_low, gscan, z_low, gstep, gmix, gpad, keep_pad, inner_low, mixed_low, gpre_low, wdt, dyp, dyp_in,
                edge_out, edge_in, norm_in, spread_b, spread_c, near_step, near_push, near_grad, near_lb, near_rq,
                near_gb, near_gc, mus, ends, rate_grad, vec, flat, sent, got, part, zsent, zgot, full,
                pay, egot, zpay, ezgot, back, final,
                send_a, recv_a, send_b, recv_b, send_c, recv_c,
                load_sem, seen_sem, x_send, x_recv, r_send, r_recv, z_send, z_recv, xbuf_sem, pair_sem, small_sem, save_sem):
    tokens, width = x_ref.shape
    channels = step_ref.shape[1]
    groups = channels // WIDTH
    chunks = width // WIDTH
    span = states * CG
    pairs = states // 2
    steps_z = planes.bit_length() - 1
    half = planes // 2
    places = Places(planes)
    low, high = places.low, places.high
    greeted = places.greet()
    blocks = tokens // NEAR

    def wout_copy(j):
        rows = pl.ds(j * WIDTH, WIDTH)
        return pltpu.make_async_copy(wout_ref.at[rows, :], wout.at[j % 2], load_sem.at[2 + j % 2])

    wout_copy(0).start()
    wout_copy(1).start()

    def seen_copy(block, slot):
        at = pl.ds(pl.multiple_of(block * (NEAR * span), 8), (NEAR + 1) * span)
        return pltpu.make_async_copy(seen_ref.at[:, at, :], seen.at[slot], seen_sem.at[slot])

    for k in range(RING - 1):
        seen_copy(blocks - 1 - k, k).start()

    def win_copy(j):
        return pltpu.make_async_copy(win_ref.at[:, :, pl.ds(j * WIDTH, WIDTH)], win.at[j % 2], load_sem.at[j % 2])

    win_copy(0).start()
    win_copy(1).start()

    greeted()
    two_copy = copy_to(gtwo_ref, gtwo_in, pair_sem.at[0], pair_sem.at[1], places.other())

    piece = math.gcd(share, LANES)

    def put_rows(read, which):
        for block in range(width // LANES):
            turned = jnp.transpose(read(lanes(block, LANES)).astype(jnp.float32)).astype(jnp.bfloat16)
            for at in range(0, LANES, piece):
                index = block * LANES + at
                owner, offset = index // share, index % share
                slot = flip_bits(owner // PLANE, high, planes)
                place = lax.div(slot, 2) + lax.rem(slot, 2) * half
                rows_out[which, owner % PLANE, place, offset : offset + piece, :] = turned[at : at + piece]

    row_copies = {}

    def send_rows(which):
        row_copies[which] = [
            copy_to(
                rows_out.at[which, lax.rem(low + shift, PLANE)],
                rows_all.at[which, :, :, pl.ds(shift * tokens, tokens)],
                r_send.at[which, shift],
                r_recv.at[which, shift],
                places.in_plane(shift),
            )
            for shift in range(1, PLANE)
        ]
        rows_all[which, :, :, :tokens] = rows_out[which, low]

    unit_copies = {}
    offsets, at = [], 0
    for unit_width, unused in units:
        offsets.append(at)
        at += unit_width

    def unit_source(u):
        return (hidden_ref, ggu_ref.at[0], ggu_ref.at[1], gated_ref, z_low, inner_low)[u]

    ring_width = max(unit_width for unit_width, unused in units)
    turn = (0, 2, 3, 1, 4, 5)

    def unit_columns(u):
        return pl.ds(offsets[u], units[u][0])

    def ring_columns(u):
        return pl.ds(turn[u] % 2 * ring_width, units[u][0])

    def columns_of(u, j):
        return pl.ds(pl.multiple_of(offsets[u] + j * WIDTH, WIDTH), WIDTH)

    def ring_of(u, j):
        return pl.ds(pl.multiple_of(turn[u] % 2 * ring_width + j * WIDTH, WIDTH), WIDTH)

    def first_slot(step):
        return sum(planes // 2 ** (k + 1) for k in range(1, step))

    def send_unit(u):
        unit_copies[u] = [
            copy_to(
                unit_source(u), xin.at[shift - 1, :, unit_columns(u)], x_send.at[u, shift], x_recv.at[u, shift], places.in_plane(shift)
            )
            for shift in range(1, PLANE)
        ]

    def partner(step):
        size = 2**step
        bit = lax.rem(lax.div(high, size), 2)
        return {"seq": (high + (1 - 2 * bit) * size) * PLANE + low}

    z_copies = {}

    def load_chunk(u, j, slot, with_z):
        local = pl.ds(pl.multiple_of(j * WIDTH, WIDTH), WIDTH)
        whole = columns_of(u, j)
        copies = [
            pltpu.make_async_copy(unit_source(u).at[:, local], xbuf.at[slot, pl.ds(0, tokens), :], xbuf_sem.at[slot, 0])
        ]
        for shift in range(1, PLANE):
            copies.append(
                pltpu.make_async_copy(
                    xin.at[shift - 1, :, whole], xbuf.at[slot, pl.ds(shift * tokens, tokens), :], xbuf_sem.at[slot, shift]
                )
            )
        if with_z:
            copies.append(pltpu.make_async_copy(zr0.at[:, :, whole], zbuf.at[slot], xbuf_sem.at[slot, PLANE]))
        return copies

    def over_chunks(u, with_z, use):
        count = units[u][0] // WIDTH
        for copy in load_chunk(u, 0, 0, with_z):
            copy.start()

        def body(j, carry):
            slot = lax.rem(j, 2)

            @pl.when(j + 1 < count)
            def _():
                for copy in load_chunk(u, j + 1, 1 - slot, with_z):
                    copy.start()

            for copy in load_chunk(u, j, slot, with_z):
                copy.wait()
            use(slot, j)
            return carry

        lax.fori_loop(0, count, body, 0)

    def product(u, slot, first):
        left = rows_all[units[u][1], first : first + half, :, :].reshape(half * rows_all.shape[3 - 1], PLANE * tokens)
        return jnp.dot(left, xbuf[slot], preferred_element_type=jnp.float32).reshape(half, rows_all.shape[2], WIDTH)

    def stage_one(u):
        wait_all(unit_copies[u])
        which = units[u][1]
        if which in row_copies:
            wait_all(row_copies.pop(which))

        def use(slot, j):
            zs0[:, :, ring_of(u, j)] = product(u, slot, half).astype(jnp.bfloat16)

        over_chunks(u, False, use)
        z_copies[u] = copy_to(zs0.at[:, :, ring_columns(u)], zr0.at[:, :, unit_columns(u)], z_send.at[u, 0], z_recv.at[u, 0], partner(0))

    def split(u, step, value, j):
        count = value.shape[0]
        columns = ring_of(u, j)
        if count == 1:
            acc[0, :, columns] = value[0]
            return
        for i in range(count // 2):
            acc[i, :, columns] = value[2 * i]
            zs_more[first_slot(step) + i, :, columns] = value[2 * i + 1].astype(jnp.bfloat16)

    def send_more(u, step):
        slots = pl.ds(first_slot(step), planes // 2 ** (step + 1))
        z_copies[u] = copy_to(
            zs_more.at[slots, :, ring_columns(u)],
            zr_more.at[slots, :, unit_columns(u)],
            z_send.at[u, step],
            z_recv.at[u, step],
            partner(step),
        )

    def stage_two(u):
        z_copies.pop(u).wait()
        for other in list(saves):
            if turn[other] % 2 == turn[u] % 2:
                saves.pop(other).wait()

        def use(slot, j):
            split(u, 1, product(u, slot, 0) + zbuf[slot].astype(jnp.float32), j)

        over_chunks(u, True, use)
        if steps_z > 1:
            send_more(u, 1)

    saves = {}

    def stage_three(u):
        count_chunks = units[u][0] // WIDTH
        for step in range(2, steps_z + 1):
            z_copies.pop(u).wait()
            count = planes // 2**step

            def body(j, carry):
                first = first_slot(step - 1)
                value = acc[:count, :, ring_of(u, j)] + zr_more[first : first + count, :, columns_of(u, j)].astype(jnp.float32)
                split(u, step, value, j)
                return carry

            lax.fori_loop(0, count_chunks, body, 0)
            if count > 1:
                send_more(u, step)
        save = pltpu.make_async_copy(acc.at[0, :, ring_columns(u)], grads_ref.at[:, unit_columns(u)], save_sem.at[u])
        save.start()
        saves[u] = save

    HIDDEN, GATE, UP, GATED, Z, INNER = range(6)
    send_unit(HIDDEN)
    put_rows(lambda cols: d_ref[:, cols], 0)
    send_rows(0)
    put_rows(lambda cols: two_ref[:, cols], 2)
    send_rows(2)

    keep_pad[:8, :] = jnp.ones((8, 1), jnp.float32)
    keep_pad[8 : 8 + tokens, :] = (1 - start_column[...]).astype(jnp.float32)
    keep_pad[8 + tokens :, :] = jnp.ones((8, 1), jnp.float32)
    wdt[:rank, :] = wdt_ref[...]
    wdt[rank:, :] = jnp.zeros((LANES - rank, channels), jnp.bfloat16)
    vec[...] = jnp.zeros_like(vec)
    rate_grad[...] = jnp.zeros_like(rate_grad)

    two_copy.wait()

    def mid(block, carry):
        rows = block16(block)
        grad = gtwo_ref[rows, :] + gtwo_in[rows, :]
        back_to, gain_part = rms_back(grad, resid_ref[rows, :], gain2_ref[...])
        value = d_ref[rows, :].astype(jnp.float32) + back_to
        dx_ref[rows, :] = value
        gmix_low[rows, :] = value.astype(jnp.bfloat16)
        return carry + sum8(gain_part)

    norm2 = lax.fori_loop(0, tokens // 16, mid, jnp.zeros((8, width), jnp.float32))
    vec[8:9, :] = jnp.sum(norm2, axis=0, keepdims=True)
    send_unit(GATED)

    for j in range(groups):
        wout_copy(j).wait()
        gscan[:, lanes(j)] = lax.dot_general(
            gmix_low[...], wout[j % 2], (((1,), (1,)), ((), ())), preferred_element_type=jnp.float32
        )
        if j + 2 < groups:
            wout_copy(j + 2).start()

    def gate(block, carry):
        rows = block16(block)
        out = []
        for j in range(groups):
            cols = lanes(j)
            act, slope = silu_and_slope(z_ref[rows, cols].astype(jnp.float32))
            grad = gscan[rows, cols]
            grad_scanned = grad * act
            gscan[rows, cols] = grad_scanned
            z_low[rows, cols] = (grad * scanned_ref[rows, cols] * slope).astype(jnp.bfloat16)
            mixed = mixed_ref[rows, cols]
            mixed_low[rows, cols] = mixed.astype(jnp.bfloat16)
            out.append(carry[j] + sum8(grad_scanned * mixed))
        return tuple(out)

    skips = lax.fori_loop(0, tokens // 16, gate, (jnp.zeros((8, WIDTH), jnp.float32),) * groups)
    for j in range(groups):
        vec[6:7, lanes(j)] = jnp.sum(skips[j], axis=0, keepdims=True)

    def keep_of(t):
        return (1 - starts_ref[t]).astype(jnp.float32)

    def near_block(block):
        return pl.ds(pl.multiple_of(block * NEAR, NEAR), NEAR)

    def rate_of(g, p):
        return rate_ref[g, p * 8 : p * 8 + 8, :]

    mus[...] = jnp.zeros_like(mus)

    def feed(k, carry):
        block = blocks - 1 - k
        at = near_block(block)
        near_spread_rows(rows_ref[at, :], rank + states, states, spread_c)
        near_spread_channels(step_ref[at, :], near_step)
        near_spread_channels(gscan[at, :], near_grad)
        for g in range(groups):
            held = [mus[g, p * 8 : p * 8 + 8, :] for p in range(pairs)]
            for i in range(NEAR - 1, -1, -1):
                size = near_step[g, near_rows(i), :]
                grad = near_grad[g, near_rows(i), :]
                keep = keep_of(block * NEAR + i)
                for p in range(pairs):
                    lam = held[p] + spread_c[near_rows(i, p), :] * grad
                    held[p] = jnp.exp2(size * rate_of(g, p)) * (lam * keep)
            for p in range(pairs):
                mus[g, p * 8 : p * 8 + 8, :] = held[p]
        return carry

    lax.fori_loop(0, blocks, feed, 0)
    ends[...] = mus[...]
    put_rows(lambda cols: dx_ref[:, cols], 3)
    send_rows(3)
    exchange_states(places, True, ends, sum_ref, rate_ref, pay, egot, zpay, ezgot, back, final,
                    (send_a, recv_a, send_b, recv_b, send_c, recv_c))
    per = pairs // PLANE
    for g in range(groups):
        for p in range(pairs):
            mus[g, p * 8 : p * 8 + 8, :] = final[p // per, g, (p % per) * 8 : (p % per) * 8 + 8, :]
    send_unit(GATE)
    stage_one(HIDDEN)

    def scan(k, carry):
        block = blocks - 1 - k
        at = near_block(block)
        slot = lax.rem(k, RING)

        @pl.when(k + RING - 1 < blocks)
        def _():
            seen_copy(block - (RING - 1), lax.rem(k + RING - 1, RING)).start()

        near_spread_rows(rows_ref[at, :], rank, states, spread_b)
        near_spread_rows(rows_ref[at, :], rank + states, states, spread_c)
        near_spread_channels(step_ref[at, :], near_step)
        near_spread_channels(step_ref[at, :] * mixed_ref[at, :], near_push)
        near_spread_channels(gscan[at, :], near_grad)
        seen_copy(block, slot).wait()
        held = [[mus[g, p * 8 : p * 8 + 8, :] for p in range(pairs)] for g in range(groups)]
        for i in range(NEAR - 1, -1, -1):
            keep = keep_of(block * NEAR + i)
            sizes = [near_step[g, near_rows(i), :] for g in range(groups)]
            pushes = [near_push[g, near_rows(i), :] for g in range(groups)]
            grads = [near_grad[g, near_rows(i), :] for g in range(groups)]
            lbs, rqs = [None] * groups, [None] * groups
            for p in range(pairs):
                b_value = spread_b[near_rows(i, p), :]
                c_value = spread_c[near_rows(i, p), :]
                gb = gc = None
                for g in range(groups):
                    rate = rate_of(g, p)
                    before = seen[slot, g, i * span + p * 8 : i * span + p * 8 + 8, :]
                    now = seen[slot, g, (i + 1) * span + p * 8 : (i + 1) * span + p * 8 + 8, :]
                    lam = held[g][p] + c_value * grads[g]
                    mu = jnp.exp2(sizes[g] * rate) * (lam * keep)
                    held[g][p] = mu
                    q = mu * before
                    rate_grad[g, p * 8 : p * 8 + 8, :] += q * sizes[g]
                    lb, rq = lam * b_value, q * rate
                    lbs[g] = lb if lbs[g] is None else lbs[g] + lb
                    rqs[g] = rq if rqs[g] is None else rqs[g] + rq
                    gb_term, gc_term = lam * pushes[g], now * grads[g]
                    gb = gb_term if gb is None else gb + gb_term
                    gc = gc_term if gc is None else gc + gc_term
                near_gb[near_rows(i, p), :] = gb
                near_gc[near_rows(i, p), :] = gc
            for g in range(groups):
                near_lb[g, near_rows(i), :] = lbs[g]
                near_rq[g, near_rows(i), :] = rqs[g]
        for g in range(groups):
            for p in range(pairs):
                mus[g, p * 8 : p * 8 + 8, :] = held[g][p]
        for j in range(channels // LANES):
            g, k_group = j // CG, j % CG
            cols = lanes(j, LANES)
            lb = near_fold_channels(near_lb, g, k_group)
            rq = near_fold_channels(near_rq, g, k_group)
            gmix[at, cols] = step_ref[at, cols] * lb
            gstep[at, cols] = mixed_ref[at, cols] * lb + LN2 * rq
        row = jnp.zeros((NEAR, LANES), jnp.float32)
        row = near_fold_rows(near_gb, states, rank, row)
        dyp[at, :] = near_fold_rows(near_gc, states, rank + states, row)
        return carry

    lax.fori_loop(0, blocks, scan, 0)
    send_unit(UP)
    stage_one(GATED)
    stage_two(HIDDEN)

    def pre_grad(block, carry):
        rows = block16(block)
        out = []
        for j in range(groups):
            grad = gstep[rows, lanes(j)] * jax.nn.sigmoid(pre_ref[rows, lanes(j)])
            gpre_low[rows, lanes(j)] = grad.astype(jnp.bfloat16)
            out.append(carry[j] + sum8(grad))
        return tuple(out)

    biases = lax.fori_loop(0, tokens // 16, pre_grad, (jnp.zeros((8, WIDTH), jnp.float32),) * groups)
    for j in range(groups):
        vec[5:6, lanes(j)] = jnp.sum(biases[j], axis=0, keepdims=True)
    dyp[...] += lax.dot_general(gpre_low[...], wdt[...], (((1,), (1,)), ((), ())), preferred_element_type=jnp.float32)
    dyp_copy = copy_to(dyp, dyp_in, pair_sem.at[2], pair_sem.at[3], places.other())
    turned = jnp.transpose(rows_ref[...]).astype(jnp.bfloat16)
    at_flat = channels // LANES * LANES
    for j in range(channels // LANES):
        value = jnp.dot(turned[:rank], gpre_low[:, lanes(j, LANES)], preferred_element_type=jnp.float32)
        flat[at_flat + j * rank : at_flat + (j + 1) * rank, :] = value
    dyp_copy.wait()
    projected = proj_ref[...]
    scale = lax.rsqrt(third_means(projected * projected, rank, states) + EPSILON)
    scaled = projected * scale
    grad = dyp[...] + dyp_in[...]
    pull = grad * gains_ref[...]
    proj_grad = scale * (pull - scaled * third_means(pull * scaled, rank, states))
    vec[9:10, :LANES] = jnp.sum(sum8(grad * scaled), axis=0, keepdims=True)
    proj_low = proj_grad.astype(jnp.bfloat16)
    turned_proj = jnp.transpose(proj_grad).astype(jnp.bfloat16)

    for j in range(groups):
        gmix[:, lanes(j)] += lax.dot_general(
            proj_low, wx_ref[lanes(j), :], (((1,), (1,)), ((), ())), preferred_element_type=jnp.float32
        )
    gpad[:8, :] = jnp.zeros((8, channels), jnp.float32)
    gpad[8 + tokens :, :] = jnp.zeros((8, channels), jnp.float32)

    def conv_grad(block, carry):
        rows = block16(block)
        to = pl.ds(pl.multiple_of(block * 16 + 8, 8), 16)
        near = pl.ds(pl.multiple_of(block * 16, 8), 24)
        keeps = keep_pad[near, :]
        keep = keeps[8:]
        two = keep * keeps[7:23]
        three = two * keeps[6:22]
        out = []
        for j in range(groups):
            cols = lanes(j)
            unused, slope = silu_and_slope(conv_ref[rows, cols])
            grad = (gmix[rows, cols] + skip_ref[:, cols] * gscan[rows, cols]) * slope
            gpad[to, cols] = grad
            values = inner_ref[near, cols]
            sums = [carry[j][4] + sum8(grad), carry[j][3] + sum8(grad * values[8:])]
            for offset, mask in ((1, keep), (2, two), (3, three)):
                sums.append(carry[j][3 - offset] + sum8(grad * values[8 - offset : 24 - offset] * mask))
            out.append((sums[4], sums[3], sums[2], sums[1], sums[0]))
        return tuple(out)

    empty = jnp.zeros((8, WIDTH), jnp.float32)
    taps = lax.fori_loop(0, tokens // 16, conv_grad, ((empty,) * 5,) * groups)
    for j in range(groups):
        for i in range(5):
            vec[i : i + 1, lanes(j)] = jnp.sum(taps[j][i], axis=0, keepdims=True)

    def taps_back(start, count, columns):
        near = pl.ds(pl.multiple_of(start, 8), count + 8)
        keeps = keep_pad[near, :]
        grads = gpad[near, columns]
        total = conv_w_ref[3:4, columns] * grads[:count]
        mask = None
        for offset in (1, 2, 3):
            mask = keeps[1 : count + 1] if mask is None else mask * keeps[offset : count + offset]
            total += conv_w_ref[3 - offset : 4 - offset, columns] * grads[offset : count + offset] * mask
        return total

    for j in range(groups):
        edge_out[:, lanes(j)] = taps_back(0, 8, lanes(j))
    edge_copy = copy_to(edge_out, edge_in, pair_sem.at[4], pair_sem.at[5], places.along(-1))

    def inner_grad(block, carry):
        rows = block16(block)
        for j in range(groups):
            inner_low[rows, lanes(j)] = taps_back(block * 16 + 8, 16, lanes(j)).astype(jnp.bfloat16)
        return carry

    lax.fori_loop(0, tokens // 16 - 1, inner_grad, 0)
    last_keep, before_keep = keep_of(tokens - 1), keep_of(tokens - 2)
    row = lax.broadcasted_iota(jnp.int32, (16, 1), 0)
    tail = jnp.where(
        row == 15, 1.0, jnp.where(row == 14, last_keep, jnp.where(row == 13, last_keep * before_keep, 0.0))
    )
    tail = jnp.where(places.me == places.count - 1, 0.0, tail)
    edge_copy.wait()
    for j in range(groups):
        here = taps_back(tokens - 8, 16, lanes(j))
        edge = jnp.concatenate([jnp.zeros((8, WIDTH), jnp.float32), edge_in[:, lanes(j)]], 0) * tail
        inner_low[tokens - 16 :, lanes(j)] = (here + edge).astype(jnp.bfloat16)
    send_unit(Z)
    put_rows(lambda cols: normed_ref[:, cols], 1)
    send_rows(1)
    send_unit(INNER)
    for j in range(channels // LANES):
        flat[j * LANES : (j + 1) * LANES, :] = jnp.dot(
            turned_proj, mixed_low[:, lanes(j, LANES)], preferred_element_type=jnp.float32
        )

    for j in range(groups):
        win_copy(j).wait()
        both = lax.dot_general(
            jnp.concatenate([inner_low[:, lanes(j)], z_low[:, lanes(j)]], 0),
            win[j % 2].reshape(2 * width, WIDTH),
            (((1,), (1,)), ((), ())),
            preferred_element_type=jnp.float32,
        )
        if j == 0:
            wide[...] = both
        else:
            wide[...] += both
        if j + 2 < groups:
            win_copy(j + 2).start()
    narrow(wide, gtwo_in)
    norm_copy = copy_to(gtwo_in, norm_in, pair_sem.at[6], pair_sem.at[7], places.other())
    stage_one(GATE)
    stage_two(GATED)
    stage_three(HIDDEN)
    norm_copy.wait()

    def first_norm(block, carry):
        rows = block16(block)
        grad = gtwo_in[rows, :] + norm_in[rows, :]
        back_to, gain_part = rms_back(grad, x_ref[rows, :].astype(jnp.float32), gain1_ref[...])
        dx_ref[rows, :] += back_to
        return carry + sum8(gain_part)

    norm1 = lax.fori_loop(0, tokens // 16, first_norm, jnp.zeros((8, width), jnp.float32))
    vec[7:8, :] = jnp.sum(norm1, axis=0, keepdims=True)

    rows_flat = flat.shape[0]
    quarter = rows_flat // PLANE
    chunk = quarter // planes
    at_vec = at_flat + channels // LANES * rank
    for j in range(channels // LANES):
        flat[at_vec + j * 16 : at_vec + (j + 1) * 16, :] = vec[:, lanes(j, LANES)]
    at_rate = at_vec + channels // LANES * 16
    for g in range(groups):
        flat[at_rate + g * span : at_rate + (g + 1) * span, :] = -rate_grad[g]
    at_end = at_rate + groups * span
    if at_end < rows_flat:
        flat[at_end:, :] = jnp.zeros((rows_flat - at_end, LANES), jnp.float32)
    sent[...] = flat[...].astype(jnp.bfloat16)

    def quarter_at(index):
        return pl.ds(pl.multiple_of(index * quarter, 16), quarter)

    def chunk_at(index):
        return pl.ds(pl.multiple_of(index * chunk, 16), chunk)

    small_copies = [
        copy_to(sent.at[quarter_at(lax.rem(low + shift, PLANE))], got.at[shift], small_sem.at[0, shift], small_sem.at[1, shift],
                places.in_plane(shift))
        for shift in range(1, PLANE)
    ]
    part[...] = flat[quarter_at(low), :]
    stage_one(UP)
    stage_two(GATE)
    stage_three(GATED)
    wait_all(small_copies)
    for shift in range(1, PLANE):
        part[...] += got[shift].astype(jnp.float32)
    zsent[...] = part[...].astype(jnp.bfloat16)
    small_copies = [
        copy_to(zsent.at[chunk_at(lax.rem(high + shift, planes))], zgot.at[shift], small_sem.at[2, shift], small_sem.at[3, shift],
                places.across(shift))
        for shift in range(1, planes)
    ]
    stage_one(Z)
    stage_two(UP)
    wait_all(small_copies)
    total = part[chunk_at(high), :]
    for shift in range(1, planes):
        total += zgot[shift].astype(jnp.float32)
    mine = pl.ds(pl.multiple_of(low * quarter + high * chunk, 16), chunk)
    full[mine, :] = total.astype(jnp.bfloat16)
    small_copies = [
        copy_to(full.at[mine], full.at[mine], small_sem.at[4, shift], small_sem.at[5, shift], places.across(shift))
        for shift in range(1, planes)
    ]
    stage_three(GATE)
    stage_one(INNER)
    wait_all(small_copies)
    small_copies = [
        copy_to(full.at[quarter_at(low)], full.at[quarter_at(low)], small_sem.at[6, shift], small_sem.at[7, shift],
                places.in_plane(shift))
        for shift in range(1, PLANE)
    ]
    stage_two(Z)
    stage_three(UP)
    stage_two(INNER)
    wait_all(small_copies)
    for j in range(channels // LANES):
        wx_out[:, lanes(j, LANES)] = full[j * LANES : (j + 1) * LANES, :].astype(jnp.float32)
        wdt_out[:, lanes(j, LANES)] = full[at_flat + j * rank : at_flat + (j + 1) * rank, :].astype(jnp.float32)
        vec_out[:, lanes(j, LANES)] = full[at_vec + j * 16 : at_vec + (j + 1) * 16, :].astype(jnp.float32)
    for g in range(groups):
        rate_out[g] = full[at_rate + g * span : at_rate + (g + 1) * span, :].astype(jnp.float32)
    stage_three(Z)
    stage_three(INNER)
    wait_all(saves.values())


def mixer_back(d_out, x_in, kept, gtwo, hidden, ggu, doc_start, norm1_gain, norm2_gain, gains, conv_w, skip, w_x, w_dt, rates,
               w_out, input_weight, states, gated, seen, sums):
    tokens, width = x_in.shape
    channels = conv_w.shape[1]
    unit_ff = hidden.shape[1]
    rank = w_dt.shape[0]
    groups, span, unused = rates.shape
    count = lax.axis_size("seq")
    planes = count // PLANE
    share = width // count
    held = share + -share % 32
    units = ((unit_ff, 0), (unit_ff, 2), (unit_ff, 2), (channels, 3), (channels, 1), (channels, 1))
    columns = sum(u for u, unused in units)
    vmem = pl.BlockSpec(memory_space=pltpu.VMEM)
    smem = pl.BlockSpec(memory_space=pltpu.SMEM)
    hbm = pl.BlockSpec(memory_space=pl.ANY)
    dma = pltpu.SemaphoreType.DMA
    bf16 = jnp.bfloat16
    half = planes // 2
    ring = 2 * max(u for u, unused in units)
    more = max(planes // 4, 1)
    steps_z = planes.bit_length() - 1
    rows = channels + channels // LANES * (rank + 16) + groups * span
    rows += -rows % (16 * count)
    near = 8 * (NEAR + 1)

    def fast(shape, kind=jnp.float32):
        return pltpu.VMEM(shape, kind)

    return pl.pallas_call(
        functools.partial(back_kernel, planes, rank, states, share, units),
        out_shape=(
            f32(tokens, width),
            f32(held, columns),
            f32(LANES, channels),
            f32(rank, channels),
            f32(16, channels),
            f32(groups, span, LANES),
            jax.ShapeDtypeStruct((PLANE - 1, tokens, columns), bf16),
            jax.ShapeDtypeStruct((half, held, columns), bf16),
        ),
        in_specs=[vmem] * 16 + [smem] + [vmem] * 9 + [hbm] * 6,
        out_specs=(vmem, hbm, vmem, vmem, vmem, vmem, hbm, hbm),
        scratch_shapes=[
            fast((2, WIDTH, width), bf16),
            fast((2, width, 2, WIDTH), bf16),
            fast((2 * tokens, 2 * width)),
            fast((RING, groups, (NEAR + 1) * span, LANES)),
            fast((4, PLANE, planes, held, tokens), bf16),
            fast((4, planes, held, PLANE * tokens), bf16),
            fast((2, PLANE * tokens, WIDTH), bf16),
            fast((2, half, held, WIDTH), bf16),
            fast((half, held, ring), bf16),
            fast((max(half - 1, 1), held, ring), bf16),
            fast((max(half - 1, 1), held, columns), bf16),
            fast((more, held, ring)),
            fast((tokens, width)),
            fast((tokens, width), bf16),
            fast((tokens, channels)),
            fast((tokens, channels), bf16),
            fast((tokens, channels)),
            fast((tokens, channels)),
            fast((tokens + 16, channels)),
            fast((tokens + 16, 1)),
            fast((tokens, channels), bf16),
            fast((tokens, channels), bf16),
            fast((tokens, channels), bf16),
            fast((LANES, channels), bf16),
            fast((tokens, LANES)),
            fast((tokens, LANES)),
            fast((8, channels)),
            fast((8, channels)),
            fast((tokens, width)),
            fast((span * (NEAR + 1), LANES)),
            fast((span * (NEAR + 1), LANES)),
            fast((groups, near, LANES)),
            fast((groups, near, LANES)),
            fast((groups, near, LANES)),
            fast((groups, near, LANES)),
            fast((groups, near, LANES)),
            fast((span * (NEAR + 1), LANES)),
            fast((span * (NEAR + 1), LANES)),
            fast((groups, span, LANES)),
            fast((groups, span, LANES)),
            fast((groups, span, LANES)),
            fast((16, channels)),
            fast((rows, LANES)),
            fast((rows, LANES), bf16),
            fast((PLANE, rows // PLANE, LANES), bf16),
            fast((rows // PLANE, LANES)),
            fast((rows // PLANE, LANES), bf16),
            fast((planes, rows // count, LANES), bf16),
            fast((rows, LANES), bf16),
        ]
        + exchange_scratch(planes, groups, span)
        + [
            dma((4,)),
            dma((RING,)),
            dma((6, PLANE)),
            dma((6, PLANE)),
            dma((4, PLANE)),
            dma((4, PLANE)),
            dma((6, steps_z)),
            dma((6, steps_z)),
            dma((2, PLANE + 1)),
            dma((8,)),
            dma((8, max(PLANE, planes))),
            dma((6,)),
        ],
        compiler_params=params(collective_id=2, has_side_effects=True),
        name="mixer_back",
    )(
        d_out, x_in, *kept, gtwo, sums, doc_start, doc_start[:, None], norm1_gain[None], norm2_gain[None], gains[None],
        conv_w, skip[None], w_x, w_dt, rates, hidden, ggu, gated, seen, w_out, input_weight,
    )


def local(
    x_in,
    doc_start,
    norm1_gain,
    input_weight,
    conv_w,
    conv_b,
    w_x,
    dt_gain,
    b_gain,
    c_gain,
    w_dt,
    dt_bias,
    state_rate,
    skip,
    w_out,
    norm2_gain,
    w_gu,
    w_down,
    d_out,
):
    states = b_gain.shape[0]
    rank = dt_gain.shape[0]
    rates = rates_in(state_rate)
    gains = jnp.concatenate([dt_gain, b_gain, c_gain])
    (
        normed, z_low, conv_out, mixed, projected, rows, steps, pre, scanned, gated, resid_mid, two, seen, sums, padded,
    ) = mixer(
        x_in, doc_start, norm1_gain, input_weight, conv_w, conv_b, w_x, gains, w_dt, dt_bias, rates, skip, w_out, norm2_gain,
        states,
    )
    hidden, grad_gu, ffn_part, grad_two = ffn(two, d_out, w_gu, w_down)
    output = (resid_mid + (ffn_part + swap_cores(ffn_part))).astype(jnp.bfloat16)
    kept = (
        z_low, normed, two, resid_mid, conv_out, mixed, projected, rows, steps, pre, scanned, padded,
    )
    d_x, grads, wx_sum, wdt_sum, vectors, rate_sum, unused_x, unused_z = mixer_back(
        d_out, x_in, kept, grad_two, hidden, grad_gu, doc_start, norm1_gain, norm2_gain, gains, conv_w, skip, w_x, w_dt, rates,
        w_out, input_weight, states, gated, seen, sums,
    )
    count = lax.axis_size("seq")
    share = x_in.shape[1] // count
    units, channels = hidden.shape[1], conv_w.shape[1]

    def own(row):
        return lax.dynamic_slice(vectors[row], (lax.axis_index("seq") * share,), (share,))

    def part(start, size):
        return grads[:share, start : start + size]

    after_ff = 3 * units
    gain_row = vectors[9]
    return (
        output,
        d_x,
        own(7),
        jnp.stack([part(after_ff + 2 * channels, channels), part(after_ff + channels, channels)], 1),
        vectors[:4],
        vectors[4],
        wx_sum.T,
        gain_row[:rank],
        gain_row[rank : rank + states],
        gain_row[rank + states : rank + 2 * states],
        wdt_sum,
        vectors[5],
        rates_out(rate_sum),
        vectors[6],
        part(after_ff, channels).T,
        own(8),
        jnp.stack([part(units, units), part(2 * units, units)], 1),
        part(0, units).T,
    )


def solution(mesh):
    placed = (
        P("seq", None),
        P("seq"),
        P(),
        P(None, None, "head"),
        P(None, "head"),
        P("head"),
        P("head", None),
        P(),
        P(),
        P(),
        P(None, "head"),
        P("head"),
        P("head", None),
        P("head"),
        P("head", None),
        P(),
        P(None, None, "head"),
        P("head", None),
        P("seq", None),
    )
    return jax.shard_map(
        local,
        mesh=mesh,
        in_specs=placed,
        out_specs=(
            P("seq", None),
            P("seq", None),
            P("seq"),
            P("seq", None, "head"),
            P(None, "head"),
            P("head"),
            P("head", None),
            P(),
            P(),
            P(),
            P(None, "head"),
            P("head"),
            P("head", None),
            P("head"),
            P("head", "seq"),
            P("seq"),
            P("seq", None, "head"),
            P("head", "seq"),
        ),
        check_vma=False,
    )
```

```python
import functools
import math

import jax
import jax.numpy as jnp
from jax import lax
from jax.experimental import pallas as pl
from jax.experimental.pallas import tpu as pltpu
from jax.sharding import PartitionSpec as P

EPSILON = 1e-06
LANES = 128
CG = 4
WIDTH = CG * LANES
PLANE = 4
LOG2E = math.log2(math.e)
LN2 = math.log(2.0)
MESH = pl.DeviceIdType.MESH
VMEM_BYTES = 60 * 1024 * 1024


def f32(*shape):
    return jax.ShapeDtypeStruct(shape, jnp.float32)


def params(**more):
    return pltpu.CompilerParams(vmem_limit_bytes=VMEM_BYTES, **more)


def rates_in(state_rate):
    channels, states = state_rate.shape
    groups = channels // WIDTH
    parts = state_rate.reshape(groups, CG, LANES, states)
    return jnp.transpose(parts, (0, 3, 1, 2)).reshape(groups, states * CG, LANES) * (-LOG2E)


def rates_out(grad):
    groups, span, lanes = grad.shape
    parts = grad.reshape(groups, span // CG, CG, lanes)
    return jnp.transpose(parts, (0, 2, 3, 1)).reshape(groups * WIDTH, span // CG)


def pick_even(odd):
    row = lax.broadcasted_iota(jnp.int32, (LANES, 2 * LANES), 0)
    column = lax.broadcasted_iota(jnp.int32, (LANES, 2 * LANES), 1)
    return (column == 2 * row + odd).astype(jnp.float32).astype(jnp.bfloat16)


def widen(source, target):
    tokens, width = source.shape
    for block in range(width // LANES):
        piece = source[:, block * LANES : (block + 1) * LANES]
        for odd in range(2):
            target[odd * tokens : (odd + 1) * tokens, block * 2 * LANES : (block + 1) * 2 * LANES] = jnp.dot(
                piece, pick_even(odd), preferred_element_type=jnp.float32
            ).astype(jnp.bfloat16)


def narrow(source, target):
    tokens, width = target.shape
    row = lax.broadcasted_iota(jnp.int32, (2 * LANES, LANES), 0)
    column = lax.broadcasted_iota(jnp.int32, (2 * LANES, LANES), 1)
    pairs = (lax.div(row, 2) == column).astype(jnp.float32).astype(jnp.bfloat16)
    even = lax.rem(lax.broadcasted_iota(jnp.int32, (tokens, 2 * LANES), 1), 2) == 0
    for block in range(width // LANES):
        columns = slice(block * 2 * LANES, (block + 1) * 2 * LANES)
        value = jnp.where(even, source[:tokens, columns], source[tokens:, columns])
        total = None
        for unused in range(3):
            piece = value.astype(jnp.bfloat16)
            value = value - piece.astype(jnp.float32)
            term = jnp.dot(piece, pairs, preferred_element_type=jnp.float32)
            total = term if total is None else total + term
        target[:, block * LANES : (block + 1) * LANES] = total


def copy_to(source, target, send_sem, recv_sem, where):
    copy = pltpu.make_async_remote_copy(
        src_ref=source, dst_ref=target, send_sem=send_sem, recv_sem=recv_sem, device_id=where, device_id_type=MESH
    )
    copy.start()
    return copy


def wait_all(copies):
    for copy in copies:
        copy.wait()


class Places:
    def __init__(self, planes):
        self.planes = planes
        self.count = planes * PLANE
        self.me = lax.axis_index("seq")
        self.low = lax.rem(self.me, PLANE)
        self.high = lax.div(self.me, PLANE)
        self.core = lax.axis_index("head")

    def other(self):
        return {"head": 1 - self.core}

    def in_plane(self, shift):
        return {"seq": self.high * PLANE + lax.rem(self.low + shift, PLANE)}

    def across(self, shift):
        return {"seq": lax.rem(self.high + shift, self.planes) * PLANE + self.low}

    def along(self, shift):
        return {"seq": lax.rem(self.me + shift + self.count, self.count)}

    def mirror(self, mask):
        return self.low + sum((1 - 2 * lax.rem(lax.div(self.low, bit), 2)) * bit for bit in (1, 2) if mask & bit)

    def mirrored(self, mask):
        return {"seq": self.high * PLANE + self.mirror(mask)}

    def greet(self):
        partners = [self.other(), self.along(1), self.along(-1)]
        partners += [self.in_plane(shift) for shift in range(1, PLANE)]
        partners += [self.across(shift) for shift in range(1, self.planes)]
        barrier = pltpu.get_barrier_semaphore()
        for partner in partners:
            pl.semaphore_signal(barrier, inc=1, device_id=partner, device_id_type=MESH)
        return functools.partial(pl.semaphore_wait, barrier, len(partners))


class RowOf:
    def __init__(self, ref, row, width=None):
        self.ref, self.row, self.width = ref, row, width

    def __getitem__(self, key):
        columns = slice(0, self.width) if key is Ellipsis else key[1]
        return self.ref[self.row : self.row + 1, columns]


def as_column(row):
    return jnp.transpose(jnp.broadcast_to(row, (LANES, row.shape[1])))[:, :1]


def exchange_states(places, reverse, ends, sums, rates, pay, got, zpay, zgot, back, final, sems):
    low, high, planes = places.low, places.high, places.planes
    quarter = ends.shape[1] // PLANE
    send_a, recv_a, send_b, recv_b, send_c, recv_c = sems
    for k in range(PLANE):
        pay[k, :, :quarter, :] = ends[:, k * quarter : (k + 1) * quarter, :]
        pay[k, :, quarter:, :] = sums[...]
    copies = [
        copy_to(pay.at[lax.rem(low + shift, PLANE)], got.at[shift], send_a.at[shift], recv_a.at[shift], places.in_plane(shift))
        for shift in range(1, PLANE)
    ]
    got[0] = pay[low]
    mine = rates[:, pl.ds(pl.multiple_of(low * quarter, 8), quarter), :]

    def decay(total):
        return jnp.exp2(mine * jnp.concatenate([total] * (quarter // 8), axis=1))

    wait_all(copies)
    order = range(PLANE - 1, -1, -1) if reverse else range(PLANE)
    held, decays = {}, {}
    plane_end = plane_sum = None
    for j in order:
        part = got[lax.rem(low - j + PLANE, PLANE)]
        held[j] = part[:, :quarter, :]
        size = part[:, quarter:, :]
        decays[j] = decay(size)
        plane_end = held[j] if plane_end is None else plane_end * decays[j] + held[j]
        plane_sum = size if plane_sum is None else plane_sum + size
    zpay[:, :quarter, :] = plane_end
    zpay[:, quarter:, :] = plane_sum
    copies = [
        copy_to(zpay, zgot.at[shift], send_b.at[shift], recv_b.at[shift], places.across(shift))
        for shift in range(1, planes)
    ]
    zgot[0] = zpay[...]
    wait_all(copies)
    state = jnp.zeros_like(plane_end)
    for h in range(planes - 1, -1, -1) if reverse else range(planes):
        part = zgot[lax.rem(high - h + planes, planes)]
        after_h = state * decay(part[:, quarter:, :]) + part[:, :quarter, :]
        state = jnp.where(h > high if reverse else h < high, after_h, state)
    for j in order:
        back[j] = state
        state = state * decays[j] + held[j]
    copies = [
        copy_to(back.at[lax.rem(low + shift, PLANE)], final.at[low], send_c.at[shift], recv_c.at[shift], places.in_plane(shift))
        for shift in range(1, PLANE)
    ]
    final[low] = back[low]
    wait_all(copies)


def exchange_scratch(planes, groups, span):
    quarter = span // PLANE
    size = (groups, quarter + 8, LANES)
    dma = pltpu.SemaphoreType.DMA
    return [
        pltpu.VMEM((PLANE,) + size, jnp.float32),
        pltpu.VMEM((PLANE,) + size, jnp.float32),
        pltpu.VMEM(size, jnp.float32),
        pltpu.VMEM((planes,) + size, jnp.float32),
        pltpu.VMEM((PLANE, groups, quarter, LANES), jnp.float32),
        pltpu.VMEM((PLANE, groups, quarter, LANES), jnp.float32),
        dma((PLANE,)), dma((PLANE,)), dma((planes,)), dma((planes,)), dma((PLANE,)), dma((PLANE,)),
    ]


def block16(block):
    return pl.ds(pl.multiple_of(block * 16, 16), 16)


def lanes(j, width=WIDTH):
    return slice(j * width, (j + 1) * width)


def norm_rows(read, gain, write, tokens):
    def step(block, carry):
        rows = block16(block)
        value = read(rows)
        scale = lax.rsqrt(jnp.mean(value * value, axis=-1, keepdims=True) + EPSILON)
        write(rows, value * scale * gain[...])
        return carry

    lax.fori_loop(0, tokens // 16, step, 0)


def third_masks(shape, rank, states):
    lane = lax.broadcasted_iota(jnp.int32, shape, 1)
    return lane < rank, (lane >= rank) & (lane < rank + states), lane >= rank + states


def third_means(value, rank, states):
    out = None
    for mask, count in zip(third_masks(value.shape, rank, states), (rank, states, states)):
        mean = jnp.sum(jnp.where(mask, value, 0.0), axis=-1, keepdims=True) * (1.0 / count)
        part = jnp.where(mask, mean, 0.0)
        out = part if out is None else out + part
    return out


class Rows:
    def __init__(self, places, share, out, landed, send_sem, recv_sem):
        self.places, self.share, self.out, self.landed = places, share, out, landed
        self.send_sem, self.recv_sem = send_sem, recv_sem

    def put(self, read, width, which):
        planes = self.places.planes
        piece = math.gcd(self.share, LANES)
        for block in range(width // LANES):
            turned = jnp.transpose(read(lanes(block, LANES)).astype(jnp.float32)).astype(jnp.bfloat16)
            for at in range(0, LANES, piece):
                index = block * LANES + at
                owner, offset = index // self.share, index % self.share
                slot = flip_bits(owner // PLANE, self.places.high, planes)
                place = lax.div(slot, 2) + lax.rem(slot, 2) * (planes // 2)
                self.out[which, owner % PLANE, place, offset : offset + piece, :] = turned[at : at + piece]

    def send(self, which):
        tokens = self.out.shape[-1]
        copies = [
            copy_to(
                self.out.at[which, self.places.mirror(mask)],
                self.landed.at[which, :, :, pl.ds(mask * tokens, tokens)],
                self.send_sem.at[which, mask],
                self.recv_sem.at[which, mask],
                self.places.mirrored(mask),
            )
            for mask in range(1, PLANE)
        ]
        self.landed[which, :, :, :tokens] = self.out[which, self.places.low]
        return copies


def send_columns(places, source, landing, start, size, send_sem, recv_sem):
    return [
        copy_to(source, landing.at[mask - 1, :, pl.ds(start, size)], send_sem.at[mask], recv_sem.at[mask], places.mirrored(mask))
        for mask in (1, 2)
    ]


def relay_columns(places, landing, start, size, send_sem, recv_sem):
    copies = []
    for mask, at in ((1, start), (2, start + size // 2)):
        columns = pl.ds(at, size // 2)
        copies.append(
            copy_to(
                landing.at[mask - 1, :, columns],
                landing.at[PLANE - 2, :, columns],
                send_sem.at[3 * (mask - 1)],
                recv_sem.at[3 * (mask - 1)],
                places.mirrored(3 - mask),
            )
        )
    return copies


def front_kernel(planes, rank, states, share,
                 x_ref, d_ref, starts_ref, start_row, pack_ref, win_ref, wx_ref, wdt_ref, rate_ref, wout_ref, gu_ref, down_ref,
                 z_ref, conv_ref, mixed_ref, proj_ref, rows_ref, step_ref, pre_ref, scanned_ref, gated_ref, resid_ref,
                 sum_ref, padded, hidden_ref, ggu_ref, gtwo_ref, output_ref, landed_ref, seen_ref, xin,
                 normed, two, wide, big, wout, wdown, keep_pad, edge_out, edge_in, mixed_low, proj_out, proj_in, wdt,
                 spread_b, spread_c, near_step, near_push, near_out, held_ref, ends, seen, mix_out, mix_in, rows_out, landed,
                 gates, ups, total, ffn_out, ffn_in, two_in,
                 pay, got, zpay, zgot, back, final, send_a, recv_a, send_b, recv_b, send_c, recv_c,
                 load_sem, save_sem, edge_sem, proj_sem, mix_sem, r_send, r_recv, x_send, x_recv, pair_sem):
    conv_w_ref, conv_b_ref, dt_bias_ref, skip_ref = pack_ref, RowOf(pack_ref, 4), RowOf(pack_ref, 5), RowOf(pack_ref, 6)
    gain1_ref, gain2_ref, gains_ref = RowOf(pack_ref, 7), RowOf(pack_ref, 8), RowOf(pack_ref, 9, LANES)
    tokens, width = x_ref.shape
    channels = step_ref.shape[1]
    units = hidden_ref.shape[1]
    groups = channels // WIDTH
    tiles = units // WIDTH
    span = states * CG
    pairs = states // 2
    blocks = tokens // NEAR
    places = Places(planes)
    greeted = places.greet()

    def win_copy(j):
        return pltpu.make_async_copy(win_ref.at[:, :, pl.ds(j * WIDTH, WIDTH)], big.at[j], load_sem.at[j])

    def gu_copy(j):
        slot = (j + groups) % (groups + 1)
        return pltpu.make_async_copy(gu_ref.at[:, :, pl.ds(j * WIDTH, WIDTH)], big.at[slot], load_sem.at[groups + j])

    load_out = pltpu.make_async_copy(wout_ref, wout, load_sem.at[groups + tiles])
    load_down = pltpu.make_async_copy(down_ref, wdown, load_sem.at[groups + tiles + 1])
    for j in range(groups):
        win_copy(j).start()
    load_out.start()
    gu_copy(0).start()
    load_down.start()

    def put_normed(rows, value):
        normed[rows, :] = value.astype(jnp.bfloat16)

    norm_rows(lambda rows: x_ref[rows, :].astype(jnp.float32), gain1_ref, put_normed, tokens)
    widen(normed, wide)
    keep_pad[:8, :] = jnp.ones((8, 1), jnp.float32)
    keep_pad[8:, :] = as_column((1 - start_row[...]).astype(jnp.float32))
    wdt[:rank, :] = wdt_ref[...]
    wdt[rank:, :] = jnp.zeros((LANES - rank, channels), jnp.bfloat16)
    for j in range(groups):
        win_copy(j).wait()
        both = jnp.dot(wide[...], big[j].reshape(2 * width, WIDTH), preferred_element_type=jnp.float32).astype(jnp.bfloat16)
        padded[8:, lanes(j)] = both[:tokens].astype(jnp.float32)
        z_ref[:, lanes(j)] = both[tokens:]
        if j + 1 < tiles:
            gu_copy(j + 1).start()

    last_keep = (1 - starts_ref[tokens - 1]).astype(jnp.float32)
    before_keep = (1 - starts_ref[tokens - 2]).astype(jnp.float32)
    row = lax.broadcasted_iota(jnp.int32, (16, 1), 0)
    tail = jnp.where(
        row == 15, 1.0, jnp.where(row == 14, last_keep, jnp.where(row == 13, last_keep * before_keep, 0.0))
    )
    edge_out[...] = (padded[tokens - 8 :, :] * tail).astype(jnp.bfloat16)
    greeted()
    edge = copy_to(edge_out, edge_in, edge_sem.at[0], edge_sem.at[1], places.along(1))
    sender = Rows(places, share, rows_out, landed, r_send, r_recv)
    sender.put(lambda cols: d_ref[:, cols], width, 0)
    edge.wait()
    row_copies = sender.send(0)
    padded[:8, :] = edge_in[8:, :].astype(jnp.float32)

    def conv(block, carry):
        start = block * 16
        rows = block16(block)
        near = pl.ds(pl.multiple_of(start, 8), 24)
        keeps = keep_pad[near, :]
        keep = keeps[8:]
        two_keep = keep * keeps[7:23]
        three = two_keep * keeps[6:22]
        for j in range(groups):
            values = padded[near, lanes(j)]
            mix = conv_b_ref[:, lanes(j)] + conv_w_ref[3:4, lanes(j)] * values[8:]
            for offset, mask in ((1, keep), (2, two_keep), (3, three)):
                mix += conv_w_ref[3 - offset : 4 - offset, lanes(j)] * values[8 - offset : 24 - offset] * mask
            conv_ref[rows, lanes(j)] = mix
            mixed = mix * jax.nn.sigmoid(mix)
            mixed_ref[rows, lanes(j)] = mixed
            mixed_low[rows, lanes(j)] = mixed.astype(jnp.bfloat16)
        return carry

    lax.fori_loop(0, tokens // 16, conv, 0)
    proj_out[...] = jnp.dot(mixed_low[...], wx_ref[...], preferred_element_type=jnp.float32)
    proj = copy_to(proj_out, proj_in, proj_sem.at[0], proj_sem.at[1], places.other())
    sender.put(lambda cols: normed[:, cols], width, 1)
    proj.wait()
    row_copies += sender.send(1)
    projected = proj_out[...] + proj_in[...]
    proj_ref[...] = projected
    scaled = projected * lax.rsqrt(third_means(projected * projected, rank, states) + EPSILON) * gains_ref[...]
    rows_ref[...] = scaled
    low_rows = jnp.where(third_masks(scaled.shape, rank, states)[0], scaled, 0.0).astype(jnp.bfloat16)
    for j in range(groups):
        pre = jnp.dot(low_rows, wdt[:, lanes(j)], preferred_element_type=jnp.float32) + dt_bias_ref[:, lanes(j)]
        pre_ref[:, lanes(j)] = pre
        step_ref[:, lanes(j)] = jnp.maximum(pre, 0.0) + jnp.log1p(jnp.exp(-jnp.abs(pre)))

    def keep_of(t):
        return (1 - starts_ref[t]).astype(jnp.float32)

    def near_block(block):
        return pl.ds(pl.multiple_of(block * NEAR, NEAR), NEAR)

    def rate_of(g, p):
        return rate_ref[g, p * 8 : p * 8 + 8, :]

    held_ref[...] = jnp.zeros_like(held_ref)
    sum_ref[...] = jnp.zeros_like(sum_ref)

    def end(block, carry):
        at = near_block(block)
        near_spread_rows(rows_ref[at, :], rank, states, spread_b)
        near_spread_channels(step_ref[at, :], near_step)
        near_spread_channels(step_ref[at, :] * mixed_ref[at, :], near_push)
        for g in range(groups):
            held = [held_ref[g, p * 8 : p * 8 + 8, :] for p in range(pairs)]
            sizes = sum_ref[g]
            for i in range(NEAR):
                size = near_step[g, near_rows(i), :]
                push = near_push[g, near_rows(i), :]
                keep = keep_of(block * NEAR + i)
                sizes = sizes + size
                for p in range(pairs):
                    decay = jnp.exp2(size * rate_of(g, p))
                    held[p] = decay * (held[p] * keep) + push * spread_b[near_rows(i, p), :]
            for p in range(pairs):
                held_ref[g, p * 8 : p * 8 + 8, :] = held[p]
            sum_ref[g] = sizes
        return carry

    lax.fori_loop(0, blocks, end, 0)
    ends[...] = held_ref[...]
    exchange_states(places, False, ends, sum_ref, rate_ref, pay, got, zpay, zgot, back, final,
                    (send_a, recv_a, send_b, recv_b, send_c, recv_c))
    per = pairs // PLANE
    for g in range(groups):
        for p in range(pairs):
            held_ref[g, p * 8 : p * 8 + 8, :] = final[p // per, g, (p % per) * 8 : (p % per) * 8 + 8, :]

    def seen_copy(block, slot):
        at = pl.ds(pl.multiple_of(block * (NEAR * span), 8), NEAR * span)
        return pltpu.make_async_copy(seen.at[slot], seen_ref.at[:, at, :], save_sem.at[slot])

    def scan(block, carry):
        at = near_block(block)
        slot = lax.rem(block, RING)

        @pl.when(block >= RING)
        def _():
            seen_copy(block - RING, slot).wait()

        near_spread_rows(rows_ref[at, :], rank, states, spread_b)
        near_spread_rows(rows_ref[at, :], rank + states, states, spread_c)
        near_spread_channels(step_ref[at, :], near_step)
        near_spread_channels(step_ref[at, :] * mixed_ref[at, :], near_push)
        for g in range(groups):
            held = [held_ref[g, p * 8 : p * 8 + 8, :] for p in range(pairs)]
            for i in range(NEAR):
                size = near_step[g, near_rows(i), :]
                push = near_push[g, near_rows(i), :]
                keep = keep_of(block * NEAR + i)
                out = None
                for p in range(pairs):
                    seen[slot, g, i * span + p * 8 : i * span + p * 8 + 8, :] = held[p]
                    decay = jnp.exp2(size * rate_of(g, p))
                    held[p] = decay * (held[p] * keep) + push * spread_b[near_rows(i, p), :]
                    term = held[p] * spread_c[near_rows(i, p), :]
                    out = term if out is None else out + term
                near_out[g, near_rows(i), :] = out
            for p in range(pairs):
                held_ref[g, p * 8 : p * 8 + 8, :] = held[p]
        seen_copy(block, slot).start()
        for j in range(channels // LANES):
            cols = lanes(j, LANES)
            scanned_ref[at, cols] = near_fold_channels(near_out, j // CG, j % CG) + skip_ref[:, cols] * mixed_ref[at, cols]
        return carry

    lax.fori_loop(0, blocks, scan, 0)
    last_state = pltpu.make_async_copy(held_ref, seen_ref.at[:, pl.ds(tokens * span, span), :], save_sem.at[RING])
    last_state.start()

    def gate(block, carry):
        rows = block16(block)
        for j in range(groups):
            z = z_ref[rows, lanes(j)].astype(jnp.float32)
            gated_ref[rows, lanes(j)] = (scanned_ref[rows, lanes(j)] * (z * jax.nn.sigmoid(z))).astype(jnp.bfloat16)
        return carry

    lax.fori_loop(0, tokens // 16, gate, 0)
    gated_copies = send_columns(places, gated_ref, xin, 0, channels, x_send.at[0], x_recv.at[0])
    load_out.wait()
    copies = []
    for j in range(width // WIDTH):
        mix_out[j] = jnp.dot(gated_ref[...], wout[:, lanes(j)], preferred_element_type=jnp.float32)
        copies.append(copy_to(mix_out.at[j], mix_in.at[j], mix_sem.at[0, j], mix_sem.at[1, j], places.other()))
    wait_all(copies)

    def put_two(rows, value):
        two[rows, :] = value.astype(jnp.bfloat16)

    def read_mid(rows):
        for j in range(width // WIDTH):
            resid_ref[rows, lanes(j)] = x_ref[rows, lanes(j)].astype(jnp.float32) + (mix_out[j, rows, :] + mix_in[j, rows, :])
        return resid_ref[rows, :]

    norm_rows(read_mid, gain2_ref, put_two, tokens)

    widen(two, wide)
    for j in range(tiles):
        gu_copy(j).wait()
        both = jnp.dot(
            wide[...], big[(j + groups) % (groups + 1)].reshape(2 * width, WIDTH), preferred_element_type=jnp.float32
        )
        gate_part, up_part = both[:tokens], both[tokens:]
        gates[:, lanes(j)] = gate_part
        ups[:, lanes(j)] = up_part
        hidden_ref[:, lanes(j)] = (gate_part * jax.nn.sigmoid(gate_part) * up_part).astype(jnp.bfloat16)
    wait_all(gated_copies)
    gated_copies = relay_columns(places, xin, 0, channels, x_send.at[0], x_recv.at[0])
    hidden_copies = send_columns(places, hidden_ref, xin, channels, units, x_send.at[1], x_recv.at[1])
    sender.put(lambda cols: two[:, cols], width, 2)
    row_copies += sender.send(2)
    load_down.wait()

    def backward(j, carry):
        cols = pl.ds(pl.multiple_of(j * WIDTH, WIDTH), WIDTH)
        down = wdown[cols, :]
        grad_hidden = lax.dot_general(
            d_ref[...], down, (((1,), (1,)), ((), ())), preferred_element_type=jnp.float32
        )
        act, slope = silu_and_slope(gates[:, cols])
        grad_gate = (grad_hidden * ups[:, cols] * slope).astype(jnp.bfloat16)
        grad_up = (grad_hidden * act).astype(jnp.bfloat16)
        ggu_ref[0, :, cols] = grad_gate
        ggu_ref[1, :, cols] = grad_up
        ffn = jnp.dot(hidden_ref[:, cols], down, preferred_element_type=jnp.float32)
        ffn_out[...] = jnp.where(j == 0, ffn, ffn_out[...] + ffn)
        weights = big[lax.rem(j + groups, groups + 1)].reshape(2 * width, WIDTH)
        back_part = lax.dot_general(
            jnp.concatenate([grad_gate, grad_up], 0), weights, (((1,), (1,)), ((), ())), preferred_element_type=jnp.float32
        )
        total[...] = jnp.where(j == 0, back_part, total[...] + back_part)
        return carry

    lax.fori_loop(0, tiles, backward, 0)
    ffn_copy = copy_to(ffn_out, ffn_in, pair_sem.at[0], pair_sem.at[1], places.other())
    narrow(total, gtwo_ref)
    two_copy = copy_to(gtwo_ref, two_in, pair_sem.at[2], pair_sem.at[3], places.other())
    wait_all(hidden_copies)
    hidden_copies = relay_columns(places, xin, channels, units, x_send.at[1], x_recv.at[1])
    ffn_copy.wait()

    def put_output(block, carry):
        rows = block16(block)
        output_ref[rows, :] = (resid_ref[rows, :] + (ffn_out[rows, :] + ffn_in[rows, :])).astype(jnp.bfloat16)
        return carry

    lax.fori_loop(0, tokens // 16, put_output, 0)
    two_copy.wait()
    gtwo_ref[...] += two_in[...]
    wait_all(row_copies)
    landed_ref[...] = landed[...]
    last_state.wait()
    for block in range(blocks - RING, blocks):
        seen_copy(block, block % RING).wait()
    wait_all(gated_copies)
    wait_all(hidden_copies)


def front(x_in, d_out, doc_start, pack, input_weight, w_x, w_dt, rates, w_out, w_gu, w_down, states):
    tokens, width = x_in.shape
    channels = w_x.shape[0]
    units = w_down.shape[0]
    rank = w_dt.shape[0]
    groups, span, unused = rates.shape
    count = lax.axis_size("seq")
    planes = count // PLANE
    share = width // count
    share_held = share + -share % 32
    vmem = pl.BlockSpec(memory_space=pltpu.VMEM)
    smem = pl.BlockSpec(memory_space=pltpu.SMEM)
    hbm = pl.BlockSpec(memory_space=pl.ANY)
    dma = pltpu.SemaphoreType.DMA
    chunks = width // WIDTH
    tiles = units // WIDTH
    near = 8 * (NEAR + 1)

    def fast(shape, kind=jnp.float32):
        return pltpu.VMEM(shape, kind)

    def low(*shape):
        return jax.ShapeDtypeStruct(shape, jnp.bfloat16)

    bf16 = jnp.bfloat16
    return pl.pallas_call(
        functools.partial(front_kernel, planes, rank, states, share),
        out_shape=(
            low(tokens, channels),
            f32(tokens, channels),
            f32(tokens, channels),
            f32(tokens, LANES),
            f32(tokens, LANES),
            f32(tokens, channels),
            f32(tokens, channels),
            f32(tokens, channels),
            low(tokens, channels),
            f32(tokens, width),
            f32(groups, 8, LANES),
            f32(tokens + 8, channels),
            low(tokens, units),
            low(2, tokens, units),
            f32(tokens, width),
            low(tokens, width),
            low(3, planes, share_held, PLANE * tokens),
            f32(groups, (tokens + 1) * span, LANES),
            low(PLANE - 1, tokens, channels + units),
        ),
        in_specs=[vmem, vmem, smem, vmem, vmem, hbm, vmem, vmem, vmem, hbm, hbm, hbm],
        out_specs=(vmem,) * 17 + (hbm, hbm),
        scratch_shapes=[
            fast((tokens, width), bf16),
            fast((tokens, width), bf16),
            fast((2 * tokens, 2 * width), bf16),
            fast((groups + 1, width, 2, WIDTH), bf16),
            fast((channels, width), bf16),
            fast((units, width), bf16),
            fast((tokens + 8, 1)),
            fast((16, channels), bf16),
            fast((16, channels), bf16),
            fast((tokens, channels), bf16),
            fast((tokens, LANES)),
            fast((tokens, LANES)),
            fast((LANES, channels), bf16),
            fast((span * (NEAR + 1), LANES)),
            fast((span * (NEAR + 1), LANES)),
            fast((groups, near, LANES)),
            fast((groups, near, LANES)),
            fast((groups, near, LANES)),
            fast((groups, span, LANES)),
            fast((groups, span, LANES)),
            fast((RING, groups, NEAR * span, LANES)),
            fast((chunks, tokens, WIDTH)),
            fast((chunks, tokens, WIDTH)),
            fast((3, PLANE, planes, share_held, tokens), bf16),
            fast((3, planes, share_held, PLANE * tokens), bf16),
            fast((tokens, units)),
            fast((tokens, units)),
            fast((2 * tokens, 2 * width)),
            fast((tokens, width)),
            fast((tokens, width)),
            fast((tokens, width)),
        ]
        + exchange_scratch(planes, groups, span)
        + [
            dma((groups + tiles + 2,)),
            dma((RING + 1,)),
            dma((2,)),
            dma((2,)),
            dma((2, chunks)),
            dma((3, PLANE)),
            dma((3, PLANE)),
            dma((2, PLANE)),
            dma((2, PLANE)),
            dma((4,)),
        ],
        compiler_params=params(collective_id=1, has_side_effects=True),
        name="front",
    )(
        x_in, d_out, doc_start, doc_start[None], pack, input_weight, w_x, w_dt, rates, w_out, w_gu, w_down,
    )


RING = 3
NEAR = 8


def near_rows(i, p=0):
    return pl.ds(i + p * 8 * (NEAR + 1), 8, stride=NEAR + 1)


def near_slot(slot):
    return pl.ds(slot * (NEAR + 1), NEAR)


def near_spread_rows(rows, first, states, target):
    for n in range(states):
        column = jnp.broadcast_to(rows[:, first + n : first + n + 1], (NEAR, LANES))
        for group in range(CG):
            target[near_slot(n * CG + group), :] = column


def near_spread_channels(value, target):
    for j in range(value.shape[1] // LANES):
        g, k = j // CG, j % CG
        piece = value[:, lanes(j, LANES)]
        target[g, near_slot(k), :] = piece
        target[g, near_slot(CG + k), :] = piece


def near_fold_channels(source, g, k):
    return source[g, near_slot(k), :] + source[g, near_slot(CG + k), :]


def near_fold_rows(source, states, first, out):
    lane = lax.broadcasted_iota(jnp.int32, out.shape, 1)
    for n in range(states):
        total = None
        for group in range(CG):
            part = source[near_slot(n * CG + group), :]
            total = part if total is None else total + part
        out = jnp.where(lane == first + n, jnp.sum(total, axis=1, keepdims=True), out)
    return out


def flip_bits(k, high, planes):
    out = 0
    step = 1
    while step < planes:
        out = out + lax.rem(lax.div(k, step) + lax.div(high, step), 2) * step
        step *= 2
    return out


def slot_place(k, planes):
    return k // 2 + (k % 2) * (planes // 2)


def rms_back(grad, value, gain):
    scale = lax.rsqrt(jnp.mean(value * value, axis=-1, keepdims=True) + EPSILON)
    scaled = value * scale
    pull = grad * gain
    inner = jnp.mean(pull * scaled, axis=-1, keepdims=True)
    return scale * (pull - scaled * inner), grad * scaled


def silu_and_slope(value):
    sigmoid = jax.nn.sigmoid(value)
    return value * sigmoid, sigmoid * (1.0 + value * (1.0 - sigmoid))


def sum8(value):
    total = value[:8]
    for i in range(1, value.shape[0] // 8):
        total = total + value[i * 8 : (i + 1) * 8]
    return total


def back_kernel(planes, rank, states, share, units,
                d_ref, z_ref, resid_ref, mixed_ref, proj_ref, rows_ref, step_ref,
                scanned_ref, gtwo_ref, landed_ref, sum_ref, starts_ref, start_row, pack_ref, wx_ref, wdt_ref, rate_ref,
                hidden_ref, ggu_ref, gated_ref, seen_ref, wout_ref, win_ref, xfront, x_far, conv_far, pre_far, inner_far,
                dx_ref, grads_ref, wx_out, wdt_out, vec_out, rate_out, xin, zr0,
                x_ref, conv_ref, pre_ref, inner_ref, wout, win, wide, seen, rows_out, rows_mix, xbuf, zbuf, zs0, zs_more, zr_more, acc,
                gtwo_in, gmix_low, gscan, z_low, gstep, gmix, gpad, keep_pad, inner_low, mixed_low, gpre_low, wdt, dyp, dyp_in,
                edge_out, edge_in, norm_in, spread_b, spread_c, near_step, near_push, near_grad, near_lb, near_rq,
                near_gb, near_gc, mus, ends, rate_grad, vec, flat, sent, got, part, zsent, zgot, full,
                pay, egot, zpay, ezgot, back, final,
                send_a, recv_a, send_b, recv_b, send_c, recv_c,
                load_sem, seen_sem, x_send, x_recv, r_send, r_recv, z_send, z_recv, xbuf_sem, pair_sem, small_sem, save_sem, late_sem):
    conv_w_ref, skip_ref = pack_ref, RowOf(pack_ref, 6)
    gain1_ref, gain2_ref, gains_ref = RowOf(pack_ref, 7), RowOf(pack_ref, 8), RowOf(pack_ref, 9, LANES)
    tokens, width = d_ref.shape
    channels = step_ref.shape[1]
    groups = channels // WIDTH
    chunks = width // WIDTH
    span = states * CG
    pairs = states // 2
    steps_z = planes.bit_length() - 1
    half = planes // 2
    places = Places(planes)
    low, high = places.low, places.high
    greeted = places.greet()
    blocks = tokens // NEAR

    late = [
        pltpu.make_async_copy(far, near, late_sem.at[i])
        for i, (far, near) in enumerate(((conv_far, conv_ref), (pre_far, pre_ref), (inner_far, inner_ref), (x_far, x_ref)))
    ]
    def wout_copy(j):
        rows = pl.ds(j * WIDTH, WIDTH)
        return pltpu.make_async_copy(wout_ref.at[rows, :], wout.at[j % 2], load_sem.at[2 + j % 2])

    wout_copy(0).start()
    wout_copy(1).start()

    def seen_copy(block, slot):
        at = pl.ds(pl.multiple_of(block * (NEAR * span), 8), (NEAR + 1) * span)
        return pltpu.make_async_copy(seen_ref.at[:, at, :], seen.at[slot], seen_sem.at[slot])

    for k in range(RING - 1):
        seen_copy(blocks - 1 - k, k).start()

    def win_copy(j):
        return pltpu.make_async_copy(win_ref.at[:, :, pl.ds(j * WIDTH, WIDTH)], win.at[j % 2], load_sem.at[j % 2])

    win_copy(0).start()
    win_copy(1).start()
    for load in late:
        load.start()

    greeted()
    sender = Rows(places, share, rows_out, rows_mix, r_send, r_recv)
    row_copies = {}

    unit_copies = {}
    offsets, at = [], 0
    for unit_width, unused in units:
        offsets.append(at)
        at += unit_width

    def unit_source(u):
        return (hidden_ref, ggu_ref.at[0], ggu_ref.at[1], gated_ref, z_low, inner_low)[u]

    ring_width = max(unit_width for unit_width, unused in units)
    turn = (0, 2, 3, 1, 4, 5)

    def unit_columns(u):
        return pl.ds(offsets[u], units[u][0])

    def ring_columns(u):
        return pl.ds(turn[u] % 2 * ring_width, units[u][0])

    def columns_of(u, j):
        return pl.ds(pl.multiple_of(offsets[u] + j * WIDTH, WIDTH), WIDTH)

    def ring_of(u, j):
        return pl.ds(pl.multiple_of(turn[u] % 2 * ring_width + j * WIDTH, WIDTH), WIDTH)

    def first_slot(step):
        return sum(planes // 2 ** (k + 1) for k in range(1, step))

    landed_units = (0, 3)
    landed_at = {3: 0, 0: units[3][0]}

    def send_unit(u):
        unit_copies[u] = send_columns(places, unit_source(u), xin, offsets[u], units[u][0], x_send.at[u], x_recv.at[u])

    def relay(u):
        wait_all(unit_copies[u])
        unit_copies[u] = relay_columns(places, xin, offsets[u], units[u][0], x_send.at[u], x_recv.at[u])

    def partner(step):
        size = 2**step
        bit = lax.rem(lax.div(high, size), 2)
        return {"seq": (high + (1 - 2 * bit) * size) * PLANE + low}

    z_copies = {}

    def load_chunk(u, j, slot, with_z):
        local = pl.ds(pl.multiple_of(j * WIDTH, WIDTH), WIDTH)
        whole = columns_of(u, j)
        copies = [
            pltpu.make_async_copy(unit_source(u).at[:, local], xbuf.at[slot, pl.ds(0, tokens), :], xbuf_sem.at[slot, 0])
        ]
        for shift in range(1, PLANE):
            if u in landed_units:
                arrived = xfront.at[shift - 1, :, pl.ds(pl.multiple_of(landed_at[u] + j * WIDTH, WIDTH), WIDTH)]
            else:
                arrived = xin.at[shift - 1, :, whole]
            copies.append(
                pltpu.make_async_copy(
                    arrived, xbuf.at[slot, pl.ds(shift * tokens, tokens), :], xbuf_sem.at[slot, shift]
                )
            )
        if with_z:
            copies.append(pltpu.make_async_copy(zr0.at[:, :, whole], zbuf.at[slot], xbuf_sem.at[slot, PLANE]))
        return copies

    def over_chunks(u, with_z, use):
        count = units[u][0] // WIDTH
        for copy in load_chunk(u, 0, 0, with_z):
            copy.start()

        def body(j, carry):
            slot = lax.rem(j, 2)

            @pl.when(j + 1 < count)
            def _():
                for copy in load_chunk(u, j + 1, 1 - slot, with_z):
                    copy.start()

            for copy in load_chunk(u, j, slot, with_z):
                copy.wait()
            use(slot, j)
            return carry

        lax.fori_loop(0, count, body, 0)

    def product(u, slot, first):
        which = units[u][1]
        rows = rows_mix[0, first : first + half] if which == 3 else landed_ref[which, first : first + half]
        left = rows.reshape(half * rows_mix.shape[2], PLANE * tokens)
        return jnp.dot(left, xbuf[slot], preferred_element_type=jnp.float32).reshape(half, rows_mix.shape[2], WIDTH)

    def stage_one(u):
        if u not in landed_units:
            wait_all(unit_copies[u])
        which = units[u][1]
        if which in row_copies:
            wait_all(row_copies.pop(which))

        def use(slot, j):
            zs0[:, :, ring_of(u, j)] = product(u, slot, half).astype(jnp.bfloat16)

        over_chunks(u, False, use)
        z_copies[u] = copy_to(zs0.at[:, :, ring_columns(u)], zr0.at[:, :, unit_columns(u)], z_send.at[u, 0], z_recv.at[u, 0], partner(0))

    def split(u, step, value, j):
        count = value.shape[0]
        columns = ring_of(u, j)
        if count == 1:
            acc[0, :, columns] = value[0]
            return
        for i in range(count // 2):
            acc[i, :, columns] = value[2 * i]
            zs_more[first_slot(step) + i, :, columns] = value[2 * i + 1].astype(jnp.bfloat16)

    def send_more(u, step):
        slots = pl.ds(first_slot(step), planes // 2 ** (step + 1))
        z_copies[u] = copy_to(
            zs_more.at[slots, :, ring_columns(u)],
            zr_more.at[slots, :, unit_columns(u)],
            z_send.at[u, step],
            z_recv.at[u, step],
            partner(step),
        )

    def stage_two(u):
        z_copies.pop(u).wait()
        for other in list(saves):
            if turn[other] % 2 == turn[u] % 2:
                saves.pop(other).wait()

        def use(slot, j):
            split(u, 1, product(u, slot, 0) + zbuf[slot].astype(jnp.float32), j)

        over_chunks(u, True, use)
        if steps_z > 1:
            send_more(u, 1)

    saves = {}

    def stage_three(u):
        count_chunks = units[u][0] // WIDTH
        for step in range(2, steps_z + 1):
            z_copies.pop(u).wait()
            count = planes // 2**step

            def body(j, carry):
                first = first_slot(step - 1)
                value = acc[:count, :, ring_of(u, j)] + zr_more[first : first + count, :, columns_of(u, j)].astype(jnp.float32)
                split(u, step, value, j)
                return carry

            lax.fori_loop(0, count_chunks, body, 0)
            if count > 1:
                send_more(u, step)
        save = pltpu.make_async_copy(acc.at[0, :, ring_columns(u)], grads_ref.at[:, unit_columns(u)], save_sem.at[u])
        save.start()
        saves[u] = save

    HIDDEN, GATE, UP, GATED, Z, INNER = range(6)
    send_unit(GATE)
    stage_one(HIDDEN)
    keep_pad[:8, :] = jnp.ones((8, 1), jnp.float32)
    keep_pad[8 : 8 + tokens, :] = as_column((1 - start_row[...]).astype(jnp.float32))
    keep_pad[8 + tokens :, :] = jnp.ones((8, 1), jnp.float32)
    wdt[:rank, :] = wdt_ref[...]
    wdt[rank:, :] = jnp.zeros((LANES - rank, channels), jnp.bfloat16)
    vec[...] = jnp.zeros_like(vec)
    rate_grad[...] = jnp.zeros_like(rate_grad)


    def mid(block, carry):
        rows = block16(block)
        grad = gtwo_ref[rows, :]
        back_to, gain_part = rms_back(grad, resid_ref[rows, :], gain2_ref[...])
        value = d_ref[rows, :].astype(jnp.float32) + back_to
        dx_ref[rows, :] = value
        gmix_low[rows, :] = value.astype(jnp.bfloat16)
        return carry + sum8(gain_part)

    norm2 = lax.fori_loop(0, tokens // 16, mid, jnp.zeros((8, width), jnp.float32))
    vec[8:9, :] = jnp.sum(norm2, axis=0, keepdims=True)
    sender.put(lambda cols: dx_ref[:, cols], width, 0)
    row_copies[3] = sender.send(0)

    for j in range(groups):
        wout_copy(j).wait()
        gscan[:, lanes(j)] = lax.dot_general(
            gmix_low[...], wout[j % 2], (((1,), (1,)), ((), ())), preferred_element_type=jnp.float32
        )
        if j + 2 < groups:
            wout_copy(j + 2).start()

    relay(GATE)
    send_unit(UP)
    def gate(block, carry):
        rows = block16(block)
        out = []
        for j in range(groups):
            cols = lanes(j)
            act, slope = silu_and_slope(z_ref[rows, cols].astype(jnp.float32))
            grad = gscan[rows, cols]
            grad_scanned = grad * act
            gscan[rows, cols] = grad_scanned
            z_low[rows, cols] = (grad * scanned_ref[rows, cols] * slope).astype(jnp.bfloat16)
            mixed = mixed_ref[rows, cols]
            mixed_low[rows, cols] = mixed.astype(jnp.bfloat16)
            out.append(carry[j] + sum8(grad_scanned * mixed))
        return tuple(out)

    skips = lax.fori_loop(0, tokens // 16, gate, (jnp.zeros((8, WIDTH), jnp.float32),) * groups)
    for j in range(groups):
        vec[6:7, lanes(j)] = jnp.sum(skips[j], axis=0, keepdims=True)

    stage_one(GATED)
    def keep_of(t):
        return (1 - starts_ref[t]).astype(jnp.float32)

    def near_block(block):
        return pl.ds(pl.multiple_of(block * NEAR, NEAR), NEAR)

    def rate_of(g, p):
        return rate_ref[g, p * 8 : p * 8 + 8, :]

    mus[...] = jnp.zeros_like(mus)

    def feed(k, carry):
        block = blocks - 1 - k
        at = near_block(block)
        near_spread_rows(rows_ref[at, :], rank + states, states, spread_c)
        near_spread_channels(step_ref[at, :], near_step)
        near_spread_channels(gscan[at, :], near_grad)
        for g in range(groups):
            held = [mus[g, p * 8 : p * 8 + 8, :] for p in range(pairs)]
            for i in range(NEAR - 1, -1, -1):
                size = near_step[g, near_rows(i), :]
                grad = near_grad[g, near_rows(i), :]
                keep = keep_of(block * NEAR + i)
                for p in range(pairs):
                    lam = held[p] + spread_c[near_rows(i, p), :] * grad
                    held[p] = jnp.exp2(size * rate_of(g, p)) * (lam * keep)
            for p in range(pairs):
                mus[g, p * 8 : p * 8 + 8, :] = held[p]
        return carry

    lax.fori_loop(0, blocks, feed, 0)
    ends[...] = mus[...]
    relay(UP)
    send_unit(Z)
    exchange_states(places, True, ends, sum_ref, rate_ref, pay, egot, zpay, ezgot, back, final,
                    (send_a, recv_a, send_b, recv_b, send_c, recv_c))
    per = pairs // PLANE
    for g in range(groups):
        for p in range(pairs):
            mus[g, p * 8 : p * 8 + 8, :] = final[p // per, g, (p % per) * 8 : (p % per) * 8 + 8, :]
    stage_two(HIDDEN)
    stage_one(GATE)

    def scan(k, carry):
        block = blocks - 1 - k
        at = near_block(block)
        slot = lax.rem(k, RING)

        @pl.when(k + RING - 1 < blocks)
        def _():
            seen_copy(block - (RING - 1), lax.rem(k + RING - 1, RING)).start()

        near_spread_rows(rows_ref[at, :], rank, states, spread_b)
        near_spread_rows(rows_ref[at, :], rank + states, states, spread_c)
        near_spread_channels(step_ref[at, :], near_step)
        near_spread_channels(step_ref[at, :] * mixed_ref[at, :], near_push)
        near_spread_channels(gscan[at, :], near_grad)
        seen_copy(block, slot).wait()
        held = [[mus[g, p * 8 : p * 8 + 8, :] for p in range(pairs)] for g in range(groups)]
        for i in range(NEAR - 1, -1, -1):
            keep = keep_of(block * NEAR + i)
            sizes = [near_step[g, near_rows(i), :] for g in range(groups)]
            pushes = [near_push[g, near_rows(i), :] for g in range(groups)]
            grads = [near_grad[g, near_rows(i), :] for g in range(groups)]
            lbs, rqs = [None] * groups, [None] * groups
            for p in range(pairs):
                b_value = spread_b[near_rows(i, p), :]
                c_value = spread_c[near_rows(i, p), :]
                gb = gc = None
                for g in range(groups):
                    rate = rate_of(g, p)
                    before = seen[slot, g, i * span + p * 8 : i * span + p * 8 + 8, :]
                    now = seen[slot, g, (i + 1) * span + p * 8 : (i + 1) * span + p * 8 + 8, :]
                    lam = held[g][p] + c_value * grads[g]
                    mu = jnp.exp2(sizes[g] * rate) * (lam * keep)
                    held[g][p] = mu
                    q = mu * before
                    rate_grad[g, p * 8 : p * 8 + 8, :] += q * sizes[g]
                    lb, rq = lam * b_value, q * rate
                    lbs[g] = lb if lbs[g] is None else lbs[g] + lb
                    rqs[g] = rq if rqs[g] is None else rqs[g] + rq
                    gb_term, gc_term = lam * pushes[g], now * grads[g]
                    gb = gb_term if gb is None else gb + gb_term
                    gc = gc_term if gc is None else gc + gc_term
                near_gb[near_rows(i, p), :] = gb
                near_gc[near_rows(i, p), :] = gc
            for g in range(groups):
                near_lb[g, near_rows(i), :] = lbs[g]
                near_rq[g, near_rows(i), :] = rqs[g]
        for g in range(groups):
            for p in range(pairs):
                mus[g, p * 8 : p * 8 + 8, :] = held[g][p]
        for j in range(channels // LANES):
            g, k_group = j // CG, j % CG
            cols = lanes(j, LANES)
            lb = near_fold_channels(near_lb, g, k_group)
            rq = near_fold_channels(near_rq, g, k_group)
            gmix[at, cols] = step_ref[at, cols] * lb
            gstep[at, cols] = mixed_ref[at, cols] * lb + LN2 * rq
        row = jnp.zeros((NEAR, LANES), jnp.float32)
        row = near_fold_rows(near_gb, states, rank, row)
        dyp[at, :] = near_fold_rows(near_gc, states, rank + states, row)
        return carry

    lax.fori_loop(0, blocks // 2, scan, 0)
    relay(Z)
    lax.fori_loop(blocks // 2, blocks, scan, 0)
    stage_two(GATED)
    stage_one(UP)
    stage_three(HIDDEN)

    for load in late:
        load.wait()

    def pre_grad(block, carry):
        rows = block16(block)
        out = []
        for j in range(groups):
            grad = gstep[rows, lanes(j)] * jax.nn.sigmoid(pre_ref[rows, lanes(j)])
            gpre_low[rows, lanes(j)] = grad.astype(jnp.bfloat16)
            out.append(carry[j] + sum8(grad))
        return tuple(out)

    biases = lax.fori_loop(0, tokens // 16, pre_grad, (jnp.zeros((8, WIDTH), jnp.float32),) * groups)
    for j in range(groups):
        vec[5:6, lanes(j)] = jnp.sum(biases[j], axis=0, keepdims=True)
    dyp[...] += lax.dot_general(gpre_low[...], wdt[...], (((1,), (1,)), ((), ())), preferred_element_type=jnp.float32)
    dyp_copy = copy_to(dyp, dyp_in, pair_sem.at[2], pair_sem.at[3], places.other())
    turned = jnp.transpose(rows_ref[...]).astype(jnp.bfloat16)
    at_flat = channels // LANES * LANES
    for j in range(channels // LANES):
        value = jnp.dot(turned[:rank], gpre_low[:, lanes(j, LANES)], preferred_element_type=jnp.float32)
        flat[at_flat + j * rank : at_flat + (j + 1) * rank, :] = value
    dyp_copy.wait()
    projected = proj_ref[...]
    scale = lax.rsqrt(third_means(projected * projected, rank, states) + EPSILON)
    scaled = projected * scale
    grad = dyp[...] + dyp_in[...]
    pull = grad * gains_ref[...]
    proj_grad = scale * (pull - scaled * third_means(pull * scaled, rank, states))
    vec[9:10, :LANES] = jnp.sum(sum8(grad * scaled), axis=0, keepdims=True)
    proj_low = proj_grad.astype(jnp.bfloat16)
    turned_proj = jnp.transpose(proj_grad).astype(jnp.bfloat16)

    for j in range(groups):
        gmix[:, lanes(j)] += lax.dot_general(
            proj_low, wx_ref[lanes(j), :], (((1,), (1,)), ((), ())), preferred_element_type=jnp.float32
        )
    gpad[:8, :] = jnp.zeros((8, channels), jnp.float32)
    gpad[8 + tokens :, :] = jnp.zeros((8, channels), jnp.float32)

    def conv_grad(block, carry):
        rows = block16(block)
        to = pl.ds(pl.multiple_of(block * 16 + 8, 8), 16)
        near = pl.ds(pl.multiple_of(block * 16, 8), 24)
        keeps = keep_pad[near, :]
        keep = keeps[8:]
        two = keep * keeps[7:23]
        three = two * keeps[6:22]
        out = []
        for j in range(groups):
            cols = lanes(j)
            unused, slope = silu_and_slope(conv_ref[rows, cols])
            grad = (gmix[rows, cols] + skip_ref[:, cols] * gscan[rows, cols]) * slope
            gpad[to, cols] = grad
            values = inner_ref[near, cols]
            sums = [carry[j][4] + sum8(grad), carry[j][3] + sum8(grad * values[8:])]
            for offset, mask in ((1, keep), (2, two), (3, three)):
                sums.append(carry[j][3 - offset] + sum8(grad * values[8 - offset : 24 - offset] * mask))
            out.append((sums[4], sums[3], sums[2], sums[1], sums[0]))
        return tuple(out)

    empty = jnp.zeros((8, WIDTH), jnp.float32)
    taps = lax.fori_loop(0, tokens // 16, conv_grad, ((empty,) * 5,) * groups)
    for j in range(groups):
        for i in range(5):
            vec[i : i + 1, lanes(j)] = jnp.sum(taps[j][i], axis=0, keepdims=True)

    stage_two(GATE)
    def taps_back(start, count, columns):
        near = pl.ds(pl.multiple_of(start, 8), count + 8)
        keeps = keep_pad[near, :]
        grads = gpad[near, columns]
        total = conv_w_ref[3:4, columns] * grads[:count]
        mask = None
        for offset in (1, 2, 3):
            mask = keeps[1 : count + 1] if mask is None else mask * keeps[offset : count + offset]
            total += conv_w_ref[3 - offset : 4 - offset, columns] * grads[offset : count + offset] * mask
        return total

    for j in range(groups):
        edge_out[:, lanes(j)] = taps_back(0, 8, lanes(j))
    edge_copy = copy_to(edge_out, edge_in, pair_sem.at[4], pair_sem.at[5], places.along(-1))

    def inner_grad(block, carry):
        rows = block16(block)
        for j in range(groups):
            inner_low[rows, lanes(j)] = taps_back(block * 16 + 8, 16, lanes(j)).astype(jnp.bfloat16)
        return carry

    lax.fori_loop(0, tokens // 16 - 1, inner_grad, 0)
    last_keep, before_keep = keep_of(tokens - 1), keep_of(tokens - 2)
    row = lax.broadcasted_iota(jnp.int32, (16, 1), 0)
    tail = jnp.where(
        row == 15, 1.0, jnp.where(row == 14, last_keep, jnp.where(row == 13, last_keep * before_keep, 0.0))
    )
    tail = jnp.where(places.me == places.count - 1, 0.0, tail)
    edge_copy.wait()
    for j in range(groups):
        here = taps_back(tokens - 8, 16, lanes(j))
        edge = jnp.concatenate([jnp.zeros((8, WIDTH), jnp.float32), edge_in[:, lanes(j)]], 0) * tail
        inner_low[tokens - 16 :, lanes(j)] = (here + edge).astype(jnp.bfloat16)
    send_unit(INNER)
    stage_one(Z)
    stage_three(GATED)
    for j in range(channels // LANES):
        flat[j * LANES : (j + 1) * LANES, :] = jnp.dot(
            turned_proj, mixed_low[:, lanes(j, LANES)], preferred_element_type=jnp.float32
        )

    for j in range(groups):
        win_copy(j).wait()
        both = lax.dot_general(
            jnp.concatenate([inner_low[:, lanes(j)], z_low[:, lanes(j)]], 0),
            win[j % 2].reshape(2 * width, WIDTH),
            (((1,), (1,)), ((), ())),
            preferred_element_type=jnp.float32,
        )
        if j == 0:
            wide[...] = both
        else:
            wide[...] += both
        if j + 2 < groups:
            win_copy(j + 2).start()
    narrow(wide, gtwo_in)
    norm_copy = copy_to(gtwo_in, norm_in, pair_sem.at[6], pair_sem.at[7], places.other())
    relay(INNER)
    stage_two(UP)
    norm_copy.wait()

    def first_norm(block, carry):
        rows = block16(block)
        grad = gtwo_in[rows, :] + norm_in[rows, :]
        back_to, gain_part = rms_back(grad, x_ref[rows, :].astype(jnp.float32), gain1_ref[...])
        dx_ref[rows, :] += back_to
        return carry + sum8(gain_part)

    norm1 = lax.fori_loop(0, tokens // 16, first_norm, jnp.zeros((8, width), jnp.float32))
    vec[7:8, :] = jnp.sum(norm1, axis=0, keepdims=True)

    rows_flat = flat.shape[0]
    quarter = rows_flat // PLANE
    chunk = quarter // planes
    at_vec = at_flat + channels // LANES * rank
    for j in range(channels // LANES):
        flat[at_vec + j * 16 : at_vec + (j + 1) * 16, :] = vec[:, lanes(j, LANES)]
    at_rate = at_vec + channels // LANES * 16
    for g in range(groups):
        flat[at_rate + g * span : at_rate + (g + 1) * span, :] = -rate_grad[g]
    at_end = at_rate + groups * span
    if at_end < rows_flat:
        flat[at_end:, :] = jnp.zeros((rows_flat - at_end, LANES), jnp.float32)
    sent[...] = flat[...].astype(jnp.bfloat16)

    def quarter_at(index):
        return pl.ds(pl.multiple_of(index * quarter, 16), quarter)

    def chunk_at(index):
        return pl.ds(pl.multiple_of(index * chunk, 16), chunk)

    small_copies = [
        copy_to(sent.at[quarter_at(lax.rem(low + shift, PLANE))], got.at[shift], small_sem.at[0, shift], small_sem.at[1, shift],
                places.in_plane(shift))
        for shift in range(1, PLANE)
    ]
    part[...] = flat[quarter_at(low), :]
    stage_one(INNER)
    stage_three(GATE)
    stage_two(Z)
    wait_all(small_copies)
    for shift in range(1, PLANE):
        part[...] += got[shift].astype(jnp.float32)
    zsent[...] = part[...].astype(jnp.bfloat16)
    small_copies = [
        copy_to(zsent.at[chunk_at(lax.rem(high + shift, planes))], zgot.at[shift], small_sem.at[2, shift], small_sem.at[3, shift],
                places.across(shift))
        for shift in range(1, planes)
    ]
    stage_three(UP)
    wait_all(small_copies)
    total = part[chunk_at(high), :]
    for shift in range(1, planes):
        total += zgot[shift].astype(jnp.float32)
    mine = pl.ds(pl.multiple_of(low * quarter + high * chunk, 16), chunk)
    full[mine, :] = total.astype(jnp.bfloat16)
    small_copies = [
        copy_to(full.at[mine], full.at[mine], small_sem.at[4, shift], small_sem.at[5, shift], places.across(shift))
        for shift in range(1, planes)
    ]
    stage_two(INNER)
    wait_all(small_copies)
    small_copies = [
        copy_to(full.at[quarter_at(low)], full.at[quarter_at(low)], small_sem.at[6, shift], small_sem.at[7, shift],
                places.in_plane(shift))
        for shift in range(1, PLANE)
    ]
    stage_three(Z)
    wait_all(small_copies)
    for j in range(channels // LANES):
        wx_out[:, lanes(j, LANES)] = full[j * LANES : (j + 1) * LANES, :].astype(jnp.float32)
        wdt_out[:, lanes(j, LANES)] = full[at_flat + j * rank : at_flat + (j + 1) * rank, :].astype(jnp.float32)
        vec_out[:, lanes(j, LANES)] = full[at_vec + j * 16 : at_vec + (j + 1) * 16, :].astype(jnp.float32)
    for g in range(groups):
        rate_out[g] = full[at_rate + g * span : at_rate + (g + 1) * span, :].astype(jnp.float32)
    stage_three(INNER)
    wait_all(saves.values())


def mixer_back(d_out, x_in, kept, far, gtwo, hidden, ggu, doc_start, pack, w_x, w_dt, rates,
               w_out, input_weight, states, gated, seen, sums, landed, xfront):
    tokens, width = x_in.shape
    channels = w_x.shape[0]
    unit_ff = hidden.shape[1]
    rank = w_dt.shape[0]
    groups, span, unused = rates.shape
    count = lax.axis_size("seq")
    planes = count // PLANE
    share = width // count
    held = share + -share % 32
    units = ((unit_ff, 0), (unit_ff, 2), (unit_ff, 2), (channels, 3), (channels, 1), (channels, 1))
    columns = sum(u for u, unused in units)
    vmem = pl.BlockSpec(memory_space=pltpu.VMEM)
    smem = pl.BlockSpec(memory_space=pltpu.SMEM)
    hbm = pl.BlockSpec(memory_space=pl.ANY)
    dma = pltpu.SemaphoreType.DMA
    bf16 = jnp.bfloat16
    half = planes // 2
    ring = 2 * max(u for u, unused in units)
    more = max(planes // 4, 1)
    steps_z = planes.bit_length() - 1
    rows = channels + channels // LANES * (rank + 16) + groups * span
    rows += -rows % (16 * count)
    near = 8 * (NEAR + 1)

    def fast(shape, kind=jnp.float32):
        return pltpu.VMEM(shape, kind)

    return pl.pallas_call(
        functools.partial(back_kernel, planes, rank, states, share, units),
        out_shape=(
            f32(tokens, width),
            f32(held, columns),
            f32(LANES, channels),
            f32(rank, channels),
            f32(16, channels),
            f32(groups, span, LANES),
            jax.ShapeDtypeStruct((PLANE - 1, tokens, columns), bf16),
            jax.ShapeDtypeStruct((half, held, columns), bf16),
        ),
        in_specs=[vmem] * 11 + [smem] + [vmem] * 5 + [hbm] * 11,
        out_specs=(vmem, hbm, vmem, vmem, vmem, vmem, hbm, hbm),
        scratch_shapes=[
            fast((tokens, width), bf16),
            fast((tokens, channels)),
            fast((tokens, channels)),
            fast((tokens + 8, channels)),
            fast((2, WIDTH, width), bf16),
            fast((2, width, 2, WIDTH), bf16),
            fast((2 * tokens, 2 * width)),
            fast((RING, groups, (NEAR + 1) * span, LANES)),
            fast((1, PLANE, planes, held, tokens), bf16),
            fast((1, planes, held, PLANE * tokens), bf16),
            fast((2, PLANE * tokens, WIDTH), bf16),
            fast((2, half, held, WIDTH), bf16),
            fast((half, held, ring), bf16),
            fast((max(half - 1, 1), held, ring), bf16),
            fast((max(half - 1, 1), held, columns), bf16),
            fast((more, held, ring)),
            fast((tokens, width)),
            fast((tokens, width), bf16),
            fast((tokens, channels)),
            fast((tokens, channels), bf16),
            fast((tokens, channels)),
            fast((tokens, channels)),
            fast((tokens + 16, channels)),
            fast((tokens + 16, 1)),
            fast((tokens, channels), bf16),
            fast((tokens, channels), bf16),
            fast((tokens, channels), bf16),
            fast((LANES, channels), bf16),
            fast((tokens, LANES)),
            fast((tokens, LANES)),
            fast((8, channels)),
            fast((8, channels)),
            fast((tokens, width)),
            fast((span * (NEAR + 1), LANES)),
            fast((span * (NEAR + 1), LANES)),
            fast((groups, near, LANES)),
            fast((groups, near, LANES)),
            fast((groups, near, LANES)),
            fast((groups, near, LANES)),
            fast((groups, near, LANES)),
            fast((span * (NEAR + 1), LANES)),
            fast((span * (NEAR + 1), LANES)),
            fast((groups, span, LANES)),
            fast((groups, span, LANES)),
            fast((groups, span, LANES)),
            fast((16, channels)),
            fast((rows, LANES)),
            fast((rows, LANES), bf16),
            fast((PLANE, rows // PLANE, LANES), bf16),
            fast((rows // PLANE, LANES)),
            fast((rows // PLANE, LANES), bf16),
            fast((planes, rows // count, LANES), bf16),
            fast((rows, LANES), bf16),
        ]
        + exchange_scratch(planes, groups, span)
        + [
            dma((4,)),
            dma((RING,)),
            dma((6, PLANE)),
            dma((6, PLANE)),
            dma((1, PLANE)),
            dma((1, PLANE)),
            dma((6, steps_z)),
            dma((6, steps_z)),
            dma((2, PLANE + 1)),
            dma((8,)),
            dma((8, max(PLANE, planes))),
            dma((6,)),
            dma((4,)),
        ],
        compiler_params=params(collective_id=2, has_side_effects=True),
        name="mixer_back",
    )(
        d_out, *kept, gtwo, landed, sums, doc_start, doc_start[None], pack, w_x, w_dt, rates, hidden, ggu, gated, seen, w_out, input_weight, xfront, x_in, *far,
    )


def local(
    x_in,
    doc_start,
    norm1_gain,
    input_weight,
    conv_w,
    conv_b,
    w_x,
    dt_gain,
    b_gain,
    c_gain,
    w_dt,
    dt_bias,
    state_rate,
    skip,
    w_out,
    norm2_gain,
    w_gu,
    w_down,
    d_out,
):
    states = b_gain.shape[0]
    rank = dt_gain.shape[0]
    channels = conv_b.shape[0]
    rates = rates_in(state_rate)
    gains = jnp.concatenate([dt_gain, b_gain, c_gain])
    pack = jnp.concatenate(
        [
            conv_w,
            conv_b[None],
            dt_bias[None],
            skip[None],
            norm1_gain[None],
            norm2_gain[None],
            jnp.pad(gains, (0, channels - gains.shape[0]))[None],
        ],
        0,
    )
    (
        z_low, conv_out, mixed, projected, rows, steps, pre, scanned, gated, resid_mid, sums, padded, hidden, grad_gu, grad_two,
        output, landed, seen, gathered,
    ) = front(x_in, d_out, doc_start, pack, input_weight, w_x, w_dt, rates, w_out, w_gu, w_down, states)
    kept = (z_low, resid_mid, mixed, projected, rows, steps, scanned)
    d_x, grads, wx_sum, wdt_sum, vectors, rate_sum, unused_x, unused_z = mixer_back(
        d_out, x_in, kept, (conv_out, pre, padded), grad_two, hidden, grad_gu, doc_start, pack, w_x, w_dt, rates,
        w_out, input_weight, states, gated, seen, sums, landed, gathered,
    )
    count = lax.axis_size("seq")
    share = x_in.shape[1] // count
    units = hidden.shape[1]

    def own(row):
        return lax.dynamic_slice(vectors[row], (lax.axis_index("seq") * share,), (share,))

    def part(start, size):
        return grads[:share, start : start + size]

    after_ff = 3 * units
    gain_row = vectors[9]
    return (
        output,
        d_x,
        own(7),
        jnp.stack([part(after_ff + 2 * channels, channels), part(after_ff + channels, channels)], 1),
        vectors[:4],
        vectors[4],
        wx_sum.T,
        gain_row[:rank],
        gain_row[rank : rank + states],
        gain_row[rank + states : rank + 2 * states],
        wdt_sum,
        vectors[5],
        rates_out(rate_sum),
        vectors[6],
        part(after_ff, channels).T,
        own(8),
        jnp.stack([part(units, units), part(2 * units, units)], 1),
        part(0, units).T,
    )


def solution(mesh):
    placed = (
        P("seq", None),
        P("seq"),
        P(),
        P(None, None, "head"),
        P(None, "head"),
        P("head"),
        P("head", None),
        P(),
        P(),
        P(),
        P(None, "head"),
        P("head"),
        P("head", None),
        P("head"),
        P("head", None),
        P(),
        P(None, None, "head"),
        P("head", None),
        P("seq", None),
    )
    return jax.shard_map(
        local,
        mesh=mesh,
        in_specs=placed,
        out_specs=(
            P("seq", None),
            P("seq", None),
            P("seq"),
            P("seq", None, "head"),
            P(None, "head"),
            P("head"),
            P("head", None),
            P(),
            P(),
            P(),
            P(None, "head"),
            P("head"),
            P("head", None),
            P("head"),
            P("head", "seq"),
            P("seq"),
            P("seq", None, "head"),
            P("head", "seq"),
        ),
        check_vma=False,
    )
```

```python
import functools
import math

import jax
import jax.numpy as jnp
from jax import lax
from jax.experimental import pallas as pl
from jax.experimental.pallas import tpu as pltpu
from jax.sharding import PartitionSpec as P

EPSILON = 1e-06
LANES = 128
CG = 4
WIDTH = CG * LANES
PLANE = 4
LOG2E = math.log2(math.e)
LN2 = math.log(2.0)
MESH = pl.DeviceIdType.MESH
VMEM_BYTES = 60 * 1024 * 1024


def f32(*shape):
    return jax.ShapeDtypeStruct(shape, jnp.float32)


def params(**more):
    return pltpu.CompilerParams(vmem_limit_bytes=VMEM_BYTES, **more)


def rates_in(state_rate):
    channels, states = state_rate.shape
    groups = channels // WIDTH
    parts = state_rate.reshape(groups, CG, LANES, states)
    return jnp.transpose(parts, (0, 3, 1, 2)).reshape(groups, states * CG, LANES) * (-LOG2E)


def rates_out(grad):
    groups, span, lanes = grad.shape
    parts = grad.reshape(groups, span // CG, CG, lanes)
    return jnp.transpose(parts, (0, 2, 3, 1)).reshape(groups * WIDTH, span // CG)


def pick_even(odd):
    row = lax.broadcasted_iota(jnp.int32, (LANES, 2 * LANES), 0)
    column = lax.broadcasted_iota(jnp.int32, (LANES, 2 * LANES), 1)
    return (column == 2 * row + odd).astype(jnp.float32).astype(jnp.bfloat16)


def widen(source, target):
    tokens, width = source.shape
    for block in range(width // LANES):
        piece = source[:, block * LANES : (block + 1) * LANES]
        for odd in range(2):
            target[odd * tokens : (odd + 1) * tokens, block * 2 * LANES : (block + 1) * 2 * LANES] = jnp.dot(
                piece, pick_even(odd), preferred_element_type=jnp.float32
            ).astype(jnp.bfloat16)


def narrow(source, target):
    tokens, width = target.shape
    row = lax.broadcasted_iota(jnp.int32, (2 * LANES, LANES), 0)
    column = lax.broadcasted_iota(jnp.int32, (2 * LANES, LANES), 1)
    pairs = (lax.div(row, 2) == column).astype(jnp.float32).astype(jnp.bfloat16)
    even = lax.rem(lax.broadcasted_iota(jnp.int32, (tokens, 2 * LANES), 1), 2) == 0
    for block in range(width // LANES):
        columns = slice(block * 2 * LANES, (block + 1) * 2 * LANES)
        value = jnp.where(even, source[:tokens, columns], source[tokens:, columns])
        total = None
        for unused in range(3):
            piece = value.astype(jnp.bfloat16)
            value = value - piece.astype(jnp.float32)
            term = jnp.dot(piece, pairs, preferred_element_type=jnp.float32)
            total = term if total is None else total + term
        target[:, block * LANES : (block + 1) * LANES] = total


def copy_to(source, target, send_sem, recv_sem, where):
    copy = pltpu.make_async_remote_copy(
        src_ref=source, dst_ref=target, send_sem=send_sem, recv_sem=recv_sem, device_id=where, device_id_type=MESH
    )
    copy.start()
    return copy


def wait_all(copies):
    for copy in copies:
        copy.wait()


class Places:
    def __init__(self, planes):
        self.planes = planes
        self.count = planes * PLANE
        self.me = lax.axis_index("seq")
        self.low = lax.rem(self.me, PLANE)
        self.high = lax.div(self.me, PLANE)
        self.core = lax.axis_index("head")

    def other(self):
        return {"head": 1 - self.core}

    def in_plane(self, shift):
        return {"seq": self.high * PLANE + lax.rem(self.low + shift, PLANE)}

    def across(self, shift):
        return {"seq": lax.rem(self.high + shift, self.planes) * PLANE + self.low}

    def along(self, shift):
        return {"seq": lax.rem(self.me + shift + self.count, self.count)}

    def mirror(self, mask):
        return self.low + sum((1 - 2 * lax.rem(lax.div(self.low, bit), 2)) * bit for bit in (1, 2) if mask & bit)

    def mirrored(self, mask):
        return {"seq": self.high * PLANE + self.mirror(mask)}

    def greet(self):
        partners = [self.other(), self.along(1), self.along(-1)]
        partners += [self.in_plane(shift) for shift in range(1, PLANE)]
        partners += [self.across(shift) for shift in range(1, self.planes)]
        barrier = pltpu.get_barrier_semaphore()
        for partner in partners:
            pl.semaphore_signal(barrier, inc=1, device_id=partner, device_id_type=MESH)
        return functools.partial(pl.semaphore_wait, barrier, len(partners))


class RowOf:
    def __init__(self, ref, row, width=None):
        self.ref, self.row, self.width = ref, row, width

    def __getitem__(self, key):
        columns = slice(0, self.width) if key is Ellipsis else key[1]
        return self.ref[self.row : self.row + 1, columns]


def as_column(row):
    return jnp.transpose(jnp.broadcast_to(row, (LANES, row.shape[1])))[:, :1]


def exchange_states(places, reverse, ends, sums, rates, pay, got, zpay, zgot, back, final, sems):
    low, high, planes = places.low, places.high, places.planes
    quarter = ends.shape[1] // PLANE
    send_a, recv_a, send_b, recv_b, send_c, recv_c = sems
    for k in range(PLANE):
        pay[k, :, :quarter, :] = ends[:, k * quarter : (k + 1) * quarter, :]
        pay[k, :, quarter:, :] = sums[...]
    copies = [
        copy_to(pay.at[lax.rem(low + shift, PLANE)], got.at[shift], send_a.at[shift], recv_a.at[shift], places.in_plane(shift))
        for shift in range(1, PLANE)
    ]
    got[0] = pay[low]
    mine = rates[:, pl.ds(pl.multiple_of(low * quarter, 8), quarter), :]

    def decay(total):
        return jnp.exp2(mine * jnp.concatenate([total] * (quarter // 8), axis=1))

    wait_all(copies)
    order = range(PLANE - 1, -1, -1) if reverse else range(PLANE)
    held, decays = {}, {}
    plane_end = plane_sum = None
    for j in order:
        part = got[lax.rem(low - j + PLANE, PLANE)]
        held[j] = part[:, :quarter, :]
        size = part[:, quarter:, :]
        decays[j] = decay(size)
        plane_end = held[j] if plane_end is None else plane_end * decays[j] + held[j]
        plane_sum = size if plane_sum is None else plane_sum + size
    zpay[:, :quarter, :] = plane_end
    zpay[:, quarter:, :] = plane_sum
    copies = [
        copy_to(zpay, zgot.at[shift], send_b.at[shift], recv_b.at[shift], places.across(shift))
        for shift in range(1, planes)
    ]
    zgot[0] = zpay[...]
    wait_all(copies)
    state = jnp.zeros_like(plane_end)
    for h in range(planes - 1, -1, -1) if reverse else range(planes):
        part = zgot[lax.rem(high - h + planes, planes)]
        after_h = state * decay(part[:, quarter:, :]) + part[:, :quarter, :]
        state = jnp.where(h > high if reverse else h < high, after_h, state)
    for j in order:
        back[j] = state
        state = state * decays[j] + held[j]
    copies = [
        copy_to(back.at[lax.rem(low + shift, PLANE)], final.at[low], send_c.at[shift], recv_c.at[shift], places.in_plane(shift))
        for shift in range(1, PLANE)
    ]
    final[low] = back[low]
    wait_all(copies)


def exchange_scratch(planes, groups, span):
    quarter = span // PLANE
    size = (groups, quarter + 8, LANES)
    dma = pltpu.SemaphoreType.DMA
    return [
        pltpu.VMEM((PLANE,) + size, jnp.float32),
        pltpu.VMEM((PLANE,) + size, jnp.float32),
        pltpu.VMEM(size, jnp.float32),
        pltpu.VMEM((planes,) + size, jnp.float32),
        pltpu.VMEM((PLANE, groups, quarter, LANES), jnp.float32),
        pltpu.VMEM((PLANE, groups, quarter, LANES), jnp.float32),
        dma((PLANE,)), dma((PLANE,)), dma((planes,)), dma((planes,)), dma((PLANE,)), dma((PLANE,)),
    ]


def block16(block):
    return pl.ds(pl.multiple_of(block * 16, 16), 16)


def lanes(j, width=WIDTH):
    return slice(j * width, (j + 1) * width)


def norm_rows(read, gain, write, tokens):
    def step(block, carry):
        rows = block16(block)
        value = read(rows)
        scale = lax.rsqrt(jnp.mean(value * value, axis=-1, keepdims=True) + EPSILON)
        write(rows, value * scale * gain[...])
        return carry

    lax.fori_loop(0, tokens // 16, step, 0)


def third_masks(shape, rank, states):
    lane = lax.broadcasted_iota(jnp.int32, shape, 1)
    return lane < rank, (lane >= rank) & (lane < rank + states), lane >= rank + states


def third_means(value, rank, states):
    out = None
    for mask, count in zip(third_masks(value.shape, rank, states), (rank, states, states)):
        mean = jnp.sum(jnp.where(mask, value, 0.0), axis=-1, keepdims=True) * (1.0 / count)
        part = jnp.where(mask, mean, 0.0)
        out = part if out is None else out + part
    return out


class Rows:
    def __init__(self, places, share, out, landed, send_sem, recv_sem):
        self.places, self.share, self.out, self.landed = places, share, out, landed
        self.send_sem, self.recv_sem = send_sem, recv_sem

    def put(self, read, width, which):
        planes = self.places.planes
        piece = math.gcd(self.share, LANES)
        for block in range(width // LANES):
            turned = jnp.transpose(read(lanes(block, LANES)).astype(jnp.float32)).astype(jnp.bfloat16)
            for at in range(0, LANES, piece):
                index = block * LANES + at
                owner, offset = index // self.share, index % self.share
                slot = flip_bits(owner // PLANE, self.places.high, planes)
                place = lax.div(slot, 2) + lax.rem(slot, 2) * (planes // 2)
                self.out[which, owner % PLANE, place, offset : offset + piece, :] = turned[at : at + piece]

    def send(self, which):
        tokens = self.out.shape[-1]
        copies = [
            copy_to(
                self.out.at[which, self.places.mirror(mask)],
                self.landed.at[which, :, :, pl.ds(mask * tokens, tokens)],
                self.send_sem.at[which, mask],
                self.recv_sem.at[which, mask],
                self.places.mirrored(mask),
            )
            for mask in range(1, PLANE)
        ]
        self.landed[which, :, :, :tokens] = self.out[which, self.places.low]
        return copies


def send_columns(places, source, landing, start, size, send_sem, recv_sem):
    return [
        copy_to(source, landing.at[mask - 1, :, pl.ds(start, size)], send_sem.at[mask], recv_sem.at[mask], places.mirrored(mask))
        for mask in (1, 2)
    ]


def relay_columns(places, landing, start, size, send_sem, recv_sem):
    copies = []
    for mask, at in ((1, start), (2, start + size // 2)):
        columns = pl.ds(at, size // 2)
        copies.append(
            copy_to(
                landing.at[mask - 1, :, columns],
                landing.at[PLANE - 2, :, columns],
                send_sem.at[3 * (mask - 1)],
                recv_sem.at[3 * (mask - 1)],
                places.mirrored(3 - mask),
            )
        )
    return copies


def front_kernel(planes, rank, states, share,
                 x_ref, d_ref, starts_ref, start_row, pack_ref, win_ref, wx_ref, wdt_ref, rate_ref, wout_ref, gu_ref, down_ref,
                 z_ref, conv_ref, mixed_ref, proj_ref, rows_ref, step_ref, pre_ref, scanned_ref, gated_ref, resid_ref,
                 sum_ref, padded, hidden_ref, ggu_ref, gtwo_ref, output_ref, landed_ref, seen_ref, xin,
                 normed, two, wide, big, wout, wdown, keep_pad, edge_out, edge_in, mixed_low, proj_out, proj_in, wdt,
                 spread_b, spread_c, near_step, near_push, near_out, held_ref, ends, seen, mix_out, mix_in, rows_out, landed,
                 gates, ups, total, ffn_out, ffn_in, two_in,
                 pay, got, zpay, zgot, back, final, send_a, recv_a, send_b, recv_b, send_c, recv_c,
                 load_sem, save_sem, edge_sem, proj_sem, mix_sem, r_send, r_recv, x_send, x_recv, pair_sem):
    conv_w_ref, conv_b_ref, dt_bias_ref, skip_ref = pack_ref, RowOf(pack_ref, 4), RowOf(pack_ref, 5), RowOf(pack_ref, 6)
    gain1_ref, gain2_ref, gains_ref = RowOf(pack_ref, 7), RowOf(pack_ref, 8), RowOf(pack_ref, 9, LANES)
    tokens, width = x_ref.shape
    channels = step_ref.shape[1]
    units = hidden_ref.shape[1]
    groups = channels // WIDTH
    tiles = units // WIDTH
    span = states * CG
    pairs = states // 2
    blocks = tokens // NEAR
    places = Places(planes)
    greeted = places.greet()

    def win_copy(j):
        return pltpu.make_async_copy(win_ref.at[:, :, pl.ds(j * WIDTH, WIDTH)], big.at[j], load_sem.at[j])

    def gu_copy(j):
        slot = (j + groups) % (groups + 1)
        return pltpu.make_async_copy(gu_ref.at[:, :, pl.ds(j * WIDTH, WIDTH)], big.at[slot], load_sem.at[groups + j])

    load_out = pltpu.make_async_copy(wout_ref, wout, load_sem.at[groups + tiles])
    load_down = pltpu.make_async_copy(down_ref, wdown, load_sem.at[groups + tiles + 1])
    for j in range(groups):
        win_copy(j).start()

    def put_normed(rows, value):
        normed[rows, :] = value.astype(jnp.bfloat16)

    norm_rows(lambda rows: x_ref[rows, :].astype(jnp.float32), gain1_ref, put_normed, tokens)
    widen(normed, wide)
    keep_pad[:8, :] = jnp.ones((8, 1), jnp.float32)
    keep_pad[8:, :] = as_column((1 - start_row[...]).astype(jnp.float32))
    wdt[:rank, :] = wdt_ref[...]
    wdt[rank:, :] = jnp.zeros((LANES - rank, channels), jnp.bfloat16)
    for j in range(groups):
        win_copy(j).wait()
        both = jnp.dot(wide[...], big[j].reshape(2 * width, WIDTH), preferred_element_type=jnp.float32).astype(jnp.bfloat16)
        padded[8:, lanes(j)] = both[:tokens].astype(jnp.float32)
        z_ref[:, lanes(j)] = both[tokens:]

    load_out.start()
    for j in range(tiles):
        gu_copy(j).start()
    load_down.start()
    last_keep = (1 - starts_ref[tokens - 1]).astype(jnp.float32)
    before_keep = (1 - starts_ref[tokens - 2]).astype(jnp.float32)
    row = lax.broadcasted_iota(jnp.int32, (16, 1), 0)
    tail = jnp.where(
        row == 15, 1.0, jnp.where(row == 14, last_keep, jnp.where(row == 13, last_keep * before_keep, 0.0))
    )
    edge_out[...] = (padded[tokens - 8 :, :] * tail).astype(jnp.bfloat16)
    greeted()
    edge = copy_to(edge_out, edge_in, edge_sem.at[0], edge_sem.at[1], places.along(1))
    sender = Rows(places, share, rows_out, landed, r_send, r_recv)
    sender.put(lambda cols: d_ref[:, cols], width, 0)
    edge.wait()
    row_copies = sender.send(0)
    padded[:8, :] = edge_in[8:, :].astype(jnp.float32)

    def conv(block, carry):
        start = block * 16
        rows = block16(block)
        near = pl.ds(pl.multiple_of(start, 8), 24)
        keeps = keep_pad[near, :]
        keep = keeps[8:]
        two_keep = keep * keeps[7:23]
        three = two_keep * keeps[6:22]
        for j in range(groups):
            values = padded[near, lanes(j)]
            mix = conv_b_ref[:, lanes(j)] + conv_w_ref[3:4, lanes(j)] * values[8:]
            for offset, mask in ((1, keep), (2, two_keep), (3, three)):
                mix += conv_w_ref[3 - offset : 4 - offset, lanes(j)] * values[8 - offset : 24 - offset] * mask
            conv_ref[rows, lanes(j)] = mix
            mixed = mix * jax.nn.sigmoid(mix)
            mixed_ref[rows, lanes(j)] = mixed
            mixed_low[rows, lanes(j)] = mixed.astype(jnp.bfloat16)
        return carry

    lax.fori_loop(0, tokens // 16, conv, 0)
    proj_out[...] = jnp.dot(mixed_low[...], wx_ref[...], preferred_element_type=jnp.float32)
    proj = copy_to(proj_out, proj_in, proj_sem.at[0], proj_sem.at[1], places.other())
    sender.put(lambda cols: normed[:, cols], width, 1)
    proj.wait()
    row_copies += sender.send(1)
    projected = proj_out[...] + proj_in[...]
    proj_ref[...] = projected
    scaled = projected * lax.rsqrt(third_means(projected * projected, rank, states) + EPSILON) * gains_ref[...]
    rows_ref[...] = scaled
    low_rows = jnp.where(third_masks(scaled.shape, rank, states)[0], scaled, 0.0).astype(jnp.bfloat16)
    for j in range(groups):
        pre = jnp.dot(low_rows, wdt[:, lanes(j)], preferred_element_type=jnp.float32) + dt_bias_ref[:, lanes(j)]
        pre_ref[:, lanes(j)] = pre
        step_ref[:, lanes(j)] = jnp.maximum(pre, 0.0) + jnp.log1p(jnp.exp(-jnp.abs(pre)))

    def keep_of(t):
        return (1 - starts_ref[t]).astype(jnp.float32)

    def near_block(block):
        return pl.ds(pl.multiple_of(block * NEAR, NEAR), NEAR)

    def rate_of(g, p):
        return rate_ref[g, p * 8 : p * 8 + 8, :]

    held_ref[...] = jnp.zeros_like(held_ref)
    sum_ref[...] = jnp.zeros_like(sum_ref)

    def end(block, carry):
        at = near_block(block)
        near_spread_rows(rows_ref[at, :], rank, states, spread_b)
        near_spread_channels(step_ref[at, :], near_step)
        near_spread_channels(step_ref[at, :] * mixed_ref[at, :], near_push)
        for g in range(groups):
            held = [held_ref[g, p * 8 : p * 8 + 8, :] for p in range(pairs)]
            sizes = sum_ref[g]
            for i in range(NEAR):
                size = near_step[g, near_rows(i), :]
                push = near_push[g, near_rows(i), :]
                keep = keep_of(block * NEAR + i)
                sizes = sizes + size
                for p in range(pairs):
                    decay = jnp.exp2(size * rate_of(g, p))
                    held[p] = decay * (held[p] * keep) + push * spread_b[near_rows(i, p), :]
            for p in range(pairs):
                held_ref[g, p * 8 : p * 8 + 8, :] = held[p]
            sum_ref[g] = sizes
        return carry

    lax.fori_loop(0, blocks, end, 0)
    ends[...] = held_ref[...]
    exchange_states(places, False, ends, sum_ref, rate_ref, pay, got, zpay, zgot, back, final,
                    (send_a, recv_a, send_b, recv_b, send_c, recv_c))
    per = pairs // PLANE
    for g in range(groups):
        for p in range(pairs):
            held_ref[g, p * 8 : p * 8 + 8, :] = final[p // per, g, (p % per) * 8 : (p % per) * 8 + 8, :]

    def seen_copy(block, slot):
        at = pl.ds(pl.multiple_of(block * (NEAR * span), 8), NEAR * span)
        return pltpu.make_async_copy(seen.at[slot], seen_ref.at[:, at, :], save_sem.at[slot])

    def scan(block, carry):
        at = near_block(block)
        slot = lax.rem(block, RING)

        @pl.when(block >= RING)
        def _():
            seen_copy(block - RING, slot).wait()

        near_spread_rows(rows_ref[at, :], rank, states, spread_b)
        near_spread_rows(rows_ref[at, :], rank + states, states, spread_c)
        near_spread_channels(step_ref[at, :], near_step)
        near_spread_channels(step_ref[at, :] * mixed_ref[at, :], near_push)
        for g in range(groups):
            held = [held_ref[g, p * 8 : p * 8 + 8, :] for p in range(pairs)]
            for i in range(NEAR):
                size = near_step[g, near_rows(i), :]
                push = near_push[g, near_rows(i), :]
                keep = keep_of(block * NEAR + i)
                out = None
                for p in range(pairs):
                    seen[slot, g, i * span + p * 8 : i * span + p * 8 + 8, :] = held[p]
                    decay = jnp.exp2(size * rate_of(g, p))
                    held[p] = decay * (held[p] * keep) + push * spread_b[near_rows(i, p), :]
                    term = held[p] * spread_c[near_rows(i, p), :]
                    out = term if out is None else out + term
                near_out[g, near_rows(i), :] = out
            for p in range(pairs):
                held_ref[g, p * 8 : p * 8 + 8, :] = held[p]
        seen_copy(block, slot).start()
        for j in range(channels // LANES):
            cols = lanes(j, LANES)
            scanned_ref[at, cols] = near_fold_channels(near_out, j // CG, j % CG) + skip_ref[:, cols] * mixed_ref[at, cols]
        return carry

    lax.fori_loop(0, blocks, scan, 0)
    last_state = pltpu.make_async_copy(held_ref, seen_ref.at[:, pl.ds(tokens * span, span), :], save_sem.at[RING])
    last_state.start()

    def gate(block, carry):
        rows = block16(block)
        for j in range(groups):
            z = z_ref[rows, lanes(j)].astype(jnp.float32)
            gated_ref[rows, lanes(j)] = (scanned_ref[rows, lanes(j)] * (z * jax.nn.sigmoid(z))).astype(jnp.bfloat16)
        return carry

    lax.fori_loop(0, tokens // 16, gate, 0)
    gated_copies = send_columns(places, gated_ref, xin, 0, channels, x_send.at[0], x_recv.at[0])
    load_out.wait()
    copies = []
    for j in range(width // WIDTH):
        mix_out[j] = jnp.dot(gated_ref[...], wout[:, lanes(j)], preferred_element_type=jnp.float32)
        copies.append(copy_to(mix_out.at[j], mix_in.at[j], mix_sem.at[0, j], mix_sem.at[1, j], places.other()))
    wait_all(copies)

    def put_two(rows, value):
        two[rows, :] = value.astype(jnp.bfloat16)

    def read_mid(rows):
        for j in range(width // WIDTH):
            resid_ref[rows, lanes(j)] = x_ref[rows, lanes(j)].astype(jnp.float32) + (mix_out[j, rows, :] + mix_in[j, rows, :])
        return resid_ref[rows, :]

    norm_rows(read_mid, gain2_ref, put_two, tokens)

    widen(two, wide)
    for j in range(tiles):
        gu_copy(j).wait()
        both = jnp.dot(
            wide[...], big[(j + groups) % (groups + 1)].reshape(2 * width, WIDTH), preferred_element_type=jnp.float32
        )
        gate_part, up_part = both[:tokens], both[tokens:]
        gates[:, lanes(j)] = gate_part
        ups[:, lanes(j)] = up_part
        hidden_ref[:, lanes(j)] = (gate_part * jax.nn.sigmoid(gate_part) * up_part).astype(jnp.bfloat16)
    wait_all(gated_copies)
    gated_copies = relay_columns(places, xin, 0, channels, x_send.at[0], x_recv.at[0])
    hidden_copies = send_columns(places, hidden_ref, xin, channels, units, x_send.at[1], x_recv.at[1])
    sender.put(lambda cols: two[:, cols], width, 2)
    row_copies += sender.send(2)
    load_down.wait()

    def backward(j, carry):
        cols = pl.ds(pl.multiple_of(j * WIDTH, WIDTH), WIDTH)
        down = wdown[cols, :]
        grad_hidden = lax.dot_general(
            d_ref[...], down, (((1,), (1,)), ((), ())), preferred_element_type=jnp.float32
        )
        act, slope = silu_and_slope(gates[:, cols])
        grad_gate = (grad_hidden * ups[:, cols] * slope).astype(jnp.bfloat16)
        grad_up = (grad_hidden * act).astype(jnp.bfloat16)
        ggu_ref[0, :, cols] = grad_gate
        ggu_ref[1, :, cols] = grad_up
        ffn = jnp.dot(hidden_ref[:, cols], down, preferred_element_type=jnp.float32)
        ffn_out[...] = jnp.where(j == 0, ffn, ffn_out[...] + ffn)
        weights = big[lax.rem(j + groups, groups + 1)].reshape(2 * width, WIDTH)
        back_part = lax.dot_general(
            jnp.concatenate([grad_gate, grad_up], 0), weights, (((1,), (1,)), ((), ())), preferred_element_type=jnp.float32
        )
        total[...] = jnp.where(j == 0, back_part, total[...] + back_part)
        return carry

    lax.fori_loop(0, tiles, backward, 0)
    ffn_copy = copy_to(ffn_out, ffn_in, pair_sem.at[0], pair_sem.at[1], places.other())
    narrow(total, gtwo_ref)
    two_copy = copy_to(gtwo_ref, two_in, pair_sem.at[2], pair_sem.at[3], places.other())
    ffn_copy.wait()

    def put_output(block, carry):
        rows = block16(block)
        output_ref[rows, :] = (resid_ref[rows, :] + (ffn_out[rows, :] + ffn_in[rows, :])).astype(jnp.bfloat16)
        return carry

    lax.fori_loop(0, tokens // 16, put_output, 0)
    two_copy.wait()
    gtwo_ref[...] += two_in[...]
    wait_all(row_copies)
    landed_ref[...] = landed[...]
    last_state.wait()
    for block in range(blocks - RING, blocks):
        seen_copy(block, block % RING).wait()
    wait_all(gated_copies)
    wait_all(hidden_copies)


def front(x_in, d_out, doc_start, pack, input_weight, w_x, w_dt, rates, w_out, w_gu, w_down, states):
    tokens, width = x_in.shape
    channels = w_x.shape[0]
    units = w_down.shape[0]
    rank = w_dt.shape[0]
    groups, span, unused = rates.shape
    count = lax.axis_size("seq")
    planes = count // PLANE
    share = width // count
    share_held = share + -share % 32
    vmem = pl.BlockSpec(memory_space=pltpu.VMEM)
    smem = pl.BlockSpec(memory_space=pltpu.SMEM)
    hbm = pl.BlockSpec(memory_space=pl.ANY)
    dma = pltpu.SemaphoreType.DMA
    chunks = width // WIDTH
    tiles = units // WIDTH
    near = 8 * (NEAR + 1)

    def fast(shape, kind=jnp.float32):
        return pltpu.VMEM(shape, kind)

    def low(*shape):
        return jax.ShapeDtypeStruct(shape, jnp.bfloat16)

    bf16 = jnp.bfloat16
    return pl.pallas_call(
        functools.partial(front_kernel, planes, rank, states, share),
        out_shape=(
            low(tokens, channels),
            f32(tokens, channels),
            f32(tokens, channels),
            f32(tokens, LANES),
            f32(tokens, LANES),
            f32(tokens, channels),
            f32(tokens, channels),
            f32(tokens, channels),
            low(tokens, channels),
            f32(tokens, width),
            f32(groups, 8, LANES),
            f32(tokens + 8, channels),
            low(tokens, units),
            low(2, tokens, units),
            f32(tokens, width),
            low(tokens, width),
            low(3, planes, share_held, PLANE * tokens),
            f32(groups, (tokens + 1) * span, LANES),
            low(PLANE - 1, tokens, channels + units),
        ),
        in_specs=[vmem, vmem, smem, vmem, vmem, hbm, vmem, vmem, vmem, hbm, hbm, hbm],
        out_specs=(vmem,) * 17 + (hbm, hbm),
        scratch_shapes=[
            fast((tokens, width), bf16),
            fast((tokens, width), bf16),
            fast((2 * tokens, 2 * width), bf16),
            fast((groups + 1, width, 2, WIDTH), bf16),
            fast((channels, width), bf16),
            fast((units, width), bf16),
            fast((tokens + 8, 1)),
            fast((16, channels), bf16),
            fast((16, channels), bf16),
            fast((tokens, channels), bf16),
            fast((tokens, LANES)),
            fast((tokens, LANES)),
            fast((LANES, channels), bf16),
            fast((span * (NEAR + 1), LANES)),
            fast((span * (NEAR + 1), LANES)),
            fast((groups, near, LANES)),
            fast((groups, near, LANES)),
            fast((groups, near, LANES)),
            fast((groups, span, LANES)),
            fast((groups, span, LANES)),
            fast((RING, groups, NEAR * span, LANES)),
            fast((chunks, tokens, WIDTH)),
            fast((chunks, tokens, WIDTH)),
            fast((3, PLANE, planes, share_held, tokens), bf16),
            fast((3, planes, share_held, PLANE * tokens), bf16),
            fast((tokens, units)),
            fast((tokens, units)),
            fast((2 * tokens, 2 * width)),
            fast((tokens, width)),
            fast((tokens, width)),
            fast((tokens, width)),
        ]
        + exchange_scratch(planes, groups, span)
        + [
            dma((groups + tiles + 2,)),
            dma((RING + 1,)),
            dma((2,)),
            dma((2,)),
            dma((2, chunks)),
            dma((3, PLANE)),
            dma((3, PLANE)),
            dma((2, PLANE)),
            dma((2, PLANE)),
            dma((4,)),
        ],
        compiler_params=params(collective_id=1, has_side_effects=True),
        name="front",
    )(
        x_in, d_out, doc_start, doc_start[None], pack, input_weight, w_x, w_dt, rates, w_out, w_gu, w_down,
    )


RING = 3
NEAR = 8


def near_rows(i, p=0):
    return pl.ds(i + p * 8 * (NEAR + 1), 8, stride=NEAR + 1)


def near_slot(slot):
    return pl.ds(slot * (NEAR + 1), NEAR)


def near_spread_rows(rows, first, states, target):
    for n in range(states):
        column = jnp.broadcast_to(rows[:, first + n : first + n + 1], (NEAR, LANES))
        for group in range(CG):
            target[near_slot(n * CG + group), :] = column


def near_spread_channels(value, target):
    for j in range(value.shape[1] // LANES):
        g, k = j // CG, j % CG
        piece = value[:, lanes(j, LANES)]
        target[g, near_slot(k), :] = piece
        target[g, near_slot(CG + k), :] = piece


def near_fold_channels(source, g, k):
    return source[g, near_slot(k), :] + source[g, near_slot(CG + k), :]


def near_fold_rows(source, states, first, out):
    lane = lax.broadcasted_iota(jnp.int32, out.shape, 1)
    for n in range(states):
        total = None
        for group in range(CG):
            part = source[near_slot(n * CG + group), :]
            total = part if total is None else total + part
        out = jnp.where(lane == first + n, jnp.sum(total, axis=1, keepdims=True), out)
    return out


def flip_bits(k, high, planes):
    out = 0
    step = 1
    while step < planes:
        out = out + lax.rem(lax.div(k, step) + lax.div(high, step), 2) * step
        step *= 2
    return out


def slot_place(k, planes):
    return k // 2 + (k % 2) * (planes // 2)


def rms_back(grad, value, gain):
    scale = lax.rsqrt(jnp.mean(value * value, axis=-1, keepdims=True) + EPSILON)
    scaled = value * scale
    pull = grad * gain
    inner = jnp.mean(pull * scaled, axis=-1, keepdims=True)
    return scale * (pull - scaled * inner), grad * scaled


def silu_and_slope(value):
    sigmoid = jax.nn.sigmoid(value)
    return value * sigmoid, sigmoid * (1.0 + value * (1.0 - sigmoid))


def sum8(value):
    total = value[:8]
    for i in range(1, value.shape[0] // 8):
        total = total + value[i * 8 : (i + 1) * 8]
    return total


def back_kernel(planes, rank, states, share, units,
                d_ref, resid_ref, proj_ref, rows_ref,
                gtwo_ref, landed_ref, sum_ref, starts_ref, start_row, pack_ref, wx_ref, wdt_ref, rate_ref,
                hidden_ref, ggu_ref, gated_ref, seen_ref, wout_ref, win_ref, xfront, x_far, conv_far, pre_far, inner_far,
                z_far, scanned_far, mixed_far, step_far,
                dx_ref, grads_ref, wx_out, wdt_out, vec_out, rate_out, xin, zr0,
                x_ref, conv_ref, pre_ref, inner_ref, z_ref, scanned_ref, mixed_ref, step_ref, wout, win, wide, seen, rows_out, rows_mix, xbuf, zbuf, zs0, zs_more, zr_more, acc,
                gtwo_in, gmix_low, gscan, z_low, gstep, gmix, gpad, keep_pad, inner_low, mixed_low, gpre_low, wdt, dyp, dyp_in,
                edge_out, edge_in, norm_in, spread_b, spread_c, near_step, near_push, near_grad, near_lb, near_rq,
                near_gb, near_gc, mus, ends, rate_grad, vec, flat, sent, got, part, zsent, zgot, full, first_out, first_got, first_mid, first_zgot,
                pay, egot, zpay, ezgot, back, final,
                send_a, recv_a, send_b, recv_b, send_c, recv_c,
                load_sem, seen_sem, x_send, x_recv, r_send, r_recv, z_send, z_recv, xbuf_sem, pair_sem, small_sem, save_sem, late_sem, first_sem):
    conv_w_ref, skip_ref = pack_ref, RowOf(pack_ref, 6)
    gain1_ref, gain2_ref, gains_ref = RowOf(pack_ref, 7), RowOf(pack_ref, 8), RowOf(pack_ref, 9, LANES)
    tokens, width = d_ref.shape
    channels = pack_ref.shape[1]
    groups = channels // WIDTH
    chunks = width // WIDTH
    span = states * CG
    pairs = states // 2
    steps_z = planes.bit_length() - 1
    half = planes // 2
    places = Places(planes)
    low, high = places.low, places.high
    greeted = places.greet()
    blocks = tokens // NEAR

    late = [
        pltpu.make_async_copy(far, near, late_sem.at[i])
        for i, (far, near) in enumerate(
            (
                (z_far, z_ref),
                (scanned_far, scanned_ref),
                (mixed_far, mixed_ref),
                (step_far, step_ref),
                (conv_far, conv_ref),
                (pre_far, pre_ref),
                (inner_far, inner_ref),
                (x_far, x_ref),
            )
        )
    ]
    def wout_copy(j):
        rows = pl.ds(j * WIDTH, WIDTH)
        return pltpu.make_async_copy(wout_ref.at[rows, :], wout.at[j % 2], load_sem.at[2 + j % 2])

    wout_copy(0).start()
    wout_copy(1).start()

    def seen_copy(block, slot):
        at = pl.ds(pl.multiple_of(block * (NEAR * span), 8), (NEAR + 1) * span)
        return pltpu.make_async_copy(seen_ref.at[:, at, :], seen.at[slot], seen_sem.at[slot])

    for k in range(RING - 1):
        seen_copy(blocks - 1 - k, k).start()

    def win_copy(j):
        return pltpu.make_async_copy(win_ref.at[:, :, pl.ds(j * WIDTH, WIDTH)], win.at[j % 2], load_sem.at[j % 2])

    for load in late:
        load.start()
    win_copy(0).start()
    win_copy(1).start()

    greeted()
    sender = Rows(places, share, rows_out, rows_mix, r_send, r_recv)
    row_copies = {}

    HIDDEN, GATE, UP, GATED, Z, INNER = range(6)
    unit_copies = {}
    offsets, at = [], 0
    for unit_width, unused in units:
        offsets.append(at)
        at += unit_width

    def unit_source(u):
        return (hidden_ref, ggu_ref.at[0], ggu_ref.at[1], gated_ref, z_low, inner_low)[u]

    ring_width = max(unit_width for unit_width, unused in units)
    turn = (0, 2, 3, 1, 4, 5)

    def unit_columns(u):
        return pl.ds(offsets[u], units[u][0])

    def ring_columns(u):
        return pl.ds(turn[u] % 2 * ring_width, units[u][0])

    def columns_of(u, j):
        return pl.ds(pl.multiple_of(offsets[u] + j * WIDTH, WIDTH), WIDTH)

    def ring_of(u, j):
        return pl.ds(pl.multiple_of(turn[u] % 2 * ring_width + j * WIDTH, WIDTH), WIDTH)

    def first_slot(step):
        return sum(planes // 2 ** (k + 1) for k in range(1, step))

    landed_at = {3: 0, 0: units[3][0]}

    def send_unit(u):
        unit_copies[u] = send_columns(places, unit_source(u), xin, offsets[u], units[u][0], x_send.at[u], x_recv.at[u])

    def relay_landed(u):
        start, size = landed_at[u], units[u][0] // 2
        unit_copies[u] = [
            copy_to(
                xfront.at[mask - 1, :, pl.ds(start + at, size)],
                xin.at[PLANE - 2, :, pl.ds(offsets[u] + at, size)],
                x_send.at[u, mask],
                x_recv.at[u, mask],
                places.mirrored(3 - mask),
            )
            for mask, at in ((1, 0), (2, size))
        ]

    def relay(u):
        wait_all(unit_copies[u])
        unit_copies[u] = relay_columns(places, xin, offsets[u], units[u][0], x_send.at[u], x_recv.at[u])

    def partner(step):
        size = 2**step
        bit = lax.rem(lax.div(high, size), 2)
        return {"seq": (high + (1 - 2 * bit) * size) * PLANE + low}

    z_copies = {}

    def load_chunk(u, j, slot, with_z):
        local = pl.ds(pl.multiple_of(j * WIDTH, WIDTH), WIDTH)
        whole = columns_of(u, j)
        copies = [
            pltpu.make_async_copy(unit_source(u).at[:, local], xbuf.at[slot, pl.ds(0, tokens), :], xbuf_sem.at[slot, 0])
        ]
        for shift in range(1, PLANE):
            if u == GATED or u == HIDDEN and shift < PLANE - 1:
                arrived = xfront.at[shift - 1, :, pl.ds(pl.multiple_of(landed_at[u] + j * WIDTH, WIDTH), WIDTH)]
            else:
                arrived = xin.at[shift - 1, :, whole]
            copies.append(
                pltpu.make_async_copy(
                    arrived, xbuf.at[slot, pl.ds(shift * tokens, tokens), :], xbuf_sem.at[slot, shift]
                )
            )
        if with_z:
            copies.append(pltpu.make_async_copy(zr0.at[:, :, whole], zbuf.at[slot], xbuf_sem.at[slot, PLANE]))
        return copies

    def over_chunks(u, with_z, use):
        count = units[u][0] // WIDTH
        for copy in load_chunk(u, 0, 0, with_z):
            copy.start()

        def body(j, carry):
            slot = lax.rem(j, 2)

            @pl.when(j + 1 < count)
            def _():
                for copy in load_chunk(u, j + 1, 1 - slot, with_z):
                    copy.start()

            for copy in load_chunk(u, j, slot, with_z):
                copy.wait()
            use(slot, j)
            return carry

        lax.fori_loop(0, count, body, 0)

    def product(u, slot, first):
        which = units[u][1]
        rows = rows_mix[0, first : first + half] if which == 3 else landed_ref[which, first : first + half]
        left = rows.reshape(half * rows_mix.shape[2], PLANE * tokens)
        return jnp.dot(left, xbuf[slot], preferred_element_type=jnp.float32).reshape(half, rows_mix.shape[2], WIDTH)

    def stage_one(u):
        if u != GATED:
            wait_all(unit_copies[u])
        which = units[u][1]
        if which in row_copies:
            wait_all(row_copies.pop(which))

        def use(slot, j):
            zs0[:, :, ring_of(u, j)] = product(u, slot, half).astype(jnp.bfloat16)

        over_chunks(u, False, use)
        z_copies[u] = copy_to(zs0.at[:, :, ring_columns(u)], zr0.at[:, :, unit_columns(u)], z_send.at[u, 0], z_recv.at[u, 0], partner(0))

    def split(u, step, value, j):
        count = value.shape[0]
        columns = ring_of(u, j)
        if count == 1:
            acc[0, :, columns] = value[0]
            return
        for i in range(count // 2):
            acc[i, :, columns] = value[2 * i]
            zs_more[first_slot(step) + i, :, columns] = value[2 * i + 1].astype(jnp.bfloat16)

    def send_more(u, step):
        slots = pl.ds(first_slot(step), planes // 2 ** (step + 1))
        z_copies[u] = copy_to(
            zs_more.at[slots, :, ring_columns(u)],
            zr_more.at[slots, :, unit_columns(u)],
            z_send.at[u, step],
            z_recv.at[u, step],
            partner(step),
        )

    def stage_two(u):
        z_copies.pop(u).wait()
        for other in list(saves):
            if turn[other] % 2 == turn[u] % 2:
                saves.pop(other).wait()

        def use(slot, j):
            split(u, 1, product(u, slot, 0) + zbuf[slot].astype(jnp.float32), j)

        over_chunks(u, True, use)
        if steps_z > 1:
            send_more(u, 1)

    saves = {}

    def stage_three(u):
        count_chunks = units[u][0] // WIDTH
        for step in range(2, steps_z + 1):
            z_copies.pop(u).wait()
            count = planes // 2**step

            def body(j, carry):
                first = first_slot(step - 1)
                value = acc[:count, :, ring_of(u, j)] + zr_more[first : first + count, :, columns_of(u, j)].astype(jnp.float32)
                split(u, step, value, j)
                return carry

            lax.fori_loop(0, count_chunks, body, 0)
            if count > 1:
                send_more(u, step)
        save = pltpu.make_async_copy(acc.at[0, :, ring_columns(u)], grads_ref.at[:, unit_columns(u)], save_sem.at[u])
        save.start()
        saves[u] = save

    relay_landed(HIDDEN)
    send_unit(GATE)
    stage_one(HIDDEN)
    keep_pad[:8, :] = jnp.ones((8, 1), jnp.float32)
    keep_pad[8 : 8 + tokens, :] = as_column((1 - start_row[...]).astype(jnp.float32))
    keep_pad[8 + tokens :, :] = jnp.ones((8, 1), jnp.float32)
    wdt[:rank, :] = wdt_ref[...]
    wdt[rank:, :] = jnp.zeros((LANES - rank, channels), jnp.bfloat16)
    vec[...] = jnp.zeros_like(vec)
    rate_grad[...] = jnp.zeros_like(rate_grad)


    def mid(block, carry):
        rows = block16(block)
        grad = gtwo_ref[rows, :]
        back_to, gain_part = rms_back(grad, resid_ref[rows, :], gain2_ref[...])
        value = d_ref[rows, :].astype(jnp.float32) + back_to
        dx_ref[rows, :] = value
        gmix_low[rows, :] = value.astype(jnp.bfloat16)
        return carry + sum8(gain_part)

    norm2 = lax.fori_loop(0, tokens // 16, mid, jnp.zeros((8, width), jnp.float32))
    vec[8:9, :] = jnp.sum(norm2, axis=0, keepdims=True)
    sender.put(lambda cols: dx_ref[:, cols], width, 0)
    row_copies[3] = sender.send(0)

    for j in range(groups):
        wout_copy(j).wait()
        gscan[:, lanes(j)] = lax.dot_general(
            gmix_low[...], wout[j % 2], (((1,), (1,)), ((), ())), preferred_element_type=jnp.float32
        )
        if j + 2 < groups:
            wout_copy(j + 2).start()

    for load in late[:4]:
        load.wait()
    relay(GATE)
    def gate(block, carry):
        rows = block16(block)
        out = []
        for j in range(groups):
            cols = lanes(j)
            act, slope = silu_and_slope(z_ref[rows, cols].astype(jnp.float32))
            grad = gscan[rows, cols]
            grad_scanned = grad * act
            gscan[rows, cols] = grad_scanned
            z_low[rows, cols] = (grad * scanned_ref[rows, cols] * slope).astype(jnp.bfloat16)
            mixed = mixed_ref[rows, cols]
            mixed_low[rows, cols] = mixed.astype(jnp.bfloat16)
            out.append(carry[j] + sum8(grad_scanned * mixed))
        return tuple(out)

    skips = lax.fori_loop(0, tokens // 16, gate, (jnp.zeros((8, WIDTH), jnp.float32),) * groups)
    for j in range(groups):
        vec[6:7, lanes(j)] = jnp.sum(skips[j], axis=0, keepdims=True)

    def keep_of(t):
        return (1 - starts_ref[t]).astype(jnp.float32)

    def near_block(block):
        return pl.ds(pl.multiple_of(block * NEAR, NEAR), NEAR)

    def rate_of(g, p):
        return rate_ref[g, p * 8 : p * 8 + 8, :]

    mus[...] = jnp.zeros_like(mus)

    def feed(k, carry):
        block = blocks - 1 - k
        at = near_block(block)
        near_spread_rows(rows_ref[at, :], rank + states, states, spread_c)
        near_spread_channels(step_ref[at, :], near_step)
        near_spread_channels(gscan[at, :], near_grad)
        for g in range(groups):
            held = [mus[g, p * 8 : p * 8 + 8, :] for p in range(pairs)]
            for i in range(NEAR - 1, -1, -1):
                size = near_step[g, near_rows(i), :]
                grad = near_grad[g, near_rows(i), :]
                keep = keep_of(block * NEAR + i)
                for p in range(pairs):
                    lam = held[p] + spread_c[near_rows(i, p), :] * grad
                    held[p] = jnp.exp2(size * rate_of(g, p)) * (lam * keep)
            for p in range(pairs):
                mus[g, p * 8 : p * 8 + 8, :] = held[p]
        return carry

    lax.fori_loop(0, blocks, feed, 0)
    ends[...] = mus[...]
    exchange_states(places, True, ends, sum_ref, rate_ref, pay, egot, zpay, ezgot, back, final,
                    (send_a, recv_a, send_b, recv_b, send_c, recv_c))
    per = pairs // PLANE
    for g in range(groups):
        for p in range(pairs):
            mus[g, p * 8 : p * 8 + 8, :] = final[p // per, g, (p % per) * 8 : (p % per) * 8 + 8, :]
    stage_one(GATED)
    send_unit(UP)
    stage_two(HIDDEN)
    stage_one(GATE)

    def scan(k, carry):
        block = blocks - 1 - k
        at = near_block(block)
        slot = lax.rem(k, RING)

        @pl.when(k + RING - 1 < blocks)
        def _():
            seen_copy(block - (RING - 1), lax.rem(k + RING - 1, RING)).start()

        near_spread_rows(rows_ref[at, :], rank, states, spread_b)
        near_spread_rows(rows_ref[at, :], rank + states, states, spread_c)
        near_spread_channels(step_ref[at, :], near_step)
        near_spread_channels(step_ref[at, :] * mixed_ref[at, :], near_push)
        near_spread_channels(gscan[at, :], near_grad)
        seen_copy(block, slot).wait()
        held = [[mus[g, p * 8 : p * 8 + 8, :] for p in range(pairs)] for g in range(groups)]
        for i in range(NEAR - 1, -1, -1):
            keep = keep_of(block * NEAR + i)
            sizes = [near_step[g, near_rows(i), :] for g in range(groups)]
            pushes = [near_push[g, near_rows(i), :] for g in range(groups)]
            grads = [near_grad[g, near_rows(i), :] for g in range(groups)]
            lbs, rqs = [None] * groups, [None] * groups
            for p in range(pairs):
                b_value = spread_b[near_rows(i, p), :]
                c_value = spread_c[near_rows(i, p), :]
                gb = gc = None
                for g in range(groups):
                    rate = rate_of(g, p)
                    before = seen[slot, g, i * span + p * 8 : i * span + p * 8 + 8, :]
                    now = seen[slot, g, (i + 1) * span + p * 8 : (i + 1) * span + p * 8 + 8, :]
                    lam = held[g][p] + c_value * grads[g]
                    mu = jnp.exp2(sizes[g] * rate) * (lam * keep)
                    held[g][p] = mu
                    q = mu * before
                    rate_grad[g, p * 8 : p * 8 + 8, :] += q * sizes[g]
                    lb, rq = lam * b_value, q * rate
                    lbs[g] = lb if lbs[g] is None else lbs[g] + lb
                    rqs[g] = rq if rqs[g] is None else rqs[g] + rq
                    gb_term, gc_term = lam * pushes[g], now * grads[g]
                    gb = gb_term if gb is None else gb + gb_term
                    gc = gc_term if gc is None else gc + gc_term
                near_gb[near_rows(i, p), :] = gb
                near_gc[near_rows(i, p), :] = gc
            for g in range(groups):
                near_lb[g, near_rows(i), :] = lbs[g]
                near_rq[g, near_rows(i), :] = rqs[g]
        for g in range(groups):
            for p in range(pairs):
                mus[g, p * 8 : p * 8 + 8, :] = held[g][p]
        for j in range(channels // LANES):
            g, k_group = j // CG, j % CG
            cols = lanes(j, LANES)
            lb = near_fold_channels(near_lb, g, k_group)
            rq = near_fold_channels(near_rq, g, k_group)
            gmix[at, cols] = step_ref[at, cols] * lb
            gstep[at, cols] = mixed_ref[at, cols] * lb + LN2 * rq
        row = jnp.zeros((NEAR, LANES), jnp.float32)
        row = near_fold_rows(near_gb, states, rank, row)
        dyp[at, :] = near_fold_rows(near_gc, states, rank + states, row)
        return carry

    lax.fori_loop(0, blocks // 2, scan, 0)
    relay(UP)
    send_unit(Z)
    lax.fori_loop(blocks // 2, blocks, scan, 0)
    stage_two(GATED)

    for load in late[4:]:
        load.wait()

    def pre_grad(block, carry):
        rows = block16(block)
        out = []
        for j in range(groups):
            grad = gstep[rows, lanes(j)] * jax.nn.sigmoid(pre_ref[rows, lanes(j)])
            gpre_low[rows, lanes(j)] = grad.astype(jnp.bfloat16)
            out.append(carry[j] + sum8(grad))
        return tuple(out)

    biases = lax.fori_loop(0, tokens // 16, pre_grad, (jnp.zeros((8, WIDTH), jnp.float32),) * groups)
    for j in range(groups):
        vec[5:6, lanes(j)] = jnp.sum(biases[j], axis=0, keepdims=True)
    dyp[...] += lax.dot_general(gpre_low[...], wdt[...], (((1,), (1,)), ((), ())), preferred_element_type=jnp.float32)
    dyp_copy = copy_to(dyp, dyp_in, pair_sem.at[2], pair_sem.at[3], places.other())
    turned = jnp.transpose(rows_ref[...]).astype(jnp.bfloat16)
    at_flat = channels // LANES * LANES
    for j in range(channels // LANES):
        value = jnp.dot(turned[:rank], gpre_low[:, lanes(j, LANES)], preferred_element_type=jnp.float32)
        flat[at_flat + j * rank : at_flat + (j + 1) * rank, :] = value
    relay(Z)
    dyp_copy.wait()
    projected = proj_ref[...]
    scale = lax.rsqrt(third_means(projected * projected, rank, states) + EPSILON)
    scaled = projected * scale
    grad = dyp[...] + dyp_in[...]
    pull = grad * gains_ref[...]
    proj_grad = scale * (pull - scaled * third_means(pull * scaled, rank, states))
    vec[9:10, :LANES] = jnp.sum(sum8(grad * scaled), axis=0, keepdims=True)
    proj_low = proj_grad.astype(jnp.bfloat16)
    turned_proj = jnp.transpose(proj_grad).astype(jnp.bfloat16)

    for j in range(groups):
        gmix[:, lanes(j)] += lax.dot_general(
            proj_low, wx_ref[lanes(j), :], (((1,), (1,)), ((), ())), preferred_element_type=jnp.float32
        )
    gpad[:8, :] = jnp.zeros((8, channels), jnp.float32)
    gpad[8 + tokens :, :] = jnp.zeros((8, channels), jnp.float32)

    def conv_grad(block, carry):
        rows = block16(block)
        to = pl.ds(pl.multiple_of(block * 16 + 8, 8), 16)
        near = pl.ds(pl.multiple_of(block * 16, 8), 24)
        keeps = keep_pad[near, :]
        keep = keeps[8:]
        two = keep * keeps[7:23]
        three = two * keeps[6:22]
        out = []
        for j in range(groups):
            cols = lanes(j)
            unused, slope = silu_and_slope(conv_ref[rows, cols])
            grad = (gmix[rows, cols] + skip_ref[:, cols] * gscan[rows, cols]) * slope
            gpad[to, cols] = grad
            values = inner_ref[near, cols]
            sums = [carry[j][4] + sum8(grad), carry[j][3] + sum8(grad * values[8:])]
            for offset, mask in ((1, keep), (2, two), (3, three)):
                sums.append(carry[j][3 - offset] + sum8(grad * values[8 - offset : 24 - offset] * mask))
            out.append((sums[4], sums[3], sums[2], sums[1], sums[0]))
        return tuple(out)

    empty = jnp.zeros((8, WIDTH), jnp.float32)
    taps = lax.fori_loop(0, tokens // 16, conv_grad, ((empty,) * 5,) * groups)
    for j in range(groups):
        for i in range(5):
            vec[i : i + 1, lanes(j)] = jnp.sum(taps[j][i], axis=0, keepdims=True)

    def taps_back(start, count, columns):
        near = pl.ds(pl.multiple_of(start, 8), count + 8)
        keeps = keep_pad[near, :]
        grads = gpad[near, columns]
        total = conv_w_ref[3:4, columns] * grads[:count]
        mask = None
        for offset in (1, 2, 3):
            mask = keeps[1 : count + 1] if mask is None else mask * keeps[offset : count + offset]
            total += conv_w_ref[3 - offset : 4 - offset, columns] * grads[offset : count + offset] * mask
        return total

    for j in range(groups):
        edge_out[:, lanes(j)] = taps_back(0, 8, lanes(j))
    edge_copy = copy_to(edge_out, edge_in, pair_sem.at[4], pair_sem.at[5], places.along(-1))

    def inner_grad(block, carry):
        rows = block16(block)
        for j in range(groups):
            inner_low[rows, lanes(j)] = taps_back(block * 16 + 8, 16, lanes(j)).astype(jnp.bfloat16)
        return carry

    lax.fori_loop(0, tokens // 16 - 1, inner_grad, 0)
    last_keep, before_keep = keep_of(tokens - 1), keep_of(tokens - 2)
    row = lax.broadcasted_iota(jnp.int32, (16, 1), 0)
    tail = jnp.where(
        row == 15, 1.0, jnp.where(row == 14, last_keep, jnp.where(row == 13, last_keep * before_keep, 0.0))
    )
    tail = jnp.where(places.me == places.count - 1, 0.0, tail)
    edge_copy.wait()
    for j in range(groups):
        here = taps_back(tokens - 8, 16, lanes(j))
        edge = jnp.concatenate([jnp.zeros((8, WIDTH), jnp.float32), edge_in[:, lanes(j)]], 0) * tail
        inner_low[tokens - 16 :, lanes(j)] = (here + edge).astype(jnp.bfloat16)
    send_unit(INNER)
    stage_one(UP)
    stage_three(HIDDEN)

    for j in range(channels // LANES):
        flat[j * LANES : (j + 1) * LANES, :] = jnp.dot(
            turned_proj, mixed_low[:, lanes(j, LANES)], preferred_element_type=jnp.float32
        )
    rows_flat = flat.shape[0]
    quarter = rows_flat // PLANE
    chunk = quarter // planes
    at_vec = at_flat + channels // LANES * rank
    for j in range(channels // LANES):
        flat[at_vec + j * 16 : at_vec + (j + 1) * 16, :] = vec[:, lanes(j, LANES)]
    at_rate = at_vec + channels // LANES * 16
    for g in range(groups):
        flat[at_rate + g * span : at_rate + (g + 1) * span, :] = -rate_grad[g]
    at_end = at_rate + groups * span
    if at_end < rows_flat:
        flat[at_end:, :] = jnp.zeros((rows_flat - at_end, LANES), jnp.float32)
    sent[...] = flat[...].astype(jnp.bfloat16)

    def quarter_at(index):
        return pl.ds(pl.multiple_of(index * quarter, 16), quarter)

    def chunk_at(index):
        return pl.ds(pl.multiple_of(index * chunk, 16), chunk)

    small_copies = [
        copy_to(sent.at[quarter_at(lax.rem(low + shift, PLANE))], got.at[shift], small_sem.at[0, shift], small_sem.at[1, shift],
                places.in_plane(shift))
        for shift in range(1, PLANE)
    ]
    part[...] = flat[quarter_at(low), :]
    stage_two(GATE)
    stage_one(Z)
    stage_three(GATED)

    for j in range(groups):
        win_copy(j).wait()
        both = lax.dot_general(
            jnp.concatenate([inner_low[:, lanes(j)], z_low[:, lanes(j)]], 0),
            win[j % 2].reshape(2 * width, WIDTH),
            (((1,), (1,)), ((), ())),
            preferred_element_type=jnp.float32,
        )
        if j == 0:
            wide[...] = both
        else:
            wide[...] += both
        if j + 2 < groups:
            win_copy(j + 2).start()
    narrow(wide, gtwo_in)
    norm_copy = copy_to(gtwo_in, norm_in, pair_sem.at[6], pair_sem.at[7], places.other())
    relay(INNER)
    stage_two(UP)
    stage_one(INNER)
    wait_all(small_copies)
    for shift in range(1, PLANE):
        part[...] += got[shift].astype(jnp.float32)
    zsent[...] = part[...].astype(jnp.bfloat16)
    small_copies = [
        copy_to(zsent.at[chunk_at(lax.rem(high + shift, planes))], zgot.at[shift], small_sem.at[2, shift], small_sem.at[3, shift],
                places.across(shift))
        for shift in range(1, planes)
    ]
    norm_copy.wait()

    def first_norm(block, carry):
        rows = block16(block)
        grad = gtwo_in[rows, :] + norm_in[rows, :]
        back_to, gain_part = rms_back(grad, x_ref[rows, :].astype(jnp.float32), gain1_ref[...])
        dx_ref[rows, :] += back_to
        return carry + sum8(gain_part)

    norm1 = jnp.sum(lax.fori_loop(0, tokens // 16, first_norm, jnp.zeros((8, width), jnp.float32)), axis=0, keepdims=True)
    first_out[...] = jnp.concatenate([norm1[:, lanes(j, LANES)] for j in range(width // LANES)], 0)
    first_copies = [
        copy_to(first_out, first_got.at[shift], first_sem.at[0, shift], first_sem.at[1, shift], places.in_plane(shift))
        for shift in range(1, PLANE)
    ]
    stage_three(GATE)
    stage_two(Z)
    wait_all(small_copies)
    total = part[chunk_at(high), :]
    for shift in range(1, planes):
        total += zgot[shift].astype(jnp.float32)
    mine = pl.ds(pl.multiple_of(low * quarter + high * chunk, 16), chunk)
    full[mine, :] = total.astype(jnp.bfloat16)
    small_copies = [
        copy_to(full.at[mine], full.at[mine], small_sem.at[4, shift], small_sem.at[5, shift], places.across(shift))
        for shift in range(1, planes)
    ]
    wait_all(first_copies)
    first_sum = first_out[...]
    for shift in range(1, PLANE):
        first_sum += first_got[shift]
    first_mid[...] = first_sum
    first_copies = [
        copy_to(first_mid, first_zgot.at[shift], first_sem.at[2, shift], first_sem.at[3, shift], places.across(shift))
        for shift in range(1, planes)
    ]
    stage_three(UP)
    stage_two(INNER)
    wait_all(small_copies)
    small_copies = [
        copy_to(full.at[quarter_at(low)], full.at[quarter_at(low)], small_sem.at[6, shift], small_sem.at[7, shift],
                places.in_plane(shift))
        for shift in range(1, PLANE)
    ]
    wait_all(small_copies)
    for j in range(channels // LANES):
        wx_out[:, lanes(j, LANES)] = full[j * LANES : (j + 1) * LANES, :].astype(jnp.float32)
        wdt_out[:, lanes(j, LANES)] = full[at_flat + j * rank : at_flat + (j + 1) * rank, :].astype(jnp.float32)
        vec_out[:, lanes(j, LANES)] = full[at_vec + j * 16 : at_vec + (j + 1) * 16, :].astype(jnp.float32)
    for g in range(groups):
        rate_out[g] = full[at_rate + g * span : at_rate + (g + 1) * span, :].astype(jnp.float32)
    wait_all(first_copies)
    first_sum = first_mid[...]
    for shift in range(1, planes):
        first_sum += first_zgot[shift]
    for j in range(width // LANES):
        vec_out[7:8, lanes(j, LANES)] = first_sum[j : j + 1]
    stage_three(Z)
    stage_three(INNER)
    wait_all(saves.values())


def mixer_back(d_out, x_in, kept, far, gtwo, hidden, ggu, doc_start, pack, w_x, w_dt, rates,
               w_out, input_weight, states, gated, seen, sums, landed, xfront):
    tokens, width = x_in.shape
    channels = w_x.shape[0]
    unit_ff = hidden.shape[1]
    rank = w_dt.shape[0]
    groups, span, unused = rates.shape
    count = lax.axis_size("seq")
    planes = count // PLANE
    share = width // count
    held = share + -share % 32
    units = ((unit_ff, 0), (unit_ff, 2), (unit_ff, 2), (channels, 3), (channels, 1), (channels, 1))
    columns = sum(u for u, unused in units)
    vmem = pl.BlockSpec(memory_space=pltpu.VMEM)
    smem = pl.BlockSpec(memory_space=pltpu.SMEM)
    hbm = pl.BlockSpec(memory_space=pl.ANY)
    dma = pltpu.SemaphoreType.DMA
    bf16 = jnp.bfloat16
    half = planes // 2
    ring = 2 * max(u for u, unused in units)
    more = max(planes // 4, 1)
    steps_z = planes.bit_length() - 1
    rows = channels + channels // LANES * (rank + 16) + groups * span
    rows += -rows % (16 * count)
    near = 8 * (NEAR + 1)

    def fast(shape, kind=jnp.float32):
        return pltpu.VMEM(shape, kind)

    return pl.pallas_call(
        functools.partial(back_kernel, planes, rank, states, share, units),
        out_shape=(
            f32(tokens, width),
            f32(held, columns),
            f32(LANES, channels),
            f32(rank, channels),
            f32(16, channels),
            f32(groups, span, LANES),
            jax.ShapeDtypeStruct((PLANE - 1, tokens, columns), bf16),
            jax.ShapeDtypeStruct((half, held, columns), bf16),
        ),
        in_specs=[vmem] * 7 + [smem] + [vmem] * 5 + [hbm] * 15,
        out_specs=(vmem, hbm, vmem, vmem, vmem, vmem, hbm, hbm),
        scratch_shapes=[
            fast((tokens, width), bf16),
            fast((tokens, channels)),
            fast((tokens, channels)),
            fast((tokens + 8, channels)),
            fast((tokens, channels), bf16),
            fast((tokens, channels)),
            fast((tokens, channels)),
            fast((tokens, channels)),
            fast((2, WIDTH, width), bf16),
            fast((2, width, 2, WIDTH), bf16),
            fast((2 * tokens, 2 * width)),
            fast((RING, groups, (NEAR + 1) * span, LANES)),
            fast((1, PLANE, planes, held, tokens), bf16),
            fast((1, planes, held, PLANE * tokens), bf16),
            fast((2, PLANE * tokens, WIDTH), bf16),
            fast((2, half, held, WIDTH), bf16),
            fast((half, held, ring), bf16),
            fast((max(half - 1, 1), held, ring), bf16),
            fast((max(half - 1, 1), held, columns), bf16),
            fast((more, held, ring)),
            fast((tokens, width)),
            fast((tokens, width), bf16),
            fast((tokens, channels)),
            fast((tokens, channels), bf16),
            fast((tokens, channels)),
            fast((tokens, channels)),
            fast((tokens + 16, channels)),
            fast((tokens + 16, 1)),
            fast((tokens, channels), bf16),
            fast((tokens, channels), bf16),
            fast((tokens, channels), bf16),
            fast((LANES, channels), bf16),
            fast((tokens, LANES)),
            fast((tokens, LANES)),
            fast((8, channels)),
            fast((8, channels)),
            fast((tokens, width)),
            fast((span * (NEAR + 1), LANES)),
            fast((span * (NEAR + 1), LANES)),
            fast((groups, near, LANES)),
            fast((groups, near, LANES)),
            fast((groups, near, LANES)),
            fast((groups, near, LANES)),
            fast((groups, near, LANES)),
            fast((span * (NEAR + 1), LANES)),
            fast((span * (NEAR + 1), LANES)),
            fast((groups, span, LANES)),
            fast((groups, span, LANES)),
            fast((groups, span, LANES)),
            fast((16, channels)),
            fast((rows, LANES)),
            fast((rows, LANES), bf16),
            fast((PLANE, rows // PLANE, LANES), bf16),
            fast((rows // PLANE, LANES)),
            fast((rows // PLANE, LANES), bf16),
            fast((planes, rows // count, LANES), bf16),
            fast((rows, LANES), bf16),
            fast((width // LANES, LANES)),
            fast((PLANE, width // LANES, LANES)),
            fast((width // LANES, LANES)),
            fast((planes, width // LANES, LANES)),
        ]
        + exchange_scratch(planes, groups, span)
        + [
            dma((4,)),
            dma((RING,)),
            dma((6, PLANE)),
            dma((6, PLANE)),
            dma((1, PLANE)),
            dma((1, PLANE)),
            dma((6, steps_z)),
            dma((6, steps_z)),
            dma((2, PLANE + 1)),
            dma((8,)),
            dma((8, max(PLANE, planes))),
            dma((6,)),
            dma((8,)),
            dma((4, max(PLANE, planes))),
        ],
        compiler_params=params(collective_id=2, has_side_effects=True),
        name="mixer_back",
    )(
        d_out, *kept, gtwo, landed, sums, doc_start, doc_start[None], pack, w_x, w_dt, rates, hidden, ggu, gated, seen, w_out, input_weight, xfront, x_in, *far,
    )


def finish_kernel(units, channels, output_ref, dx_ref, grads_ref, wx_ref, wdt_ref,
                  output_out, dx_out, in_out, gu_out, out_out, down_out, x_out, dt_out):
    first = 3 * units
    rows = out_out.shape[0]
    gu_out[:, 0, :] = grads_ref[:rows, units : 2 * units]
    gu_out[:, 1, :] = grads_ref[:rows, 2 * units : first]
    in_out[:, 0, :] = grads_ref[:rows, first + 2 * channels : first + 3 * channels]
    in_out[:, 1, :] = grads_ref[:rows, first + channels : first + 2 * channels]
    down_out[...] = grads_ref[:rows, :units]
    out_out[...] = grads_ref[:rows, first : first + channels]
    output_out[...] = output_ref[...]
    dx_out[...] = dx_ref[...]
    dt_out[...] = wdt_ref[...]
    for block in range(wx_ref.shape[1] // LANES):
        x_out[lanes(block, LANES), :] = jnp.transpose(wx_ref[:, lanes(block, LANES)])


def finish(output, d_x, grads, wx_sum, wdt_sum, units, channels, share):
    tokens, width = d_x.shape
    rank = wdt_sum.shape[0]
    parts = 4 if share % 32 == 0 else 1

    def by_rows(rows, columns):
        return pl.BlockSpec((rows // parts, columns), lambda i: (i, 0))

    def by_pairs(rows, columns):
        return pl.BlockSpec((rows // parts, 2, columns), lambda i: (i, 0, 0))

    held = grads.shape[0]
    return pl.pallas_call(
        functools.partial(finish_kernel, units, channels),
        grid=(parts,),
        out_shape=(
            jax.ShapeDtypeStruct((tokens, width), jnp.bfloat16),
            f32(tokens, width),
            f32(share, 2, channels),
            f32(share, 2, units),
            f32(share, channels),
            f32(share, units),
            f32(channels, LANES),
            f32(rank, channels),
        ),
        in_specs=[
            by_rows(tokens, width),
            by_rows(tokens, width),
            by_rows(held, grads.shape[1]),
            pl.BlockSpec((LANES, channels // parts), lambda i: (0, i)),
            by_rows(rank, channels),
        ],
        out_specs=(
            by_rows(tokens, width),
            by_rows(tokens, width),
            by_pairs(share, channels),
            by_pairs(share, units),
            by_rows(share, channels),
            by_rows(share, units),
            by_rows(channels, LANES),
            by_rows(rank, channels),
        ),
        compiler_params=params(),
        name="finish",
    )(output, d_x, grads, wx_sum, wdt_sum)


def local(
    x_in,
    doc_start,
    norm1_gain,
    input_weight,
    conv_w,
    conv_b,
    w_x,
    dt_gain,
    b_gain,
    c_gain,
    w_dt,
    dt_bias,
    state_rate,
    skip,
    w_out,
    norm2_gain,
    w_gu,
    w_down,
    d_out,
):
    states = b_gain.shape[0]
    rank = dt_gain.shape[0]
    channels = conv_b.shape[0]
    rates = rates_in(state_rate)
    gains = jnp.concatenate([dt_gain, b_gain, c_gain])
    pack = jnp.concatenate(
        [
            conv_w,
            conv_b[None],
            dt_bias[None],
            skip[None],
            norm1_gain[None],
            norm2_gain[None],
            jnp.pad(gains, (0, channels - gains.shape[0]))[None],
        ],
        0,
    )
    (
        z_low, conv_out, mixed, projected, rows, steps, pre, scanned, gated, resid_mid, sums, padded, hidden, grad_gu, grad_two,
        output, landed, seen, gathered,
    ) = front(x_in, d_out, doc_start, pack, input_weight, w_x, w_dt, rates, w_out, w_gu, w_down, states)
    kept = (resid_mid, projected, rows)
    d_x, grads, wx_sum, wdt_sum, vectors, rate_sum, unused_x, unused_z = mixer_back(
        d_out, x_in, kept, (conv_out, pre, padded, z_low, scanned, mixed, steps), grad_two, hidden, grad_gu, doc_start, pack, w_x, w_dt, rates,
        w_out, input_weight, states, gated, seen, sums, landed, gathered,
    )
    count = lax.axis_size("seq")
    share = x_in.shape[1] // count
    units = hidden.shape[1]

    def own(row):
        return lax.dynamic_slice(vectors[row], (lax.axis_index("seq") * share,), (share,))

    output, d_x, g_in, g_gu, g_out, g_down, g_x, g_dt = finish(output, d_x, grads, wx_sum, wdt_sum, units, channels, share)
    gain_row = vectors[9]
    return (
        output,
        d_x,
        own(7),
        g_in,
        vectors[:4],
        vectors[4],
        g_x,
        gain_row[:rank],
        gain_row[rank : rank + states],
        gain_row[rank + states : rank + 2 * states],
        g_dt,
        vectors[5],
        rates_out(rate_sum),
        vectors[6],
        g_out.T,
        own(8),
        g_gu,
        g_down.T,
    )


def solution(mesh):
    placed = (
        P("seq", None),
        P("seq"),
        P(),
        P(None, None, "head"),
        P(None, "head"),
        P("head"),
        P("head", None),
        P(),
        P(),
        P(),
        P(None, "head"),
        P("head"),
        P("head", None),
        P("head"),
        P("head", None),
        P(),
        P(None, None, "head"),
        P("head", None),
        P("seq", None),
    )
    return jax.shard_map(
        local,
        mesh=mesh,
        in_specs=placed,
        out_specs=(
            P("seq", None),
            P("seq", None),
            P("seq"),
            P("seq", None, "head"),
            P(None, "head"),
            P("head"),
            P("head", None),
            P(),
            P(),
            P(),
            P(None, "head"),
            P("head"),
            P("head", None),
            P("head"),
            P("head", "seq"),
            P("seq"),
            P("seq", None, "head"),
            P("head", "seq"),
        ),
        check_vma=False,
    )
```

```python
import functools
import math

import jax
import jax.numpy as jnp
from jax import lax
from jax.experimental import pallas as pl
from jax.experimental.pallas import tpu as pltpu
from jax.sharding import PartitionSpec as P

EPSILON = 1e-06
LANES = 128
CG = 4
WIDTH = CG * LANES
PLANE = 4
LOG2E = math.log2(math.e)
LN2 = math.log(2.0)
MESH = pl.DeviceIdType.MESH
VMEM_BYTES = 60 * 1024 * 1024


def f32(*shape):
    return jax.ShapeDtypeStruct(shape, jnp.float32)


def params(**more):
    return pltpu.CompilerParams(vmem_limit_bytes=VMEM_BYTES, **more)


def rates_in(state_rate):
    channels, states = state_rate.shape
    groups = channels // WIDTH
    parts = state_rate.reshape(groups, CG, LANES, states)
    return jnp.transpose(parts, (0, 3, 1, 2)).reshape(groups, states * CG, LANES) * (-LOG2E)


def rates_out(grad):
    groups, span, lanes = grad.shape
    parts = grad.reshape(groups, span // CG, CG, lanes)
    return jnp.transpose(parts, (0, 2, 3, 1)).reshape(groups * WIDTH, span // CG)


def pick_even(odd):
    row = lax.broadcasted_iota(jnp.int32, (LANES, 2 * LANES), 0)
    column = lax.broadcasted_iota(jnp.int32, (LANES, 2 * LANES), 1)
    return (column == 2 * row + odd).astype(jnp.float32).astype(jnp.bfloat16)


def widen(source, target):
    tokens, width = source.shape
    for block in range(width // LANES):
        piece = source[:, block * LANES : (block + 1) * LANES]
        for odd in range(2):
            target[odd * tokens : (odd + 1) * tokens, block * 2 * LANES : (block + 1) * 2 * LANES] = jnp.dot(
                piece, pick_even(odd), preferred_element_type=jnp.float32
            ).astype(jnp.bfloat16)


def narrow(source, target):
    tokens, width = target.shape
    row = lax.broadcasted_iota(jnp.int32, (2 * LANES, LANES), 0)
    column = lax.broadcasted_iota(jnp.int32, (2 * LANES, LANES), 1)
    pairs = (lax.div(row, 2) == column).astype(jnp.float32).astype(jnp.bfloat16)
    even = lax.rem(lax.broadcasted_iota(jnp.int32, (tokens, 2 * LANES), 1), 2) == 0
    for block in range(width // LANES):
        columns = slice(block * 2 * LANES, (block + 1) * 2 * LANES)
        value = jnp.where(even, source[:tokens, columns], source[tokens:, columns])
        total = None
        for unused in range(3):
            piece = value.astype(jnp.bfloat16)
            value = value - piece.astype(jnp.float32)
            term = jnp.dot(piece, pairs, preferred_element_type=jnp.float32)
            total = term if total is None else total + term
        target[:, block * LANES : (block + 1) * LANES] = total


def copy_to(source, target, send_sem, recv_sem, where):
    copy = pltpu.make_async_remote_copy(
        src_ref=source, dst_ref=target, send_sem=send_sem, recv_sem=recv_sem, device_id=where, device_id_type=MESH
    )
    copy.start()
    return copy


def wait_all(copies):
    for copy in copies:
        copy.wait()


class Places:
    def __init__(self, planes):
        self.planes = planes
        self.count = planes * PLANE
        self.me = lax.axis_index("seq")
        self.low = lax.rem(self.me, PLANE)
        self.high = lax.div(self.me, PLANE)
        self.core = lax.axis_index("head")

    def other(self):
        return {"head": 1 - self.core}

    def in_plane(self, shift):
        return {"seq": self.high * PLANE + lax.rem(self.low + shift, PLANE)}

    def across(self, shift):
        return {"seq": lax.rem(self.high + shift, self.planes) * PLANE + self.low}

    def along(self, shift):
        return {"seq": lax.rem(self.me + shift + self.count, self.count)}

    def mirror(self, mask):
        return self.low + sum((1 - 2 * lax.rem(lax.div(self.low, bit), 2)) * bit for bit in (1, 2) if mask & bit)

    def mirrored(self, mask):
        return {"seq": self.high * PLANE + self.mirror(mask)}

    def greet(self):
        partners = [self.other(), self.along(1), self.along(-1)]
        partners += [self.in_plane(shift) for shift in range(1, PLANE)]
        partners += [self.across(shift) for shift in range(1, self.planes)]
        barrier = pltpu.get_barrier_semaphore()
        for partner in partners:
            pl.semaphore_signal(barrier, inc=1, device_id=partner, device_id_type=MESH)
        return functools.partial(pl.semaphore_wait, barrier, len(partners))


class Lined:
    def __init__(self, ref):
        self.ref = ref

    def __getitem__(self, key):
        first, last = 0, self.ref.shape[0]
        if key is not Ellipsis:
            first, last = key[1].start // LANES, key[1].stop // LANES
        return jnp.concatenate([self.ref[j : j + 1, :] for j in range(first, last)], axis=1)


def as_column(row):
    return jnp.transpose(jnp.broadcast_to(row, (LANES, row.shape[1])))[:, :1]


def exchange_states(places, reverse, ends, sums, rates, pay, got, zpay, zgot, back, final, sems, beside=None):
    low, high, planes = places.low, places.high, places.planes
    quarter = ends.shape[1] // PLANE
    send_a, recv_a, send_b, recv_b, send_c, recv_c = sems
    for k in range(PLANE):
        pay[k, :, :quarter, :] = ends[:, k * quarter : (k + 1) * quarter, :]
        pay[k, :, quarter:, :] = sums[...]
    copies = [
        copy_to(pay.at[lax.rem(low + shift, PLANE)], got.at[shift], send_a.at[shift], recv_a.at[shift], places.in_plane(shift))
        for shift in range(1, PLANE)
    ]
    got[0] = pay[low]
    mine = rates[:, pl.ds(pl.multiple_of(low * quarter, 8), quarter), :]

    def decay(total):
        return jnp.exp2(mine * jnp.concatenate([total] * (quarter // 8), axis=1))

    wait_all(copies)
    order = range(PLANE - 1, -1, -1) if reverse else range(PLANE)
    held, decays = {}, {}
    plane_end = plane_sum = None
    for j in order:
        part = got[lax.rem(low - j + PLANE, PLANE)]
        held[j] = part[:, :quarter, :]
        size = part[:, quarter:, :]
        decays[j] = decay(size)
        plane_end = held[j] if plane_end is None else plane_end * decays[j] + held[j]
        plane_sum = size if plane_sum is None else plane_sum + size
    zpay[:, :quarter, :] = plane_end
    zpay[:, quarter:, :] = plane_sum
    copies = [
        copy_to(zpay, zgot.at[shift], send_b.at[shift], recv_b.at[shift], places.across(shift))
        for shift in range(1, planes)
    ]
    zgot[0] = zpay[...]
    if beside is not None:
        beside()
    wait_all(copies)
    state = jnp.zeros_like(plane_end)
    for h in range(planes - 1, -1, -1) if reverse else range(planes):
        part = zgot[lax.rem(high - h + planes, planes)]
        after_h = state * decay(part[:, quarter:, :]) + part[:, :quarter, :]
        state = jnp.where(h > high if reverse else h < high, after_h, state)
    for j in order:
        back[j] = state
        state = state * decays[j] + held[j]
    copies = [
        copy_to(back.at[lax.rem(low + shift, PLANE)], final.at[low], send_c.at[shift], recv_c.at[shift], places.in_plane(shift))
        for shift in range(1, PLANE)
    ]
    final[low] = back[low]
    wait_all(copies)


def exchange_scratch(planes, groups, span):
    quarter = span // PLANE
    size = (groups, quarter + 8, LANES)
    dma = pltpu.SemaphoreType.DMA
    return [
        pltpu.VMEM((PLANE,) + size, jnp.float32),
        pltpu.VMEM((PLANE,) + size, jnp.float32),
        pltpu.VMEM(size, jnp.float32),
        pltpu.VMEM((planes,) + size, jnp.float32),
        pltpu.VMEM((PLANE, groups, quarter, LANES), jnp.float32),
        pltpu.VMEM((PLANE, groups, quarter, LANES), jnp.float32),
        dma((PLANE,)), dma((PLANE,)), dma((planes,)), dma((planes,)), dma((PLANE,)), dma((PLANE,)),
    ]


def block16(block):
    return pl.ds(pl.multiple_of(block * 16, 16), 16)


def lanes(j, width=WIDTH):
    return slice(j * width, (j + 1) * width)


def norm_rows(read, gain, write, tokens):
    def step(block, carry):
        rows = block16(block)
        value = read(rows)
        scale = lax.rsqrt(jnp.mean(value * value, axis=-1, keepdims=True) + EPSILON)
        write(rows, value * scale * gain[...])
        return carry

    lax.fori_loop(0, tokens // 16, step, 0)


def third_masks(shape, rank, states):
    lane = lax.broadcasted_iota(jnp.int32, shape, 1)
    return lane < rank, (lane >= rank) & (lane < rank + states), lane >= rank + states


def third_means(value, rank, states):
    out = None
    for mask, count in zip(third_masks(value.shape, rank, states), (rank, states, states)):
        mean = jnp.sum(jnp.where(mask, value, 0.0), axis=-1, keepdims=True) * (1.0 / count)
        part = jnp.where(mask, mean, 0.0)
        out = part if out is None else out + part
    return out


class Rows:
    def __init__(self, places, share, out, landed, send_sem, recv_sem):
        self.places, self.share, self.out, self.landed = places, share, out, landed
        self.send_sem, self.recv_sem = send_sem, recv_sem

    def put(self, read, width, which):
        planes = self.places.planes
        piece = math.gcd(self.share, LANES)
        for block in range(width // LANES):
            turned = jnp.transpose(read(lanes(block, LANES)).astype(jnp.float32)).astype(jnp.bfloat16)
            for at in range(0, LANES, piece):
                index = block * LANES + at
                owner, offset = index // self.share, index % self.share
                slot = flip_bits(owner // PLANE, self.places.high, planes)
                place = lax.div(slot, 2) + lax.rem(slot, 2) * (planes // 2)
                self.out[which, owner % PLANE, place, offset : offset + piece, :] = turned[at : at + piece]

    def send(self, which):
        tokens = self.out.shape[-1]
        copies = [
            copy_to(
                self.out.at[which, self.places.mirror(mask)],
                self.landed.at[which, :, :, pl.ds(mask * tokens, tokens)],
                self.send_sem.at[which, mask],
                self.recv_sem.at[which, mask],
                self.places.mirrored(mask),
            )
            for mask in range(1, PLANE)
        ]
        self.landed[which, :, :, :tokens] = self.out[which, self.places.low]
        return copies


def send_columns(places, source, landing, start, size, send_sem, recv_sem):
    return [
        copy_to(source, landing.at[mask - 1, :, pl.ds(start, size)], send_sem.at[mask], recv_sem.at[mask], places.mirrored(mask))
        for mask in (1, 2)
    ]


def relay_columns(places, landing, start, size, send_sem, recv_sem):
    copies = []
    for mask, at in ((1, start), (2, start + size // 2)):
        columns = pl.ds(at, size // 2)
        copies.append(
            copy_to(
                landing.at[mask - 1, :, columns],
                landing.at[PLANE - 2, :, columns],
                send_sem.at[3 * (mask - 1)],
                recv_sem.at[3 * (mask - 1)],
                places.mirrored(3 - mask),
            )
        )
    return copies


def front_kernel(planes, rank, states, share,
                 x_ref, d_ref, starts_ref, start_row, conv_w_ref, conv_b_rows, dt_bias_rows, skip_rows, gain1_rows, gain2_rows,
                 gains_ref, win_ref, wx_ref, wdt_ref, rate_ref, wout_ref, gu_ref, down_ref,
                 z_ref, conv_ref, mixed_ref, proj_ref, rows_ref, step_ref, pre_ref, scanned_ref, gated_ref, resid_ref,
                 sum_ref, padded, hidden_ref, ggu_ref, gtwo_ref, output_ref, landed_ref, seen_ref, xin,
                 normed, two, wide, big, wout, wdown, keep_pad, edge_out, edge_in, mixed_low, proj_out, proj_in, wdt,
                 spread_b, spread_c, near_step, near_push, near_out, held_ref, ends, seen, mix_out, mix_in, rows_out, landed,
                 gates, ups, total, ffn_out, ffn_in, two_in,
                 pay, got, zpay, zgot, back, final, send_a, recv_a, send_b, recv_b, send_c, recv_c,
                 load_sem, save_sem, edge_sem, proj_sem, mix_sem, r_send, r_recv, x_send, x_recv, pair_sem):
    conv_b_ref, dt_bias_ref, skip_ref = Lined(conv_b_rows), Lined(dt_bias_rows), Lined(skip_rows)
    gain1_ref, gain2_ref = Lined(gain1_rows), Lined(gain2_rows)
    tokens, width = x_ref.shape
    channels = step_ref.shape[1]
    units = hidden_ref.shape[1]
    groups = channels // WIDTH
    tiles = units // WIDTH
    span = states * CG
    pairs = states // 2
    blocks = tokens // NEAR
    places = Places(planes)
    greeted = places.greet()

    def win_copy(j):
        return pltpu.make_async_copy(win_ref.at[:, :, pl.ds(j * WIDTH, WIDTH)], big.at[j], load_sem.at[j])

    def gu_copy(j):
        slot = (j + groups) % (groups + 1)
        return pltpu.make_async_copy(gu_ref.at[:, :, pl.ds(j * WIDTH, WIDTH)], big.at[slot], load_sem.at[groups + j])

    load_out = pltpu.make_async_copy(wout_ref, wout, load_sem.at[groups + tiles])
    load_down = pltpu.make_async_copy(down_ref, wdown, load_sem.at[groups + tiles + 1])
    for j in range(groups):
        win_copy(j).start()

    def put_normed(rows, value):
        normed[rows, :] = value.astype(jnp.bfloat16)

    norm_rows(lambda rows: x_ref[rows, :].astype(jnp.float32), gain1_ref, put_normed, tokens)
    widen(normed, wide)
    keep_pad[:8, :] = jnp.ones((8, 1), jnp.float32)
    keep_pad[8:, :] = as_column((1 - start_row[...]).astype(jnp.float32))
    wdt[:rank, :] = wdt_ref[...]
    wdt[rank:, :] = jnp.zeros((LANES - rank, channels), jnp.bfloat16)
    for j in range(groups):
        win_copy(j).wait()
        both = jnp.dot(wide[...], big[j].reshape(2 * width, WIDTH), preferred_element_type=jnp.float32).astype(jnp.bfloat16)
        padded[8:, lanes(j)] = both[:tokens].astype(jnp.float32)
        z_ref[:, lanes(j)] = both[tokens:]

    load_out.start()
    for j in range(tiles):
        gu_copy(j).start()
    load_down.start()
    last_keep = (1 - starts_ref[tokens - 1]).astype(jnp.float32)
    before_keep = (1 - starts_ref[tokens - 2]).astype(jnp.float32)
    row = lax.broadcasted_iota(jnp.int32, (16, 1), 0)
    tail = jnp.where(
        row == 15, 1.0, jnp.where(row == 14, last_keep, jnp.where(row == 13, last_keep * before_keep, 0.0))
    )
    edge_out[...] = (padded[tokens - 8 :, :] * tail).astype(jnp.bfloat16)
    greeted()
    edge = copy_to(edge_out, edge_in, edge_sem.at[0], edge_sem.at[1], places.along(1))
    sender = Rows(places, share, rows_out, landed, r_send, r_recv)
    sender.put(lambda cols: d_ref[:, cols], width, 0)
    edge.wait()
    row_copies = sender.send(0)
    padded[:8, :] = edge_in[8:, :].astype(jnp.float32)

    def conv(block, carry):
        start = block * 16
        rows = block16(block)
        near = pl.ds(pl.multiple_of(start, 8), 24)
        keeps = keep_pad[near, :]
        keep = keeps[8:]
        two_keep = keep * keeps[7:23]
        three = two_keep * keeps[6:22]
        for j in range(groups):
            values = padded[near, lanes(j)]
            mix = conv_b_ref[:, lanes(j)] + conv_w_ref[3:4, lanes(j)] * values[8:]
            for offset, mask in ((1, keep), (2, two_keep), (3, three)):
                mix += conv_w_ref[3 - offset : 4 - offset, lanes(j)] * values[8 - offset : 24 - offset] * mask
            conv_ref[rows, lanes(j)] = mix
            mixed = mix * jax.nn.sigmoid(mix)
            mixed_ref[rows, lanes(j)] = mixed
            mixed_low[rows, lanes(j)] = mixed.astype(jnp.bfloat16)
        return carry

    lax.fori_loop(0, tokens // 16, conv, 0)
    proj_out[...] = jnp.dot(mixed_low[...], wx_ref[...], preferred_element_type=jnp.float32)
    proj = copy_to(proj_out, proj_in, proj_sem.at[0], proj_sem.at[1], places.other())
    sender.put(lambda cols: normed[:, cols], width, 1)
    proj.wait()
    row_copies += sender.send(1)
    projected = proj_out[...] + proj_in[...]
    proj_ref[...] = projected
    scaled = projected * lax.rsqrt(third_means(projected * projected, rank, states) + EPSILON) * gains_ref[...]
    rows_ref[...] = scaled
    low_rows = jnp.where(third_masks(scaled.shape, rank, states)[0], scaled, 0.0).astype(jnp.bfloat16)
    for j in range(groups):
        pre = jnp.dot(low_rows, wdt[:, lanes(j)], preferred_element_type=jnp.float32) + dt_bias_ref[:, lanes(j)]
        pre_ref[:, lanes(j)] = pre
        step_ref[:, lanes(j)] = jnp.maximum(pre, 0.0) + jnp.log1p(jnp.exp(-jnp.abs(pre)))

    def keep_of(t):
        return (1 - starts_ref[t]).astype(jnp.float32)

    def near_block(block):
        return pl.ds(pl.multiple_of(block * NEAR, NEAR), NEAR)

    def rate_of(g, p):
        return rate_ref[g, p * 8 : p * 8 + 8, :]

    held_ref[...] = jnp.zeros_like(held_ref)
    sum_ref[...] = jnp.zeros_like(sum_ref)

    def end(block, carry):
        at = near_block(block)
        near_spread_rows(rows_ref[at, :], rank, states, spread_b)
        near_spread_channels(step_ref[at, :], near_step)
        near_spread_channels(step_ref[at, :] * mixed_ref[at, :], near_push)
        for g in range(groups):
            held = [held_ref[g, p * 8 : p * 8 + 8, :] for p in range(pairs)]
            sizes = sum_ref[g]
            for i in range(NEAR):
                size = near_step[g, near_rows(i), :]
                push = near_push[g, near_rows(i), :]
                keep = keep_of(block * NEAR + i)
                sizes = sizes + size
                for p in range(pairs):
                    decay = jnp.exp2(size * rate_of(g, p))
                    held[p] = decay * (held[p] * keep) + push * spread_b[near_rows(i, p), :]
            for p in range(pairs):
                held_ref[g, p * 8 : p * 8 + 8, :] = held[p]
            sum_ref[g] = sizes
        return carry

    lax.fori_loop(0, blocks, end, 0)
    ends[...] = held_ref[...]
    exchange_states(places, False, ends, sum_ref, rate_ref, pay, got, zpay, zgot, back, final,
                    (send_a, recv_a, send_b, recv_b, send_c, recv_c))
    per = pairs // PLANE
    for g in range(groups):
        for p in range(pairs):
            held_ref[g, p * 8 : p * 8 + 8, :] = final[p // per, g, (p % per) * 8 : (p % per) * 8 + 8, :]

    def seen_copy(block, slot):
        at = pl.ds(pl.multiple_of(block * (NEAR * span), 8), NEAR * span)
        return pltpu.make_async_copy(seen.at[slot], seen_ref.at[:, at, :], save_sem.at[slot])

    def scan(block, carry):
        at = near_block(block)
        slot = lax.rem(block, RING)

        @pl.when(block >= RING)
        def _():
            seen_copy(block - RING, slot).wait()

        near_spread_rows(rows_ref[at, :], rank, states, spread_b)
        near_spread_rows(rows_ref[at, :], rank + states, states, spread_c)
        near_spread_channels(step_ref[at, :], near_step)
        near_spread_channels(step_ref[at, :] * mixed_ref[at, :], near_push)
        for g in range(groups):
            held = [held_ref[g, p * 8 : p * 8 + 8, :] for p in range(pairs)]
            for i in range(NEAR):
                size = near_step[g, near_rows(i), :]
                push = near_push[g, near_rows(i), :]
                keep = keep_of(block * NEAR + i)
                out = None
                for p in range(pairs):
                    seen[slot, g, i * span + p * 8 : i * span + p * 8 + 8, :] = held[p]
                    decay = jnp.exp2(size * rate_of(g, p))
                    held[p] = decay * (held[p] * keep) + push * spread_b[near_rows(i, p), :]
                    term = held[p] * spread_c[near_rows(i, p), :]
                    out = term if out is None else out + term
                near_out[g, near_rows(i), :] = out
            for p in range(pairs):
                held_ref[g, p * 8 : p * 8 + 8, :] = held[p]
        seen_copy(block, slot).start()
        for j in range(channels // LANES):
            cols = lanes(j, LANES)
            scanned_ref[at, cols] = near_fold_channels(near_out, j // CG, j % CG) + skip_ref[:, cols] * mixed_ref[at, cols]
        return carry

    lax.fori_loop(0, blocks, scan, 0)
    last_state = pltpu.make_async_copy(held_ref, seen_ref.at[:, pl.ds(tokens * span, span), :], save_sem.at[RING])
    last_state.start()

    def gate(block, carry):
        rows = block16(block)
        for j in range(groups):
            z = z_ref[rows, lanes(j)].astype(jnp.float32)
            gated_ref[rows, lanes(j)] = (scanned_ref[rows, lanes(j)] * (z * jax.nn.sigmoid(z))).astype(jnp.bfloat16)
        return carry

    lax.fori_loop(0, tokens // 16, gate, 0)
    gated_copies = send_columns(places, gated_ref, xin, 0, channels, x_send.at[0], x_recv.at[0])
    load_out.wait()
    copies = []
    for j in range(width // WIDTH):
        mix_out[j] = jnp.dot(gated_ref[...], wout[:, lanes(j)], preferred_element_type=jnp.float32)
        copies.append(copy_to(mix_out.at[j], mix_in.at[j], mix_sem.at[0, j], mix_sem.at[1, j], places.other()))
    wait_all(copies)

    def put_two(rows, value):
        two[rows, :] = value.astype(jnp.bfloat16)

    def read_mid(rows):
        for j in range(width // WIDTH):
            resid_ref[rows, lanes(j)] = x_ref[rows, lanes(j)].astype(jnp.float32) + (mix_out[j, rows, :] + mix_in[j, rows, :])
        return resid_ref[rows, :]

    norm_rows(read_mid, gain2_ref, put_two, tokens)

    widen(two, wide)
    for j in range(tiles):
        gu_copy(j).wait()
        both = jnp.dot(
            wide[...], big[(j + groups) % (groups + 1)].reshape(2 * width, WIDTH), preferred_element_type=jnp.float32
        )
        gate_part, up_part = both[:tokens], both[tokens:]
        gates[:, lanes(j)] = gate_part
        ups[:, lanes(j)] = up_part
        hidden_ref[:, lanes(j)] = (gate_part * jax.nn.sigmoid(gate_part) * up_part).astype(jnp.bfloat16)
    wait_all(gated_copies)
    gated_copies = relay_columns(places, xin, 0, channels, x_send.at[0], x_recv.at[0])
    hidden_copies = send_columns(places, hidden_ref, xin, channels, units, x_send.at[1], x_recv.at[1])
    sender.put(lambda cols: two[:, cols], width, 2)
    row_copies += sender.send(2)
    load_down.wait()

    def backward(j, carry):
        cols = pl.ds(pl.multiple_of(j * WIDTH, WIDTH), WIDTH)
        down = wdown[cols, :]
        grad_hidden = lax.dot_general(
            d_ref[...], down, (((1,), (1,)), ((), ())), preferred_element_type=jnp.float32
        )
        act, slope = silu_and_slope(gates[:, cols])
        grad_gate = (grad_hidden * ups[:, cols] * slope).astype(jnp.bfloat16)
        grad_up = (grad_hidden * act).astype(jnp.bfloat16)
        ggu_ref[0, :, cols] = grad_gate
        ggu_ref[1, :, cols] = grad_up
        ffn = jnp.dot(hidden_ref[:, cols], down, preferred_element_type=jnp.float32)
        ffn_out[...] = jnp.where(j == 0, ffn, ffn_out[...] + ffn)
        weights = big[lax.rem(j + groups, groups + 1)].reshape(2 * width, WIDTH)
        back_part = lax.dot_general(
            jnp.concatenate([grad_gate, grad_up], 0), weights, (((1,), (1,)), ((), ())), preferred_element_type=jnp.float32
        )
        total[...] = jnp.where(j == 0, back_part, total[...] + back_part)
        return carry

    lax.fori_loop(0, tiles, backward, 0)
    ffn_copy = copy_to(ffn_out, ffn_in, pair_sem.at[0], pair_sem.at[1], places.other())
    narrow(total, gtwo_ref)
    two_copy = copy_to(gtwo_ref, two_in, pair_sem.at[2], pair_sem.at[3], places.other())
    ffn_copy.wait()

    def put_output(block, carry):
        rows = block16(block)
        output_ref[rows, :] = (resid_ref[rows, :] + (ffn_out[rows, :] + ffn_in[rows, :])).astype(jnp.bfloat16)
        return carry

    lax.fori_loop(0, tokens // 16, put_output, 0)
    two_copy.wait()
    gtwo_ref[...] += two_in[...]
    wait_all(row_copies)
    landed_ref[...] = landed[...]
    last_state.wait()
    for block in range(blocks - RING, blocks):
        seen_copy(block, block % RING).wait()
    wait_all(gated_copies)
    wait_all(hidden_copies)


def front(x_in, d_out, doc_start, pack, input_weight, w_x, w_dt, rates, w_out, w_gu, w_down, states):
    tokens, width = x_in.shape
    channels = w_x.shape[0]
    units = w_down.shape[0]
    rank = w_dt.shape[0]
    groups, span, unused = rates.shape
    count = lax.axis_size("seq")
    planes = count // PLANE
    share = width // count
    share_held = share + -share % 32
    vmem = pl.BlockSpec(memory_space=pltpu.VMEM)
    smem = pl.BlockSpec(memory_space=pltpu.SMEM)
    hbm = pl.BlockSpec(memory_space=pl.ANY)
    dma = pltpu.SemaphoreType.DMA
    chunks = width // WIDTH
    tiles = units // WIDTH
    near = 8 * (NEAR + 1)

    def fast(shape, kind=jnp.float32):
        return pltpu.VMEM(shape, kind)

    def low(*shape):
        return jax.ShapeDtypeStruct(shape, jnp.bfloat16)

    bf16 = jnp.bfloat16
    return pl.pallas_call(
        functools.partial(front_kernel, planes, rank, states, share),
        out_shape=(
            low(tokens, channels),
            f32(tokens, channels),
            f32(tokens, channels),
            f32(tokens, LANES),
            f32(tokens, LANES),
            f32(tokens, channels),
            f32(tokens, channels),
            f32(tokens, channels),
            low(tokens, channels),
            f32(tokens, width),
            f32(groups, 8, LANES),
            f32(tokens + 8, channels),
            low(tokens, units),
            low(2, tokens, units),
            f32(tokens, width),
            low(tokens, width),
            low(3, planes, share_held, PLANE * tokens),
            f32(groups, (tokens + 1) * span, LANES),
            low(PLANE - 1, tokens, channels + units),
        ),
        in_specs=[vmem, vmem, smem] + [vmem] * 8 + [hbm, vmem, vmem, vmem, hbm, hbm, hbm],
        out_specs=(vmem,) * 17 + (hbm, hbm),
        scratch_shapes=[
            fast((tokens, width), bf16),
            fast((tokens, width), bf16),
            fast((2 * tokens, 2 * width), bf16),
            fast((groups + 1, width, 2, WIDTH), bf16),
            fast((channels, width), bf16),
            fast((units, width), bf16),
            fast((tokens + 8, 1)),
            fast((16, channels), bf16),
            fast((16, channels), bf16),
            fast((tokens, channels), bf16),
            fast((tokens, LANES)),
            fast((tokens, LANES)),
            fast((LANES, channels), bf16),
            fast((span * (NEAR + 1), LANES)),
            fast((span * (NEAR + 1), LANES)),
            fast((groups, near, LANES)),
            fast((groups, near, LANES)),
            fast((groups, near, LANES)),
            fast((groups, span, LANES)),
            fast((groups, span, LANES)),
            fast((RING, groups, NEAR * span, LANES)),
            fast((chunks, tokens, WIDTH)),
            fast((chunks, tokens, WIDTH)),
            fast((3, PLANE, planes, share_held, tokens), bf16),
            fast((3, planes, share_held, PLANE * tokens), bf16),
            fast((tokens, units)),
            fast((tokens, units)),
            fast((2 * tokens, 2 * width)),
            fast((tokens, width)),
            fast((tokens, width)),
            fast((tokens, width)),
        ]
        + exchange_scratch(planes, groups, span)
        + [
            dma((groups + tiles + 2,)),
            dma((RING + 1,)),
            dma((2,)),
            dma((2,)),
            dma((2, chunks)),
            dma((3, PLANE)),
            dma((3, PLANE)),
            dma((2, PLANE)),
            dma((2, PLANE)),
            dma((4,)),
        ],
        compiler_params=params(collective_id=1, has_side_effects=True),
        name="front",
    )(
        x_in, d_out, doc_start, doc_start[None], *pack, input_weight, w_x, w_dt, rates, w_out, w_gu, w_down,
    )


RING = 3
NEAR = 8


def near_rows(i, p=0):
    return pl.ds(i + p * 8 * (NEAR + 1), 8, stride=NEAR + 1)


def near_slot(slot):
    return pl.ds(slot * (NEAR + 1), NEAR)


def near_spread_rows(rows, first, states, target):
    for n in range(states):
        column = jnp.broadcast_to(rows[:, first + n : first + n + 1], (NEAR, LANES))
        for group in range(CG):
            target[near_slot(n * CG + group), :] = column


def near_spread_channels(value, target):
    for j in range(value.shape[1] // LANES):
        g, k = j // CG, j % CG
        piece = value[:, lanes(j, LANES)]
        target[g, near_slot(k), :] = piece
        target[g, near_slot(CG + k), :] = piece


def near_fold_channels(source, g, k):
    return source[g, near_slot(k), :] + source[g, near_slot(CG + k), :]


def near_fold_rows(source, states, first, out):
    lane = lax.broadcasted_iota(jnp.int32, out.shape, 1)
    for n in range(states):
        total = None
        for group in range(CG):
            part = source[near_slot(n * CG + group), :]
            total = part if total is None else total + part
        out = jnp.where(lane == first + n, jnp.sum(total, axis=1, keepdims=True), out)
    return out


def flip_bits(k, high, planes):
    out = 0
    step = 1
    while step < planes:
        out = out + lax.rem(lax.div(k, step) + lax.div(high, step), 2) * step
        step *= 2
    return out


def slot_place(k, planes):
    return k // 2 + (k % 2) * (planes // 2)


def rms_back(grad, value, gain):
    scale = lax.rsqrt(jnp.mean(value * value, axis=-1, keepdims=True) + EPSILON)
    scaled = value * scale
    pull = grad * gain
    inner = jnp.mean(pull * scaled, axis=-1, keepdims=True)
    return scale * (pull - scaled * inner), grad * scaled


def silu_and_slope(value):
    sigmoid = jax.nn.sigmoid(value)
    return value * sigmoid, sigmoid * (1.0 + value * (1.0 - sigmoid))


def sum8(value):
    total = value[:8]
    for i in range(1, value.shape[0] // 8):
        total = total + value[i * 8 : (i + 1) * 8]
    return total


def back_kernel(planes, rank, states, share, units,
                d_ref, resid_ref, proj_ref, rows_ref,
                gtwo_ref, landed_ref, sum_ref, starts_ref, start_row, conv_w_ref, skip_rows, gain1_rows, gain2_rows, gains_ref, wx_ref, wdt_ref, rate_ref,
                hidden_ref, ggu_ref, gated_ref, seen_ref, wout_ref, win_ref, xfront, x_far, conv_far, pre_far, inner_far,
                z_far, scanned_far, mixed_far, step_far,
                dx_ref, grads_ref, wx_out, wdt_out, vec_out, rate_out, xin, zr0,
                x_ref, conv_ref, pre_ref, inner_ref, z_ref, scanned_ref, mixed_ref, step_ref, wout, win, wide, seen, rows_out, rows_mix, xbuf, zbuf, zs0, zs_more, zr_more, acc,
                gtwo_in, gmix_low, gscan, z_low, gstep, gmix, gpad, keep_pad, inner_low, mixed_low, gpre_low, wdt, dyp, dyp_in,
                edge_out, edge_in, norm_in, spread_b, spread_c, near_step, near_push, near_grad, near_lb, near_rq,
                near_gb, near_gc, mus, ends, rate_grad, vec, flat, sent, got, part, zsent, zgot, full, first_out, first_got, first_mid, first_zgot,
                pay, egot, zpay, ezgot, back, final,
                send_a, recv_a, send_b, recv_b, send_c, recv_c,
                load_sem, seen_sem, x_send, x_recv, r_send, r_recv, z_send, z_recv, xbuf_sem, pair_sem, small_sem, save_sem, late_sem, first_sem):
    skip_ref, gain1_ref, gain2_ref = Lined(skip_rows), Lined(gain1_rows), Lined(gain2_rows)
    tokens, width = d_ref.shape
    channels = conv_w_ref.shape[1]
    groups = channels // WIDTH
    chunks = width // WIDTH
    span = states * CG
    pairs = states // 2
    steps_z = planes.bit_length() - 1
    half = planes // 2
    places = Places(planes)
    low, high = places.low, places.high
    greeted = places.greet()
    blocks = tokens // NEAR

    late = [
        pltpu.make_async_copy(far, near, late_sem.at[i])
        for i, (far, near) in enumerate(
            (
                (z_far, z_ref),
                (scanned_far, scanned_ref),
                (mixed_far, mixed_ref),
                (step_far, step_ref),
                (conv_far, conv_ref),
                (pre_far, pre_ref),
                (inner_far, inner_ref),
                (x_far, x_ref),
            )
        )
    ]
    def wout_copy(j):
        rows = pl.ds(j * WIDTH, WIDTH)
        return pltpu.make_async_copy(wout_ref.at[rows, :], wout.at[j % 2], load_sem.at[2 + j % 2])

    wout_copy(0).start()
    wout_copy(1).start()

    def seen_copy(block, slot):
        at = pl.ds(pl.multiple_of(block * (NEAR * span), 8), (NEAR + 1) * span)
        return pltpu.make_async_copy(seen_ref.at[:, at, :], seen.at[slot], seen_sem.at[slot])

    for k in range(RING - 1):
        seen_copy(blocks - 1 - k, k).start()

    def win_copy(j):
        return pltpu.make_async_copy(win_ref.at[:, :, pl.ds(j * WIDTH, WIDTH)], win.at[j % 2], load_sem.at[j % 2])

    for load in late:
        load.start()
    win_copy(0).start()
    win_copy(1).start()

    greeted()
    sender = Rows(places, share, rows_out, rows_mix, r_send, r_recv)
    row_copies = {}

    HIDDEN, GATE, UP, GATED, Z, INNER = range(6)
    unit_copies = {}
    offsets, at = [], 0
    for unit_width, unused in units:
        offsets.append(at)
        at += unit_width

    def unit_source(u):
        return (hidden_ref, ggu_ref.at[0], ggu_ref.at[1], gated_ref, z_low, inner_low)[u]

    ring_width = max(unit_width for unit_width, unused in units)
    turn = (0, 2, 3, 1, 4, 5)

    def unit_columns(u):
        return pl.ds(offsets[u], units[u][0])

    def ring_columns(u):
        return pl.ds(turn[u] % 2 * ring_width, units[u][0])

    def columns_of(u, j):
        return pl.ds(pl.multiple_of(offsets[u] + j * WIDTH, WIDTH), WIDTH)

    def ring_of(u, j):
        return pl.ds(pl.multiple_of(turn[u] % 2 * ring_width + j * WIDTH, WIDTH), WIDTH)

    def first_slot(step):
        return sum(planes // 2 ** (k + 1) for k in range(1, step))

    landed_at = {3: 0, 0: units[3][0]}

    def send_unit(u):
        unit_copies[u] = send_columns(places, unit_source(u), xin, offsets[u], units[u][0], x_send.at[u], x_recv.at[u])

    def relay_landed(u):
        start, size = landed_at[u], units[u][0] // 2
        unit_copies[u] = [
            copy_to(
                xfront.at[mask - 1, :, pl.ds(start + at, size)],
                xin.at[PLANE - 2, :, pl.ds(offsets[u] + at, size)],
                x_send.at[u, mask],
                x_recv.at[u, mask],
                places.mirrored(3 - mask),
            )
            for mask, at in ((1, 0), (2, size))
        ]

    def relay(u):
        wait_all(unit_copies[u])
        unit_copies[u] = relay_columns(places, xin, offsets[u], units[u][0], x_send.at[u], x_recv.at[u])

    def partner(step):
        size = 2**step
        bit = lax.rem(lax.div(high, size), 2)
        return {"seq": (high + (1 - 2 * bit) * size) * PLANE + low}

    z_copies = {}

    def load_chunk(u, j, slot, with_z):
        local = pl.ds(pl.multiple_of(j * WIDTH, WIDTH), WIDTH)
        whole = columns_of(u, j)
        copies = [
            pltpu.make_async_copy(unit_source(u).at[:, local], xbuf.at[slot, pl.ds(0, tokens), :], xbuf_sem.at[slot, 0])
        ]
        for shift in range(1, PLANE):
            if u == GATED or u == HIDDEN and shift < PLANE - 1:
                arrived = xfront.at[shift - 1, :, pl.ds(pl.multiple_of(landed_at[u] + j * WIDTH, WIDTH), WIDTH)]
            else:
                arrived = xin.at[shift - 1, :, whole]
            copies.append(
                pltpu.make_async_copy(
                    arrived, xbuf.at[slot, pl.ds(shift * tokens, tokens), :], xbuf_sem.at[slot, shift]
                )
            )
        if with_z:
            copies.append(pltpu.make_async_copy(zr0.at[:, :, whole], zbuf.at[slot], xbuf_sem.at[slot, PLANE]))
        return copies

    def over_chunks(u, with_z, use):
        count = units[u][0] // WIDTH
        for copy in load_chunk(u, 0, 0, with_z):
            copy.start()

        def body(j, carry):
            slot = lax.rem(j, 2)

            @pl.when(j + 1 < count)
            def _():
                for copy in load_chunk(u, j + 1, 1 - slot, with_z):
                    copy.start()

            for copy in load_chunk(u, j, slot, with_z):
                copy.wait()
            use(slot, j)
            return carry

        lax.fori_loop(0, count, body, 0)

    def product(u, slot, first):
        which = units[u][1]
        rows = rows_mix[0, first : first + half] if which == 3 else landed_ref[which, first : first + half]
        left = rows.reshape(half * rows_mix.shape[2], PLANE * tokens)
        return jnp.dot(left, xbuf[slot], preferred_element_type=jnp.float32).reshape(half, rows_mix.shape[2], WIDTH)

    def stage_one(u):
        if u != GATED:
            wait_all(unit_copies[u])
        which = units[u][1]
        if which in row_copies:
            wait_all(row_copies.pop(which))

        def use(slot, j):
            zs0[:, :, ring_of(u, j)] = product(u, slot, half).astype(jnp.bfloat16)

        over_chunks(u, False, use)
        z_copies[u] = copy_to(zs0.at[:, :, ring_columns(u)], zr0.at[:, :, unit_columns(u)], z_send.at[u, 0], z_recv.at[u, 0], partner(0))

    def split(u, step, value, j):
        count = value.shape[0]
        columns = ring_of(u, j)
        if count == 1:
            acc[0, :, columns] = value[0]
            return
        for i in range(count // 2):
            acc[i, :, columns] = value[2 * i]
            zs_more[first_slot(step) + i, :, columns] = value[2 * i + 1].astype(jnp.bfloat16)

    def send_more(u, step):
        slots = pl.ds(first_slot(step), planes // 2 ** (step + 1))
        z_copies[u] = copy_to(
            zs_more.at[slots, :, ring_columns(u)],
            zr_more.at[slots, :, unit_columns(u)],
            z_send.at[u, step],
            z_recv.at[u, step],
            partner(step),
        )

    def stage_two(u):
        z_copies.pop(u).wait()
        for other in list(saves):
            if turn[other] % 2 == turn[u] % 2:
                saves.pop(other).wait()

        def use(slot, j):
            split(u, 1, product(u, slot, 0) + zbuf[slot].astype(jnp.float32), j)

        over_chunks(u, True, use)
        if steps_z > 1:
            send_more(u, 1)

    saves = {}

    def stage_three(u):
        count_chunks = units[u][0] // WIDTH
        for step in range(2, steps_z + 1):
            z_copies.pop(u).wait()
            count = planes // 2**step

            def body(j, carry):
                first = first_slot(step - 1)
                value = acc[:count, :, ring_of(u, j)] + zr_more[first : first + count, :, columns_of(u, j)].astype(jnp.float32)
                split(u, step, value, j)
                return carry

            lax.fori_loop(0, count_chunks, body, 0)
            if count > 1:
                send_more(u, step)
        save = pltpu.make_async_copy(acc.at[0, :, ring_columns(u)], grads_ref.at[:, unit_columns(u)], save_sem.at[u])
        save.start()
        saves[u] = save

    relay_landed(HIDDEN)
    send_unit(GATE)
    stage_one(HIDDEN)
    keep_pad[:8, :] = jnp.ones((8, 1), jnp.float32)
    keep_pad[8 : 8 + tokens, :] = as_column((1 - start_row[...]).astype(jnp.float32))
    keep_pad[8 + tokens :, :] = jnp.ones((8, 1), jnp.float32)
    wdt[:rank, :] = wdt_ref[...]
    wdt[rank:, :] = jnp.zeros((LANES - rank, channels), jnp.bfloat16)
    vec[...] = jnp.zeros_like(vec)
    rate_grad[...] = jnp.zeros_like(rate_grad)


    def mid(block, carry):
        rows = block16(block)
        grad = gtwo_ref[rows, :]
        back_to, gain_part = rms_back(grad, resid_ref[rows, :], gain2_ref[...])
        value = d_ref[rows, :].astype(jnp.float32) + back_to
        dx_ref[rows, :] = value
        gmix_low[rows, :] = value.astype(jnp.bfloat16)
        return carry + sum8(gain_part)

    norm2 = lax.fori_loop(0, tokens // 16, mid, jnp.zeros((8, width), jnp.float32))
    vec[8:9, :] = jnp.sum(norm2, axis=0, keepdims=True)
    sender.put(lambda cols: dx_ref[:, cols], width, 0)
    row_copies[3] = sender.send(0)

    for j in range(groups):
        wout_copy(j).wait()
        gscan[:, lanes(j)] = lax.dot_general(
            gmix_low[...], wout[j % 2], (((1,), (1,)), ((), ())), preferred_element_type=jnp.float32
        )
        if j + 2 < groups:
            wout_copy(j + 2).start()

    for load in late[:4]:
        load.wait()
    relay(GATE)
    def gate(block, carry):
        rows = block16(block)
        out = []
        for j in range(groups):
            cols = lanes(j)
            act, slope = silu_and_slope(z_ref[rows, cols].astype(jnp.float32))
            grad = gscan[rows, cols]
            grad_scanned = grad * act
            gscan[rows, cols] = grad_scanned
            z_low[rows, cols] = (grad * scanned_ref[rows, cols] * slope).astype(jnp.bfloat16)
            mixed = mixed_ref[rows, cols]
            mixed_low[rows, cols] = mixed.astype(jnp.bfloat16)
            out.append(carry[j] + sum8(grad_scanned * mixed))
        return tuple(out)

    skips = lax.fori_loop(0, tokens // 16, gate, (jnp.zeros((8, WIDTH), jnp.float32),) * groups)
    for j in range(groups):
        vec[6:7, lanes(j)] = jnp.sum(skips[j], axis=0, keepdims=True)

    def keep_of(t):
        return (1 - starts_ref[t]).astype(jnp.float32)

    def near_block(block):
        return pl.ds(pl.multiple_of(block * NEAR, NEAR), NEAR)

    def rate_of(g, p):
        return rate_ref[g, p * 8 : p * 8 + 8, :]

    mus[...] = jnp.zeros_like(mus)

    def feed(k, carry):
        block = blocks - 1 - k
        at = near_block(block)
        near_spread_rows(rows_ref[at, :], rank + states, states, spread_c)
        near_spread_channels(step_ref[at, :], near_step)
        near_spread_channels(gscan[at, :], near_grad)
        for g in range(groups):
            held = [mus[g, p * 8 : p * 8 + 8, :] for p in range(pairs)]
            for i in range(NEAR - 1, -1, -1):
                size = near_step[g, near_rows(i), :]
                grad = near_grad[g, near_rows(i), :]
                keep = keep_of(block * NEAR + i)
                for p in range(pairs):
                    lam = held[p] + spread_c[near_rows(i, p), :] * grad
                    held[p] = jnp.exp2(size * rate_of(g, p)) * (lam * keep)
            for p in range(pairs):
                mus[g, p * 8 : p * 8 + 8, :] = held[p]
        return carry

    lax.fori_loop(0, blocks, feed, 0)
    ends[...] = mus[...]

    def beside():
        stage_one(GATED)

    exchange_states(places, True, ends, sum_ref, rate_ref, pay, egot, zpay, ezgot, back, final,
                    (send_a, recv_a, send_b, recv_b, send_c, recv_c), beside)
    per = pairs // PLANE
    for g in range(groups):
        for p in range(pairs):
            mus[g, p * 8 : p * 8 + 8, :] = final[p // per, g, (p % per) * 8 : (p % per) * 8 + 8, :]
    send_unit(UP)
    stage_two(HIDDEN)
    stage_one(GATE)

    def scan(k, carry):
        block = blocks - 1 - k
        at = near_block(block)
        slot = lax.rem(k, RING)

        @pl.when(k + RING - 1 < blocks)
        def _():
            seen_copy(block - (RING - 1), lax.rem(k + RING - 1, RING)).start()

        near_spread_rows(rows_ref[at, :], rank, states, spread_b)
        near_spread_rows(rows_ref[at, :], rank + states, states, spread_c)
        near_spread_channels(step_ref[at, :], near_step)
        near_spread_channels(step_ref[at, :] * mixed_ref[at, :], near_push)
        near_spread_channels(gscan[at, :], near_grad)
        seen_copy(block, slot).wait()
        held = [[mus[g, p * 8 : p * 8 + 8, :] for p in range(pairs)] for g in range(groups)]
        for i in range(NEAR - 1, -1, -1):
            keep = keep_of(block * NEAR + i)
            sizes = [near_step[g, near_rows(i), :] for g in range(groups)]
            pushes = [near_push[g, near_rows(i), :] for g in range(groups)]
            grads = [near_grad[g, near_rows(i), :] for g in range(groups)]
            lbs, rqs = [None] * groups, [None] * groups
            for p in range(pairs):
                b_value = spread_b[near_rows(i, p), :]
                c_value = spread_c[near_rows(i, p), :]
                gb = gc = None
                for g in range(groups):
                    rate = rate_of(g, p)
                    before = seen[slot, g, i * span + p * 8 : i * span + p * 8 + 8, :]
                    now = seen[slot, g, (i + 1) * span + p * 8 : (i + 1) * span + p * 8 + 8, :]
                    lam = held[g][p] + c_value * grads[g]
                    mu = jnp.exp2(sizes[g] * rate) * (lam * keep)
                    held[g][p] = mu
                    q = mu * before
                    rate_grad[g, p * 8 : p * 8 + 8, :] += q * sizes[g]
                    lb, rq = lam * b_value, q * rate
                    lbs[g] = lb if lbs[g] is None else lbs[g] + lb
                    rqs[g] = rq if rqs[g] is None else rqs[g] + rq
                    gb_term, gc_term = lam * pushes[g], now * grads[g]
                    gb = gb_term if gb is None else gb + gb_term
                    gc = gc_term if gc is None else gc + gc_term
                near_gb[near_rows(i, p), :] = gb
                near_gc[near_rows(i, p), :] = gc
            for g in range(groups):
                near_lb[g, near_rows(i), :] = lbs[g]
                near_rq[g, near_rows(i), :] = rqs[g]
        for g in range(groups):
            for p in range(pairs):
                mus[g, p * 8 : p * 8 + 8, :] = held[g][p]
        for j in range(channels // LANES):
            g, k_group = j // CG, j % CG
            cols = lanes(j, LANES)
            lb = near_fold_channels(near_lb, g, k_group)
            rq = near_fold_channels(near_rq, g, k_group)
            gmix[at, cols] = step_ref[at, cols] * lb
            gstep[at, cols] = mixed_ref[at, cols] * lb + LN2 * rq
        row = jnp.zeros((NEAR, LANES), jnp.float32)
        row = near_fold_rows(near_gb, states, rank, row)
        dyp[at, :] = near_fold_rows(near_gc, states, rank + states, row)
        return carry

    lax.fori_loop(0, blocks // 2, scan, 0)
    relay(UP)
    send_unit(Z)
    lax.fori_loop(blocks // 2, blocks, scan, 0)
    stage_two(GATED)

    for load in late[4:]:
        load.wait()

    def pre_grad(block, carry):
        rows = block16(block)
        out = []
        for j in range(groups):
            grad = gstep[rows, lanes(j)] * jax.nn.sigmoid(pre_ref[rows, lanes(j)])
            gpre_low[rows, lanes(j)] = grad.astype(jnp.bfloat16)
            out.append(carry[j] + sum8(grad))
        return tuple(out)

    biases = lax.fori_loop(0, tokens // 16, pre_grad, (jnp.zeros((8, WIDTH), jnp.float32),) * groups)
    for j in range(groups):
        vec[5:6, lanes(j)] = jnp.sum(biases[j], axis=0, keepdims=True)
    dyp[...] += lax.dot_general(gpre_low[...], wdt[...], (((1,), (1,)), ((), ())), preferred_element_type=jnp.float32)
    dyp_copy = copy_to(dyp, dyp_in, pair_sem.at[2], pair_sem.at[3], places.other())
    turned = jnp.transpose(rows_ref[...]).astype(jnp.bfloat16)
    at_flat = channels // LANES * LANES
    for j in range(channels // LANES):
        value = jnp.dot(turned[:rank], gpre_low[:, lanes(j, LANES)], preferred_element_type=jnp.float32)
        flat[at_flat + j * rank : at_flat + (j + 1) * rank, :] = value
    relay(Z)
    dyp_copy.wait()
    projected = proj_ref[...]
    scale = lax.rsqrt(third_means(projected * projected, rank, states) + EPSILON)
    scaled = projected * scale
    grad = dyp[...] + dyp_in[...]
    pull = grad * gains_ref[...]
    proj_grad = scale * (pull - scaled * third_means(pull * scaled, rank, states))
    vec[9:10, :LANES] = jnp.sum(sum8(grad * scaled), axis=0, keepdims=True)
    proj_low = proj_grad.astype(jnp.bfloat16)
    turned_proj = jnp.transpose(proj_grad).astype(jnp.bfloat16)

    for j in range(groups):
        gmix[:, lanes(j)] += lax.dot_general(
            proj_low, wx_ref[lanes(j), :], (((1,), (1,)), ((), ())), preferred_element_type=jnp.float32
        )
    gpad[:8, :] = jnp.zeros((8, channels), jnp.float32)
    gpad[8 + tokens :, :] = jnp.zeros((8, channels), jnp.float32)

    def conv_grad(block, carry):
        rows = block16(block)
        to = pl.ds(pl.multiple_of(block * 16 + 8, 8), 16)
        near = pl.ds(pl.multiple_of(block * 16, 8), 24)
        keeps = keep_pad[near, :]
        keep = keeps[8:]
        two = keep * keeps[7:23]
        three = two * keeps[6:22]
        out = []
        for j in range(groups):
            cols = lanes(j)
            unused, slope = silu_and_slope(conv_ref[rows, cols])
            grad = (gmix[rows, cols] + skip_ref[:, cols] * gscan[rows, cols]) * slope
            gpad[to, cols] = grad
            values = inner_ref[near, cols]
            sums = [carry[j][4] + sum8(grad), carry[j][3] + sum8(grad * values[8:])]
            for offset, mask in ((1, keep), (2, two), (3, three)):
                sums.append(carry[j][3 - offset] + sum8(grad * values[8 - offset : 24 - offset] * mask))
            out.append((sums[4], sums[3], sums[2], sums[1], sums[0]))
        return tuple(out)

    empty = jnp.zeros((8, WIDTH), jnp.float32)
    taps = lax.fori_loop(0, tokens // 16, conv_grad, ((empty,) * 5,) * groups)
    for j in range(groups):
        for i in range(5):
            vec[i : i + 1, lanes(j)] = jnp.sum(taps[j][i], axis=0, keepdims=True)

    def taps_back(start, count, columns):
        near = pl.ds(pl.multiple_of(start, 8), count + 8)
        keeps = keep_pad[near, :]
        grads = gpad[near, columns]
        total = conv_w_ref[3:4, columns] * grads[:count]
        mask = None
        for offset in (1, 2, 3):
            mask = keeps[1 : count + 1] if mask is None else mask * keeps[offset : count + offset]
            total += conv_w_ref[3 - offset : 4 - offset, columns] * grads[offset : count + offset] * mask
        return total

    for j in range(groups):
        edge_out[:, lanes(j)] = taps_back(0, 8, lanes(j))
    edge_copy = copy_to(edge_out, edge_in, pair_sem.at[4], pair_sem.at[5], places.along(-1))
    stage_one(UP)
    stage_three(HIDDEN)

    def inner_grad(block, carry):
        rows = block16(block)
        for j in range(groups):
            inner_low[rows, lanes(j)] = taps_back(block * 16 + 8, 16, lanes(j)).astype(jnp.bfloat16)
        return carry

    lax.fori_loop(0, tokens // 16 - 1, inner_grad, 0)
    last_keep, before_keep = keep_of(tokens - 1), keep_of(tokens - 2)
    row = lax.broadcasted_iota(jnp.int32, (16, 1), 0)
    tail = jnp.where(
        row == 15, 1.0, jnp.where(row == 14, last_keep, jnp.where(row == 13, last_keep * before_keep, 0.0))
    )
    tail = jnp.where(places.me == places.count - 1, 0.0, tail)
    edge_copy.wait()
    for j in range(groups):
        here = taps_back(tokens - 8, 16, lanes(j))
        edge = jnp.concatenate([jnp.zeros((8, WIDTH), jnp.float32), edge_in[:, lanes(j)]], 0) * tail
        inner_low[tokens - 16 :, lanes(j)] = (here + edge).astype(jnp.bfloat16)
    send_unit(INNER)

    for j in range(channels // LANES):
        flat[j * LANES : (j + 1) * LANES, :] = jnp.dot(
            turned_proj, mixed_low[:, lanes(j, LANES)], preferred_element_type=jnp.float32
        )
    rows_flat = flat.shape[0]
    quarter = rows_flat // PLANE
    chunk = quarter // planes
    at_vec = at_flat + channels // LANES * rank
    for j in range(channels // LANES):
        flat[at_vec + j * 16 : at_vec + (j + 1) * 16, :] = vec[:, lanes(j, LANES)]
    at_rate = at_vec + channels // LANES * 16
    for g in range(groups):
        flat[at_rate + g * span : at_rate + (g + 1) * span, :] = -rate_grad[g]
    at_end = at_rate + groups * span
    if at_end < rows_flat:
        flat[at_end:, :] = jnp.zeros((rows_flat - at_end, LANES), jnp.float32)
    sent[...] = flat[...].astype(jnp.bfloat16)

    def quarter_at(index):
        return pl.ds(pl.multiple_of(index * quarter, 16), quarter)

    def chunk_at(index):
        return pl.ds(pl.multiple_of(index * chunk, 16), chunk)

    small_copies = [
        copy_to(sent.at[quarter_at(lax.rem(low + shift, PLANE))], got.at[shift], small_sem.at[0, shift], small_sem.at[1, shift],
                places.in_plane(shift))
        for shift in range(1, PLANE)
    ]
    part[...] = flat[quarter_at(low), :]
    stage_two(GATE)
    stage_one(Z)
    stage_three(GATED)

    for j in range(groups):
        win_copy(j).wait()
        both = lax.dot_general(
            jnp.concatenate([inner_low[:, lanes(j)], z_low[:, lanes(j)]], 0),
            win[j % 2].reshape(2 * width, WIDTH),
            (((1,), (1,)), ((), ())),
            preferred_element_type=jnp.float32,
        )
        if j == 0:
            wide[...] = both
        else:
            wide[...] += both
        if j + 2 < groups:
            win_copy(j + 2).start()
    narrow(wide, gtwo_in)
    norm_copy = copy_to(gtwo_in, norm_in, pair_sem.at[6], pair_sem.at[7], places.other())
    relay(INNER)
    stage_two(UP)
    stage_one(INNER)
    wait_all(small_copies)
    for shift in range(1, PLANE):
        part[...] += got[shift].astype(jnp.float32)
    zsent[...] = part[...].astype(jnp.bfloat16)
    small_copies = [
        copy_to(zsent.at[chunk_at(lax.rem(high + shift, planes))], zgot.at[shift], small_sem.at[2, shift], small_sem.at[3, shift],
                places.across(shift))
        for shift in range(1, planes)
    ]
    norm_copy.wait()

    def first_norm(block, carry):
        rows = block16(block)
        grad = gtwo_in[rows, :] + norm_in[rows, :]
        back_to, gain_part = rms_back(grad, x_ref[rows, :].astype(jnp.float32), gain1_ref[...])
        dx_ref[rows, :] += back_to
        return carry + sum8(gain_part)

    norm1 = jnp.sum(lax.fori_loop(0, tokens // 16, first_norm, jnp.zeros((8, width), jnp.float32)), axis=0, keepdims=True)
    first_out[...] = jnp.concatenate([norm1[:, lanes(j, LANES)] for j in range(width // LANES)], 0)
    first_copies = [
        copy_to(first_out, first_got.at[shift], first_sem.at[0, shift], first_sem.at[1, shift], places.in_plane(shift))
        for shift in range(1, PLANE)
    ]
    stage_three(GATE)
    stage_two(Z)
    wait_all(small_copies)
    total = part[chunk_at(high), :]
    for shift in range(1, planes):
        total += zgot[shift].astype(jnp.float32)
    mine = pl.ds(pl.multiple_of(low * quarter + high * chunk, 16), chunk)
    full[mine, :] = total.astype(jnp.bfloat16)
    small_copies = [
        copy_to(full.at[mine], full.at[mine], small_sem.at[4, shift], small_sem.at[5, shift], places.across(shift))
        for shift in range(1, planes)
    ]
    wait_all(first_copies)
    first_sum = first_out[...]
    for shift in range(1, PLANE):
        first_sum += first_got[shift]
    first_mid[...] = first_sum
    first_copies = [
        copy_to(first_mid, first_zgot.at[shift], first_sem.at[2, shift], first_sem.at[3, shift], places.across(shift))
        for shift in range(1, planes)
    ]
    stage_three(UP)
    stage_two(INNER)
    wait_all(small_copies)
    small_copies = [
        copy_to(full.at[quarter_at(low)], full.at[quarter_at(low)], small_sem.at[6, shift], small_sem.at[7, shift],
                places.in_plane(shift))
        for shift in range(1, PLANE)
    ]
    wait_all(small_copies)
    for j in range(channels // LANES):
        wx_out[:, lanes(j, LANES)] = full[j * LANES : (j + 1) * LANES, :].astype(jnp.float32)
        wdt_out[:, lanes(j, LANES)] = full[at_flat + j * rank : at_flat + (j + 1) * rank, :].astype(jnp.float32)
        vec_out[:, lanes(j, LANES)] = full[at_vec + j * 16 : at_vec + (j + 1) * 16, :].astype(jnp.float32)
    for g in range(groups):
        rate_out[g] = full[at_rate + g * span : at_rate + (g + 1) * span, :].astype(jnp.float32)
    wait_all(first_copies)
    first_sum = first_mid[...]
    for shift in range(1, planes):
        first_sum += first_zgot[shift]
    for j in range(width // LANES):
        vec_out[7:8, lanes(j, LANES)] = first_sum[j : j + 1]
    stage_three(Z)
    stage_three(INNER)
    wait_all(saves.values())


def mixer_back(d_out, x_in, kept, far, gtwo, hidden, ggu, doc_start, pack, w_x, w_dt, rates,
               w_out, input_weight, states, gated, seen, sums, landed, xfront):
    tokens, width = x_in.shape
    channels = w_x.shape[0]
    unit_ff = hidden.shape[1]
    rank = w_dt.shape[0]
    groups, span, unused = rates.shape
    count = lax.axis_size("seq")
    planes = count // PLANE
    share = width // count
    held = share + -share % 32
    units = ((unit_ff, 0), (unit_ff, 2), (unit_ff, 2), (channels, 3), (channels, 1), (channels, 1))
    columns = sum(u for u, unused in units)
    vmem = pl.BlockSpec(memory_space=pltpu.VMEM)
    smem = pl.BlockSpec(memory_space=pltpu.SMEM)
    hbm = pl.BlockSpec(memory_space=pl.ANY)
    dma = pltpu.SemaphoreType.DMA
    bf16 = jnp.bfloat16
    half = planes // 2
    ring = 2 * max(u for u, unused in units)
    more = max(planes // 4, 1)
    steps_z = planes.bit_length() - 1
    rows = channels + channels // LANES * (rank + 16) + groups * span
    rows += -rows % (16 * count)
    near = 8 * (NEAR + 1)

    def fast(shape, kind=jnp.float32):
        return pltpu.VMEM(shape, kind)

    return pl.pallas_call(
        functools.partial(back_kernel, planes, rank, states, share, units),
        out_shape=(
            f32(tokens, width),
            f32(held, columns),
            f32(LANES, channels),
            f32(rank, channels),
            f32(16, channels),
            f32(groups, span, LANES),
            jax.ShapeDtypeStruct((PLANE - 1, tokens, columns), bf16),
            jax.ShapeDtypeStruct((half, held, columns), bf16),
        ),
        in_specs=[vmem] * 7 + [smem] + [vmem] * 9 + [hbm] * 15,
        out_specs=(vmem, hbm, vmem, vmem, vmem, vmem, hbm, hbm),
        scratch_shapes=[
            fast((tokens, width), bf16),
            fast((tokens, channels)),
            fast((tokens, channels)),
            fast((tokens + 8, channels)),
            fast((tokens, channels), bf16),
            fast((tokens, channels)),
            fast((tokens, channels)),
            fast((tokens, channels)),
            fast((2, WIDTH, width), bf16),
            fast((2, width, 2, WIDTH), bf16),
            fast((2 * tokens, 2 * width)),
            fast((RING, groups, (NEAR + 1) * span, LANES)),
            fast((1, PLANE, planes, held, tokens), bf16),
            fast((1, planes, held, PLANE * tokens), bf16),
            fast((2, PLANE * tokens, WIDTH), bf16),
            fast((2, half, held, WIDTH), bf16),
            fast((half, held, ring), bf16),
            fast((max(half - 1, 1), held, ring), bf16),
            fast((max(half - 1, 1), held, columns), bf16),
            fast((more, held, ring)),
            fast((tokens, width)),
            fast((tokens, width), bf16),
            fast((tokens, channels)),
            fast((tokens, channels), bf16),
            fast((tokens, channels)),
            fast((tokens, channels)),
            fast((tokens + 16, channels)),
            fast((tokens + 16, 1)),
            fast((tokens, channels), bf16),
            fast((tokens, channels), bf16),
            fast((tokens, channels), bf16),
            fast((LANES, channels), bf16),
            fast((tokens, LANES)),
            fast((tokens, LANES)),
            fast((8, channels)),
            fast((8, channels)),
            fast((tokens, width)),
            fast((span * (NEAR + 1), LANES)),
            fast((span * (NEAR + 1), LANES)),
            fast((groups, near, LANES)),
            fast((groups, near, LANES)),
            fast((groups, near, LANES)),
            fast((groups, near, LANES)),
            fast((groups, near, LANES)),
            fast((span * (NEAR + 1), LANES)),
            fast((span * (NEAR + 1), LANES)),
            fast((groups, span, LANES)),
            fast((groups, span, LANES)),
            fast((groups, span, LANES)),
            fast((16, channels)),
            fast((rows, LANES)),
            fast((rows, LANES), bf16),
            fast((PLANE, rows // PLANE, LANES), bf16),
            fast((rows // PLANE, LANES)),
            fast((rows // PLANE, LANES), bf16),
            fast((planes, rows // count, LANES), bf16),
            fast((rows, LANES), bf16),
            fast((width // LANES, LANES)),
            fast((PLANE, width // LANES, LANES)),
            fast((width // LANES, LANES)),
            fast((planes, width // LANES, LANES)),
        ]
        + exchange_scratch(planes, groups, span)
        + [
            dma((4,)),
            dma((RING,)),
            dma((6, PLANE)),
            dma((6, PLANE)),
            dma((1, PLANE)),
            dma((1, PLANE)),
            dma((6, steps_z)),
            dma((6, steps_z)),
            dma((2, PLANE + 1)),
            dma((8,)),
            dma((8, max(PLANE, planes))),
            dma((6,)),
            dma((8,)),
            dma((4, max(PLANE, planes))),
        ],
        compiler_params=params(collective_id=2, has_side_effects=True),
        name="mixer_back",
    )(
        d_out, *kept, gtwo, landed, sums, doc_start, doc_start[None], pack[0], *pack[3:], w_x, w_dt, rates, hidden, ggu, gated, seen, w_out, input_weight, xfront, x_in, *far,
    )


def finish_kernel(units, channels, output_ref, dx_ref, grads_ref, wx_ref, wdt_ref,
                  output_out, dx_out, in_out, gu_out, out_out, down_out, x_out, dt_out):
    first = 3 * units
    rows = out_out.shape[0]
    gu_out[:, 0, :] = grads_ref[:rows, units : 2 * units]
    gu_out[:, 1, :] = grads_ref[:rows, 2 * units : first]
    in_out[:, 0, :] = grads_ref[:rows, first + 2 * channels : first + 3 * channels]
    in_out[:, 1, :] = grads_ref[:rows, first + channels : first + 2 * channels]
    down_out[...] = grads_ref[:rows, :units]
    out_out[...] = grads_ref[:rows, first : first + channels]
    output_out[...] = output_ref[...]
    dx_out[...] = dx_ref[...]
    dt_out[...] = wdt_ref[...]
    for block in range(wx_ref.shape[1] // LANES):
        x_out[lanes(block, LANES), :] = jnp.transpose(wx_ref[:, lanes(block, LANES)])


def finish(output, d_x, grads, wx_sum, wdt_sum, units, channels, share):
    tokens, width = d_x.shape
    rank = wdt_sum.shape[0]
    parts = 4 if share % 32 == 0 else 1

    def by_rows(rows, columns):
        return pl.BlockSpec((rows // parts, columns), lambda i: (i, 0))

    def by_pairs(rows, columns):
        return pl.BlockSpec((rows // parts, 2, columns), lambda i: (i, 0, 0))

    held = grads.shape[0]
    return pl.pallas_call(
        functools.partial(finish_kernel, units, channels),
        grid=(parts,),
        out_shape=(
            jax.ShapeDtypeStruct((tokens, width), jnp.bfloat16),
            f32(tokens, width),
            f32(share, 2, channels),
            f32(share, 2, units),
            f32(share, channels),
            f32(share, units),
            f32(channels, LANES),
            f32(rank, channels),
        ),
        in_specs=[
            by_rows(tokens, width),
            by_rows(tokens, width),
            by_rows(held, grads.shape[1]),
            pl.BlockSpec((LANES, channels // parts), lambda i: (0, i)),
            by_rows(rank, channels),
        ],
        out_specs=(
            by_rows(tokens, width),
            by_rows(tokens, width),
            by_pairs(share, channels),
            by_pairs(share, units),
            by_rows(share, channels),
            by_rows(share, units),
            by_rows(channels, LANES),
            by_rows(rank, channels),
        ),
        compiler_params=params(),
        name="finish",
    )(output, d_x, grads, wx_sum, wdt_sum)


def local(
    x_in,
    doc_start,
    norm1_gain,
    input_weight,
    conv_w,
    conv_b,
    w_x,
    dt_gain,
    b_gain,
    c_gain,
    w_dt,
    dt_bias,
    state_rate,
    skip,
    w_out,
    norm2_gain,
    w_gu,
    w_down,
    d_out,
):
    states = b_gain.shape[0]
    rank = dt_gain.shape[0]
    channels = conv_b.shape[0]
    rates = rates_in(state_rate)
    gains = jnp.concatenate([dt_gain, b_gain, c_gain])
    pack = [conv_w] + [v.reshape(-1, LANES) for v in (conv_b, dt_bias, skip, norm1_gain, norm2_gain)] + [gains[None]]
    (
        z_low, conv_out, mixed, projected, rows, steps, pre, scanned, gated, resid_mid, sums, padded, hidden, grad_gu, grad_two,
        output, landed, seen, gathered,
    ) = front(x_in, d_out, doc_start, pack, input_weight, w_x, w_dt, rates, w_out, w_gu, w_down, states)
    kept = (resid_mid, projected, rows)
    d_x, grads, wx_sum, wdt_sum, vectors, rate_sum, unused_x, unused_z = mixer_back(
        d_out, x_in, kept, (conv_out, pre, padded, z_low, scanned, mixed, steps), grad_two, hidden, grad_gu, doc_start, pack, w_x, w_dt, rates,
        w_out, input_weight, states, gated, seen, sums, landed, gathered,
    )
    count = lax.axis_size("seq")
    share = x_in.shape[1] // count
    units = hidden.shape[1]

    def own(row):
        return lax.dynamic_slice(vectors[row], (lax.axis_index("seq") * share,), (share,))

    output, d_x, g_in, g_gu, g_out, g_down, g_x, g_dt = finish(output, d_x, grads, wx_sum, wdt_sum, units, channels, share)
    gain_row = vectors[9]
    return (
        output,
        d_x,
        own(7),
        g_in,
        vectors[:4],
        vectors[4],
        g_x,
        gain_row[:rank],
        gain_row[rank : rank + states],
        gain_row[rank + states : rank + 2 * states],
        g_dt,
        vectors[5],
        rates_out(rate_sum),
        vectors[6],
        g_out.T,
        own(8),
        g_gu,
        g_down.T,
    )


def solution(mesh):
    placed = (
        P("seq", None),
        P("seq"),
        P(),
        P(None, None, "head"),
        P(None, "head"),
        P("head"),
        P("head", None),
        P(),
        P(),
        P(),
        P(None, "head"),
        P("head"),
        P("head", None),
        P("head"),
        P("head", None),
        P(),
        P(None, None, "head"),
        P("head", None),
        P("seq", None),
    )
    return jax.shard_map(
        local,
        mesh=mesh,
        in_specs=placed,
        out_specs=(
            P("seq", None),
            P("seq", None),
            P("seq"),
            P("seq", None, "head"),
            P(None, "head"),
            P("head"),
            P("head", None),
            P(),
            P(),
            P(),
            P(None, "head"),
            P("head"),
            P("head", None),
            P("head"),
            P("head", "seq"),
            P("seq"),
            P("seq", None, "head"),
            P("head", "seq"),
        ),
        check_vma=False,
    )
```
